32 devices in a mesh: row: 8 (over y, x, core), col: 4 (over z).
Axes of the slice: x: 2, y: 2, z: 4, core: 2. Of those that a mesh axis runs over, the one named last changes fastest.
Arguments:
- weight: bfloat16 [8192, 24576], P('row', 'col'), may hold values from -6 to 6
- gradient: bfloat16 [8192, 24576], P('row', 'col'), may hold values from -80 to 80
- momentum: float32 [8192, 24576], P('row', 'col'), may hold values from -6 to 6
- old_basis: bfloat16 [256, 24576], P(None, 'col'), may hold values from -6 to 6
Outputs:
- new_weight: bfloat16 [8192, 24576], P('row', 'col')
- new_momentum: float32 [8192, 24576], P('row', 'col')
- new_basis: bfloat16 [256, 24576], P(None, 'col')
The draws below stay inside these ranges and needn't reach their ends.
All inputs are finite; a program needn't handle non-finite values.
Results may differ from the reference program's by a relative error of at most 0.0056.
Values may be sent and summed in bfloat16 or wider, within the bound.
No kernel may reach another device: no remote copies, remote signals or barrier semaphores. Data moves between devices by JAX's collectives and lax.ppermute only.
A program may use at most 192 MiB of HBM per device.

```python
import math
import jax
import jax.numpy as jnp
from jax import lax

D = 8192
FF = 24576
RANK = 256


def draw_gradient(key, part):
    keys = jax.random.split(key, 2)
    base = jnp.clip(jax.random.normal(keys[0], (D, FF), jnp.float32), -6.0, 6.0)
    spread = jnp.exp(jax.random.uniform(keys[1], (FF,), jnp.float32, 0.0, math.log(10.0)))
    col_ramp = 1.0 + 2.0 * jnp.arange(FF, dtype=jnp.float32) / (FF - 1)
    row_ramp = 1.0 + 2.0 * jnp.arange(D, dtype=jnp.float32) / (D - 1)
    col_part = 0.1 * spread * col_ramp
    value = base * col_part[None, :] * row_ramp[:, None]
    return value.astype(jnp.bfloat16)


def shard_levels(key, dims, cuts, least, high):
    gain, own = 1.0, jax.random.fold_in(key, 6)
    for position, shards_of in cuts:
        steps = jnp.exp(jax.random.uniform(jax.random.fold_in(own, position), (shards_of,), jnp.float32, least / len(cuts), high / len(cuts)))
        gain = gain * jnp.repeat(steps, dims[position] // shards_of).reshape([-1 if axis == position else 1 for axis in range(len(dims))])
    return gain


def scatter_about(rng, shape, deviation, most, shards=(), kind=jnp.bfloat16):
    result = jax.random.normal(rng, shape, jnp.float32) * deviation
    if len(shards) > 0:
        result = shard_levels(rng, shape, shards, -0.22, 0.18) * result
    return jnp.clip(result, min=-most, max=most).astype(kind)


def setup_inputs(seed: int = 0) -> dict:
    splits = jax.random.split(jax.random.key(seed), 5)
    weight = scatter_about(splits[0], (D, FF), 1.0, 6.0, ((0, 8), (1, 4)))
    gradient = draw_gradient(jax.random.fold_in(splits[4], 71), 0)
    momentum = scatter_about(splits[2], (D, FF), 1.0, 6.0, ((0, 8), (1, 4)), jnp.float32)
    old_basis = scatter_about(splits[3], (RANK, FF), 1.0, 6.0, ((1, 4),))
    return dict(weight=weight, gradient=gradient, momentum=momentum, old_basis=old_basis)


epsilon = 1e-06
momentum_decay = 0.6
step_rate = 0.5

def reference(weight, gradient, momentum, old_basis):
    buffer = momentum + gradient.astype(jnp.float32)
    buffer_low = buffer.astype(jnp.bfloat16)
    left_factor = lax.dot_general(buffer_low.astype(jnp.float32), old_basis.astype(jnp.float32), (((1,), (1,)), ((), ())), preferred_element_type=jnp.float32)
    gram_matrix = lax.dot_general(left_factor.astype(jnp.float32), left_factor.astype(jnp.float32), (((0,), (0,)), ((), ())), precision=lax.Precision.HIGHEST, preferred_element_type=jnp.float32)
    chol_factor = jnp.linalg.cholesky(gram_matrix)
    orthonormal = lax.linalg.triangular_solve(chol_factor, left_factor, left_side=False, lower=True, transpose_a=True).astype(jnp.bfloat16)
    right_factor = lax.dot_general(orthonormal.astype(jnp.float32), buffer_low.astype(jnp.float32), (((0,), (0,)), ((), ())), preferred_element_type=jnp.float32)
    sum_squares = lax.optimization_barrier(jnp.sum(right_factor * right_factor, axis=1))
    col_scale = jnp.sqrt(sum_squares / FF + epsilon)
    new_basis = (right_factor / col_scale[:, None]).astype(jnp.bfloat16)
    scaled = (orthonormal.astype(jnp.float32) * col_scale[None, :]).astype(jnp.bfloat16)
    factor = step_rate * math.sqrt(D / RANK)

    def update_rows(row_blocks):
        buffer_rows, ortho_rows, scaled_rows, weight_rows = row_blocks
        correction = jnp.dot(scaled_rows.astype(jnp.float32), new_basis.astype(jnp.float32), preferred_element_type=jnp.float32)
        change = jnp.dot(ortho_rows.astype(jnp.float32), new_basis.astype(jnp.float32), preferred_element_type=jnp.float32)
        moved = buffer_rows - (1.0 - momentum_decay) * correction
        stepped = (weight_rows.astype(jnp.float32) - factor * change).astype(jnp.bfloat16)
        return (moved, stepped)
    blocks = 8
    shaped = tuple((part_rows.reshape(blocks, D // blocks, part_rows.shape[1]) for part_rows in (buffer, orthonormal, scaled, weight)))
    new_momentum, new_weight = lax.map(update_rows, shaped)
    return (new_weight.reshape(D, FF), new_momentum.reshape(D, FF), new_basis)
```

```python
import functools
import math

import jax
import jax.numpy as jnp
from jax import lax
from jax.experimental import pallas as pl
from jax.experimental.pallas import tpu as pltpu
from jax.sharding import PartitionSpec as P

D = 8192
FF = 24576
RANK = 256

epsilon = 1e-06
momentum_decay = 0.6
step_rate = 0.5

bf16, f32 = jnp.bfloat16, jnp.float32
VMEM = pl.BlockSpec(memory_space=pltpu.VMEM)
ANY = pl.BlockSpec(memory_space=pl.ANY)
MIB = 1 << 20


def shape(dims, kind):
    return jax.ShapeDtypeStruct(dims, kind)


def params(mib):
    return pltpu.CompilerParams(vmem_limit_bytes=mib * MIB)


def dot(a, b, dims=((1,), (0,))):
    return lax.dot_general(a, b, (dims, ((), ())), preferred_element_type=f32)


def split(x, terms):
    parts = []
    for _ in range(terms):
        part = x.astype(bf16)
        parts.append(part)
        x = x - part.astype(f32)
    return parts


def flip(i, d):
    return lax.bitwise_xor(i, jnp.int32(d))


def swap(x, axis, d):
    return lax.ppermute(x, axis, [(i, i ^ d) for i in range(lax.axis_size(axis))])


def project_kernel(mom, grad, basis, buf, *rest):
    parts = len(rest) - 2
    lefts, gbuf, sems = rest[:parts], rest[parts], rest[parts + 1]
    m, n = buf.shape
    block = m // parts
    tile = min(128, block)
    me = lax.axis_index("col")
    chunk = 1536 if n % 1536 == 0 else n

    def copies(d, i):
        rows = pl.ds(pl.multiple_of(flip(me, d) * block + i * tile, tile), tile)
        k = d * (block // tile) + i
        return (
            pltpu.make_async_copy(mom.at[rows, :], buf.at[rows, :], sems.at[0, k]),
            pltpu.make_async_copy(grad.at[rows, :], gbuf.at[rows, :], sems.at[1, k]),
        )

    order = [(d, i) for d in reversed(range(parts)) for i in range(block // tile)]
    for d, i in order:
        for copy in copies(d, i):
            copy.start()
    for d, i in order:
        for copy in copies(d, i):
            copy.wait()
        rows = pl.ds(pl.multiple_of(flip(me, d) * block + i * tile, tile), tile)

        def step(k, acc):
            cols = pl.ds(pl.multiple_of(k * chunk, 128), chunk)
            total = buf[rows, cols] + gbuf[rows, cols].astype(f32)
            buf[rows, cols] = total
            return acc + dot(basis[:, cols], total.astype(bf16), ((1,), (1,)))

        acc = lax.fori_loop(0, n // chunk, step, jnp.zeros((basis.shape[0], tile), f32))
        lefts[d][:, i * tile : (i + 1) * tile] = acc.astype(lefts[d].dtype)


def project(momentum, gradient, basis, parts):
    m, n = momentum.shape
    r = basis.shape[0]
    block = m // parts
    kinds = [f32] + [bf16] * (parts - 1)
    return pl.pallas_call(
        project_kernel,
        out_shape=(pltpu.VMEM((m, n), f32), *[shape((r, block), k) for k in kinds]),
        in_specs=[ANY, ANY, VMEM],
        out_specs=(VMEM,) * (parts + 1),
        scratch_shapes=[
            pltpu.VMEM((m, n), bf16),
            pltpu.SemaphoreType.DMA((2, m // min(128, block))),
        ],
        compiler_params=params(20),
        name="project",
    )(momentum, gradient, basis)


def half_product_kernel(half_of, blocks, buf, *rest):
    lefts, out, whole = rest[:blocks], rest[blocks], rest[blocks + 1]
    m, n = buf.shape
    block = m // blocks
    me = lax.axis_index("col")
    half = half_of(lax.bitwise_and(lax.axis_index("row"), jnp.int32(1)))
    for d in range(blocks):
        cols = pl.ds(pl.multiple_of(flip(me, d) * block, block), block)
        whole[:, cols] = lefts[d][...]
    width = 256

    def step(k, carry):
        cols = pl.ds(pl.multiple_of(half * (n // 2) + k * width, 128), width)
        b = buf[:, cols].astype(bf16)
        out[:, pl.ds(pl.multiple_of(k * width, 128), width)] = dot(whole[...], b).astype(out.dtype)
        return carry

    lax.fori_loop(0, n // 2 // width, step, 0)


def half_product(buf, lefts, mine, kind):
    m, n = buf.shape
    r = lefts[0].shape[0]
    half_of = (lambda core: core) if mine else (lambda core: 1 - core)
    return pl.pallas_call(
        functools.partial(half_product_kernel, half_of, len(lefts)),
        out_shape=shape((r, n // 2), kind),
        in_specs=[VMEM] * (1 + len(lefts)),
        out_specs=VMEM,
        scratch_shapes=[pltpu.VMEM((r, m), bf16)],
        compiler_params=params(8),
        name="mine_product" if mine else "other_product",
    )(buf, *lefts)


def pair_sum_kernel(chips, mine, received, *outs):
    me = lax.div(lax.axis_index("row"), jnp.int32(2))
    width = outs[0].shape[1]
    for d in range(chips):
        cols = pl.ds(pl.multiple_of(flip(me, d) * width, 128), width)
        outs[d][...] = (mine[:, cols] + received[:, cols].astype(f32)).astype(outs[d].dtype)


def pair_sum(mine, received, chips):
    r, n = mine.shape
    kinds = [f32] + [bf16] * (chips - 1)
    return pl.pallas_call(
        functools.partial(pair_sum_kernel, chips),
        out_shape=[shape((r, n // chips), k) for k in kinds],
        in_specs=[VMEM, VMEM],
        out_specs=[VMEM] * chips,
        compiler_params=params(8),
        name="pair_sum",
    )(mine, received)


def gram_kernel(blocks, *refs):
    lefts, mine, other, total = refs[:blocks], refs[blocks], refs[blocks + 1], refs[blocks + 2]
    core = lax.bitwise_and(lax.axis_index("row"), jnp.int32(1))
    total[...] = sum(dot(ref[...], ref[...], ((1,), (1,))) for ref in lefts)
    h = mine.shape[0]
    mine[...] = total[pl.ds(pl.multiple_of(core * h, h), h), :]
    other[...] = total[pl.ds(pl.multiple_of((1 - core) * h, h), h), :]


def gram(lefts):
    r = lefts[0].shape[0]
    return pl.pallas_call(
        functools.partial(gram_kernel, len(lefts)),
        out_shape=[shape((r // 2, r), f32)] * 2,
        in_specs=[VMEM] * len(lefts),
        out_specs=[VMEM] * 2,
        scratch_shapes=[pltpu.VMEM((r, r), f32)],
        compiler_params=params(8),
        name="gram",
    )(*lefts)


def chol_inverse_kernel(mine, other, out, work):
    n = out.shape[0]
    h = n // 2
    core = lax.bitwise_and(lax.axis_index("row"), jnp.int32(1))
    work[pl.ds(pl.multiple_of(core * h, h), h), :n] = mine[...]
    work[pl.ds(pl.multiple_of((1 - core) * h, h), h), :n] = other[...]
    r_id = lax.broadcasted_iota(jnp.int32, (n, n), 0)
    c_id = lax.broadcasted_iota(jnp.int32, (n, n), 1)
    work[:, n:] = jnp.where(r_id == c_id, 1.0, 0.0).astype(f32)
    nb = 32
    sub = lax.broadcasted_iota(jnp.int32, (nb, 1), 0)
    for p in range(n // nb):
        lo = p * nb
        left = (lo // 128) * 128
        right = n + ((lo + nb + 127) // 128) * 128
        s = work[lo : lo + nb, left:right]
        scale = jnp.zeros((nb, 1), f32)
        for t in range(nb):
            at = lo - left + t
            col = s[:, at : at + 1]
            row = s[t : t + 1, :]
            pivot = s[t : t + 1, at : at + 1]
            factor = jnp.where(sub > t, col, 0.0) * (1.0 / pivot)
            scale = jnp.where(sub == t, lax.rsqrt(pivot), scale)
            s = s - factor * row
        s = s * scale
        work[lo : lo + nb, left:right] = s
        if lo + nb < n:
            lead = s[:, lo + nb - left : n - left]
            work[lo + nb :, left:right] -= lax.dot_general(
                lead, s, (((0,), (0,)), ((), ())), precision=lax.Precision.HIGHEST, preferred_element_type=f32
            )
    out[...] = jnp.where(r_id >= c_id, work[:, n:], 0.0)


def chol_inverse(mine, other):
    n = mine.shape[1]
    return pl.pallas_call(
        chol_inverse_kernel,
        out_shape=shape((n, n), f32),
        in_specs=[VMEM, VMEM],
        out_specs=VMEM,
        scratch_shapes=[pltpu.VMEM((n, 2 * n), f32)],
        compiler_params=params(8),
        name="chol_inverse",
    )(mine, other)


def ortho_kernel(blocks, inverse, *refs):
    lefts, out = refs[:blocks], refs[blocks]
    block = lefts[0].shape[1]
    me = lax.axis_index("col")
    parts = split(inverse[...], 3)
    for d in range(blocks):
        rows = pl.ds(pl.multiple_of(flip(me, d) * block, block), block)
        o = sum(dot(lefts[d][...], part, ((0,), (1,))) for part in reversed(parts))
        out[rows, :] = o.astype(bf16)


def ortho(inverse, lefts):
    r, block = lefts[0].shape
    return pl.pallas_call(
        functools.partial(ortho_kernel, len(lefts)),
        out_shape=shape((block * len(lefts), r), bf16),
        in_specs=[VMEM] * (1 + len(lefts)),
        out_specs=VMEM,
        compiler_params=params(8),
        name="ortho",
    )(inverse, *lefts)


def share_sum_kernel(own, *refs):
    received, out = refs[:-1], refs[-1]
    out[...] = (own[...] + sum(ref[...].astype(f32) for ref in received)).astype(bf16)


def share_sum(own, received):
    return pl.pallas_call(
        share_sum_kernel,
        out_shape=shape(own.shape, bf16),
        in_specs=[VMEM] * (1 + len(received)),
        out_specs=VMEM,
        compiler_params=params(8),
        name="share_sum",
    )(own, *received)


def right_kernel(chips, inverse, *refs):
    blocks, right, squares = refs[: 2 * chips], refs[2 * chips], refs[2 * chips + 1]
    n = right.shape[1]
    r = right.shape[0]
    row = lax.axis_index("row")
    core = lax.bitwise_and(row, jnp.int32(1))
    chip = lax.div(row, jnp.int32(2))
    width = n // (2 * chips)
    parts = split(inverse[...], 2)
    total = jnp.zeros((r, 1), f32)
    for b in range(2 * chips):
        half = core if b < chips else 1 - core
        start = half * (n // 2) + flip(chip, b % chips) * width
        block = blocks[b][...]
        value = dot(parts[1], block) + dot(parts[0], block)
        right[:, pl.ds(pl.multiple_of(start, 128), width)] = value
    for b in range(2 * chips):
        value = right[:, b * width : (b + 1) * width]
        total = total + jnp.sum(value * value, axis=1, keepdims=True)
    wide = jnp.broadcast_to(total, (r, 128))
    squares[...] = jnp.transpose(wide)[:8, :]


def right_of(inverse, blocks):
    r, width = blocks[0].shape
    n = width * len(blocks)
    return pl.pallas_call(
        functools.partial(right_kernel, len(blocks) // 2),
        out_shape=(shape((r, n), f32), shape((8, r), f32)),
        in_specs=[VMEM] * (1 + len(blocks)),
        out_specs=(VMEM, VMEM),
        compiler_params=params(16),
        name="right_factor",
    )(inverse, *blocks)


def momentum_kernel(buf, ortho_ref, right, out, obuf, sems):
    m, n = buf.shape
    width = obuf.shape[2]
    tiles = n // width
    chunk = min(256, m)

    def copy(i):
        return pltpu.make_async_copy(obuf.at[i % 2], out.at[:, pl.ds(i * width, width)], sems.at[i % 2])

    for i in range(tiles):
        cols = slice(i * width, (i + 1) * width)
        if i >= 2:
            copy(i - 2).wait()
        low = right[:, cols].astype(bf16)

        def step(k, carry):
            rows = pl.ds(pl.multiple_of(k * chunk, chunk), chunk)
            correction = dot(ortho_ref[rows, :], low)
            obuf[i % 2, rows, :] = buf[rows, cols] - (1.0 - momentum_decay) * correction
            return carry

        lax.fori_loop(0, m // chunk, step, 0)
        copy(i).start()
    for i in range(max(tiles - 2, 0), tiles):
        copy(i).wait()


def momentum_out(buf, ortho_bf, right, width):
    m, n = buf.shape
    return pl.pallas_call(
        momentum_kernel,
        out_shape=shape((m, n), f32),
        in_specs=[VMEM] * 3,
        out_specs=ANY,
        scratch_shapes=[pltpu.VMEM((2, m, width), f32), pltpu.SemaphoreType.DMA((2,))],
        compiler_params=params(12),
        name="momentum_out",
    )(buf, ortho_bf, right)


def weight_kernel(factor, weight, ortho_ref, right, *refs):
    squares, (new_weight, basis, obuf, nbuf, sems) = refs[:-5], refs[-5:]
    m, n = weight.shape
    r = right.shape[0]
    width = obuf.shape[2]
    tiles = n // width
    chunk = min(256, m)
    terms = [ref[...] for ref in squares]
    while len(terms) > 1:
        terms = [terms[2 * i] + terms[2 * i + 1] for i in range(len(terms) // 2)]
    inverse = lax.rsqrt(terms[0] / FF + epsilon)
    inverse = jnp.transpose(jnp.concatenate([inverse] * 16, axis=0))[:, :1]

    def copies(i):
        cols = pl.ds(i * width, width)
        return (
            pltpu.make_async_copy(obuf.at[i % 2], new_weight.at[:, cols], sems.at[0, i % 2]),
            pltpu.make_async_copy(nbuf.at[i % 2], basis.at[:, cols], sems.at[1, i % 2]),
        )

    for i in range(tiles):
        cols = slice(i * width, (i + 1) * width)
        if i >= 2:
            for copy in copies(i - 2):
                copy.wait()
        nbuf[i % 2] = (right[:, cols] * inverse).astype(bf16)
        low = nbuf[i % 2]

        def step(k, carry):
            rows = pl.ds(pl.multiple_of(k * chunk, chunk), chunk)
            change = dot(ortho_ref[rows, :], low)
            obuf[i % 2, rows, :] = (weight[rows, cols].astype(f32) - factor * change).astype(bf16)
            return carry

        lax.fori_loop(0, m // chunk, step, 0)
        for copy in copies(i):
            copy.start()
    for i in range(max(tiles - 2, 0), tiles):
        for copy in copies(i):
            copy.wait()


def weight_out(weight, ortho_bf, right, squares, width, factor):
    m, n = weight.shape
    r = right.shape[0]
    return pl.pallas_call(
        functools.partial(weight_kernel, factor),
        out_shape=(shape((m, n), bf16), shape((r, n), bf16)),
        in_specs=[VMEM] * (3 + len(squares)),
        out_specs=(ANY, ANY),
        scratch_shapes=[
            pltpu.VMEM((2, m, width), bf16),
            pltpu.VMEM((2, r, width), bf16),
            pltpu.SemaphoreType.DMA((2, 2)),
        ],
        compiler_params=params(12),
        name="weight_out",
    )(weight, ortho_bf, right, *squares)


def per_device(weight, gradient, momentum, old_basis):
    depth, rows = lax.axis_size("col"), lax.axis_size("row")
    chips = rows // 2
    m, n = momentum.shape
    buf, own, *sent = project(momentum, gradient, old_basis, depth)
    got = [swap(x, "col", d + 1) for d, x in enumerate(sent)]
    low = share_sum(own, got)
    lefts = [low] + [swap(low, "col", d) for d in range(1, depth)]

    other = half_product(buf, lefts, False, bf16)
    other = swap(other, "row", 1)
    g_mine, g_other = gram(lefts)
    mine = half_product(buf, lefts, True, f32)
    own, *sent = pair_sum(mine, other, chips)
    got = [swap(x, "row", 2 * (d + 1)) for d, x in enumerate(sent)]

    g_mine = g_mine + swap(g_other, "row", 1)
    terms = [g_mine] + [swap(g_mine, "row", 2 * d) for d in range(1, chips)]
    while len(terms) > 1:
        terms = [terms[2 * i] + terms[2 * i + 1] for i in range(len(terms) // 2)]
    g_mine = terms[0]
    g_other = swap(g_mine, "row", 1)
    inverse = chol_inverse(g_mine, g_other)
    ortho_bf = ortho(inverse, lefts)

    share = share_sum(own, got)
    blocks = [share] + [swap(share, "row", 2 * d) for d in range(1, chips)]
    blocks = blocks + [swap(x, "row", 1) for x in blocks]
    right, squares = right_of(inverse, blocks)
    squares = [squares] + [swap(squares, "col", d) for d in range(1, depth)]
    new_momentum = momentum_out(buf, ortho_bf, right, n // rows)
    factor = step_rate * math.sqrt(D / RANK)
    new_weight, new_basis = weight_out(weight, ortho_bf, right, squares, n // rows, factor)
    return (new_weight, new_momentum, new_basis)


def plain_per_device(weight, gradient, momentum, old_basis):
    buffer = momentum + gradient.astype(f32)
    buffer_low = buffer.astype(bf16)
    left_factor = lax.psum(dot(buffer_low, old_basis, ((1,), (1,))), "col")
    gram_share = lax.dot_general(
        left_factor,
        left_factor,
        (((0,), (0,)), ((), ())),
        precision=lax.Precision.HIGHEST,
        preferred_element_type=f32,
    )
    chol_factor = jnp.linalg.cholesky(lax.psum(gram_share, "row"))
    orthonormal = lax.linalg.triangular_solve(
        chol_factor, left_factor, left_side=False, lower=True, transpose_a=True
    ).astype(bf16)
    right_share = lax.psum_scatter(
        dot(orthonormal, buffer_low, ((0,), (0,))), "row", scatter_dimension=0, tiled=True
    )
    sum_squares = lax.psum(jnp.sum(right_share * right_share, axis=1), "col")
    scale_share = jnp.sqrt(sum_squares / FF + epsilon)
    basis_share = (right_share / scale_share[:, None]).astype(bf16)
    new_basis = lax.all_gather(basis_share, "row", axis=0, tiled=True)
    col_scale = lax.all_gather(scale_share, "row", axis=0, tiled=True)
    scaled = (orthonormal.astype(f32) * col_scale[None, :]).astype(bf16)
    new_momentum = buffer - (1.0 - momentum_decay) * dot(scaled, new_basis)
    factor = step_rate * math.sqrt(D / RANK)
    new_weight = (weight.astype(f32) - factor * dot(orthonormal, new_basis)).astype(bf16)
    return (new_weight, new_momentum, new_basis)


def power_of_two(k):
    return k > 1 and k & (k - 1) == 0


def solution(mesh):
    rows, depth = mesh.shape["row"], mesh.shape["col"]
    tiled = (
        power_of_two(rows)
        and power_of_two(depth)
        and D % (rows * depth * 128) == 0
        and FF % (rows * depth * 256) == 0
    )
    return jax.shard_map(
        per_device if tiled else plain_per_device,
        mesh=mesh,
        in_specs=(P("row", "col"), P("row", "col"), P("row", "col"), P(None, "col")),
        out_specs=(P("row", "col"), P("row", "col"), P(None, "col")),
        check_vma=False,
    )
```

```python
import functools
import math

import jax
import jax.numpy as jnp
from jax import lax
from jax.experimental import pallas as pl
from jax.experimental.pallas import tpu as pltpu
from jax.sharding import PartitionSpec as P

D = 8192
FF = 24576
RANK = 256

epsilon = 1e-06
momentum_decay = 0.6
step_rate = 0.5

bf16, f32 = jnp.bfloat16, jnp.float32
VMEM = pl.BlockSpec(memory_space=pltpu.VMEM)
ANY = pl.BlockSpec(memory_space=pl.ANY)
MIB = 1 << 20


def shape(dims, kind):
    return jax.ShapeDtypeStruct(dims, kind)


def params(mib):
    return pltpu.CompilerParams(vmem_limit_bytes=mib * MIB)


def dot(a, b, dims=((1,), (0,))):
    return lax.dot_general(a, b, (dims, ((), ())), preferred_element_type=f32)


def split(x, terms):
    parts = []
    for _ in range(terms):
        part = x.astype(bf16)
        parts.append(part)
        x = x - part.astype(f32)
    return parts


def flip(i, d):
    return lax.bitwise_xor(i, jnp.int32(d))


def swap(x, axis, d):
    return lax.ppermute(x, axis, [(i, i ^ d) for i in range(lax.axis_size(axis))])


def project_kernel(part, depth, mom, grad, basis, *rest):
    rest = rest[-(depth + 5) :]
    buf, lefts, gbuf, bbuf, sems, bsem = rest[0], rest[1 : depth + 1], *rest[depth + 1 :]
    m, n = buf.shape
    half = m // depth
    me = lax.axis_index("col")
    chunk = 1536 if n % 1536 == 0 else n

    def copies(d):
        block = flip(me, d)
        there = pl.ds(pl.multiple_of((2 * block + part) * half, half), half)
        here = pl.ds(pl.multiple_of(block * half, half), half)
        return (
            pltpu.make_async_copy(mom.at[there, :], buf.at[here, :], sems.at[0, d]),
            pltpu.make_async_copy(grad.at[there, :], gbuf.at[here, :], sems.at[1, d]),
        )

    load_basis = pltpu.make_async_copy(basis, bbuf, bsem)
    order = list(reversed(range(depth)))
    for k, d in enumerate(order):
        for copy in copies(d):
            copy.start()
        if k == 0:
            load_basis.start()
    for k, d in enumerate(order):
        for copy in copies(d):
            copy.wait()
        if k == 0:
            load_basis.wait()
        rows = pl.ds(pl.multiple_of(flip(me, d) * half, half), half)

        def step(k, acc):
            cols = pl.ds(pl.multiple_of(k * chunk, 128), chunk)
            total = buf[rows, cols] + gbuf[rows, cols].astype(f32)
            buf[rows, cols] = total
            return acc + dot(bbuf[:, cols], total.astype(bf16), ((1,), (1,)))

        acc = lax.fori_loop(0, n // chunk, step, jnp.zeros((bbuf.shape[0], half), f32))
        lefts[d][...] = acc.astype(lefts[d].dtype)


def project(momentum, gradient, basis, depth, part, after=()):
    m, n = momentum.shape
    m = m // 2
    r = basis.shape[0]
    kinds = [f32] + [bf16] * (depth - 1)
    return pl.pallas_call(
        functools.partial(project_kernel, part, depth),
        out_shape=(pltpu.VMEM((m, n), f32), *[shape((r, m // depth), k) for k in kinds]),
        in_specs=[ANY] * (3 + len(after)),
        out_specs=(VMEM,) * (depth + 1),
        scratch_shapes=[
            pltpu.VMEM((m, n), bf16),
            pltpu.VMEM((r, n), bf16),
            pltpu.SemaphoreType.DMA((2, depth)),
            pltpu.SemaphoreType.DMA,
        ],
        compiler_params=params(12),
        name="project",
    )(stay(momentum), stay(gradient), stay(basis), *after)


def keep(x):
    return pltpu.with_memory_space_constraint(x, pltpu.VMEM)


def stay(x):
    return pltpu.with_memory_space_constraint(x, pltpu.HBM)


def gather_left(lefts, whole):
    half = lefts[0].shape[1]
    me = lax.axis_index("col")
    for d, ref in enumerate(lefts):
        whole[:, pl.ds(pl.multiple_of(flip(me, d) * half, half), half)] = ref[...]
    return whole


def self_product(whole):
    return dot(whole[...], whole[...], ((1,), (1,)))


def first_kernel(depth, width, buf, *rest):
    lefts, (other, mine, gram, whole) = rest[:depth], rest[depth:]
    core = lax.bitwise_and(lax.axis_index("row"), jnp.int32(1))
    size = other.shape[1]
    gather_left(lefts, whole)
    gram[...] = self_product(whole)
    for out, half in ((other, 1 - core), (mine, core)):

        def step(k, carry, out=out, half=half):
            cols = pl.ds(pl.multiple_of(half * size + k * width, 128), width)
            out[:, pl.ds(pl.multiple_of(k * width, 128), width)] = dot(whole[...], buf[:, cols].astype(bf16))
            return carry

        lax.fori_loop(0, size // width, step, 0)


def first_product(buf, lefts, width):
    m, n = buf.shape
    r = lefts[0].shape[0]
    return pl.pallas_call(
        functools.partial(first_kernel, len(lefts), width),
        out_shape=(shape((r, n // 2), f32), shape((r, n // 2), f32), shape((r, r), f32)),
        in_specs=[VMEM] * (1 + len(lefts)),
        out_specs=[VMEM] * 3,
        scratch_shapes=[pltpu.VMEM((r, m), bf16)],
        compiler_params=params(8),
        name="first_product",
    )(keep(buf), *lefts)


def other_kernel(depth, width, buf, sums, gram, *rest):
    lefts, (out, g_mine, g_other, whole, total) = rest[:depth], rest[depth:]
    core = lax.bitwise_and(lax.axis_index("row"), jnp.int32(1))
    size = out.shape[1]
    gather_left(lefts, whole)
    total[...] = gram[...] + self_product(whole)
    h = g_mine.shape[0]
    g_mine[...] = total[pl.ds(pl.multiple_of(core * h, h), h), :]
    g_other[...] = total[pl.ds(pl.multiple_of((1 - core) * h, h), h), :]

    def step(k, carry):
        cols = pl.ds(pl.multiple_of((1 - core) * size + k * width, 128), width)
        at = pl.ds(pl.multiple_of(k * width, 128), width)
        out[:, at] = (sums[:, at] + dot(whole[...], buf[:, cols].astype(bf16))).astype(bf16)
        return carry

    lax.fori_loop(0, size // width, step, 0)


def other_product(buf, sums, gram, lefts, width):
    m, n = buf.shape
    r = lefts[0].shape[0]
    return pl.pallas_call(
        functools.partial(other_kernel, len(lefts), width),
        out_shape=(shape((r, n // 2), bf16), shape((r // 2, r), f32), shape((r // 2, r), f32)),
        in_specs=[VMEM] * (3 + len(lefts)),
        out_specs=[VMEM] * 3,
        scratch_shapes=[pltpu.VMEM((r, m), bf16), pltpu.VMEM((r, r), f32)],
        compiler_params=params(8),
        name="other_product",
    )(keep(buf), sums, gram, *lefts)


def mine_kernel(depth, width, buf, sums, *rest):
    lefts, (out, whole) = rest[:depth], rest[-2:]
    core = lax.bitwise_and(lax.axis_index("row"), jnp.int32(1))
    size = out.shape[1]
    gather_left(lefts, whole)

    def step(k, carry):
        cols = pl.ds(pl.multiple_of(core * size + k * width, 128), width)
        at = pl.ds(pl.multiple_of(k * width, 128), width)
        out[:, at] = sums[:, at] + dot(whole[...], buf[:, cols].astype(bf16))
        return carry

    lax.fori_loop(0, size // width, step, 0)


def mine_product(buf, sums, lefts, width, after):
    m, n = buf.shape
    r = lefts[0].shape[0]
    return pl.pallas_call(
        functools.partial(mine_kernel, len(lefts), width),
        out_shape=shape((r, n // 2), f32),
        in_specs=[VMEM] * (2 + len(lefts)) + [ANY],
        out_specs=VMEM,
        scratch_shapes=[pltpu.VMEM((r, m), bf16)],
        compiler_params=params(8),
        name="mine_product",
    )(keep(buf), sums, *lefts, after)


def pair_sum_kernel(chips, mine, received, _, *outs):
    me = lax.div(lax.axis_index("row"), jnp.int32(2))
    width = outs[0].shape[1]
    for d in range(chips):
        cols = pl.ds(pl.multiple_of(flip(me, d) * width, 128), width)
        outs[d][...] = (mine[:, cols] + received[:, cols].astype(f32)).astype(outs[d].dtype)


def pair_sum(mine, received, chips, after):
    r, n = mine.shape
    kinds = [f32] + [bf16] * (chips - 1)
    return pl.pallas_call(
        functools.partial(pair_sum_kernel, chips),
        out_shape=[shape((r, n // chips), k) for k in kinds],
        in_specs=[VMEM, VMEM, ANY],
        out_specs=[VMEM] * chips,
        compiler_params=params(8),
        name="pair_sum",
    )(mine, received, after)


def share_sum_kernel(own, *refs):
    received, out = refs[:-1], refs[-1]
    out[...] = (own[...] + sum(ref[...].astype(f32) for ref in received)).astype(bf16)


def share_sum(own, received):
    return pl.pallas_call(
        share_sum_kernel,
        out_shape=shape(own.shape, bf16),
        in_specs=[VMEM] * (1 + len(received)),
        out_specs=VMEM,
        compiler_params=params(8),
        name="share_sum",
    )(own, *received)


def eliminate(tiles, at, nb, group):
    sub = lax.broadcasted_iota(jnp.int32, (nb, 128), 0)
    scale = jnp.zeros((nb, 128), f32)
    for g in range(0, nb, group):
        cols = [
            jnp.broadcast_to(tiles[0][:, at + g + j : at + g + j + 1], (nb, 128)) for j in range(group)
        ]
        for j in range(group):
            t = g + j
            pivot = cols[j][t : t + 1, :]
            factor = jnp.where(sub > t, cols[j], 0.0) * (1.0 / pivot)
            scale = jnp.where(sub == t, lax.rsqrt(pivot), scale)
            for l in range(j + 1, group):
                cols[l] = cols[l] - factor * cols[l][t : t + 1, :]
            tiles = [x - factor * x[t : t + 1, :] for x in tiles]
    return [x * scale for x in tiles]


def chol_inverse_kernel(mine, other, out, work):
    n = out.shape[0]
    h = n // 2
    core = lax.bitwise_and(lax.axis_index("row"), jnp.int32(1))
    work[pl.ds(pl.multiple_of(core * h, h), h), :n] = mine[...]
    work[pl.ds(pl.multiple_of((1 - core) * h, h), h), :n] = other[...]
    r_id = lax.broadcasted_iota(jnp.int32, (n, n), 0)
    c_id = lax.broadcasted_iota(jnp.int32, (n, n), 1)
    work[:, n:] = jnp.where(r_id == c_id, 1.0, 0.0).astype(f32)
    nb = 32
    for p in range(n // nb):
        lo = p * nb
        left = (lo // 128) * 128
        right = n + ((lo + nb + 127) // 128) * 128
        tiles = [work[lo : lo + nb, c : c + 128] for c in range(left, right, 128)]
        s = jnp.concatenate(eliminate(tiles, lo - left, nb, 8), axis=1)
        work[lo : lo + nb, left:right] = s
        if lo + nb < n:
            lead = s[:, lo + nb - left : n - left]
            work[lo + nb :, left:right] -= lax.dot_general(
                lead, s, (((0,), (0,)), ((), ())), precision=lax.Precision.HIGHEST, preferred_element_type=f32
            )
    out[...] = jnp.where(r_id >= c_id, work[:, n:], 0.0)


def chol_inverse(mine, other):
    n = mine.shape[1]
    return pl.pallas_call(
        chol_inverse_kernel,
        out_shape=shape((n, n), f32),
        in_specs=[VMEM, VMEM],
        out_specs=VMEM,
        scratch_shapes=[pltpu.VMEM((n, 2 * n), f32)],
        compiler_params=params(8),
        name="chol_inverse",
    )(mine, other)


def ortho_kernel(depth, inverse, *refs):
    lefts, out = refs[: 2 * depth], refs[2 * depth]
    half = lefts[0].shape[1]
    me = lax.axis_index("col")
    parts = split(inverse[...], 3)
    for k, ref in enumerate(lefts):
        part, d = divmod(k, depth)
        rows = pl.ds(pl.multiple_of((2 * flip(me, d) + part) * half, half), half)
        out[rows, :] = sum(dot(ref[...], x, ((0,), (1,))) for x in reversed(parts)).astype(bf16)


def ortho(inverse, lefts):
    r, half = lefts[0].shape
    return pl.pallas_call(
        functools.partial(ortho_kernel, len(lefts) // 2),
        out_shape=shape((half * len(lefts), r), bf16),
        in_specs=[VMEM] * (1 + len(lefts)),
        out_specs=VMEM,
        compiler_params=params(8),
        name="ortho",
    )(inverse, *lefts)


def apply_inverse(parts, block):
    return sum(dot(x, block) for x in reversed(parts))


def share_kernel(inverse, own, *refs):
    received, (out, squares) = refs[:-2], refs[-2:]
    out[...] = (own[...] + sum(ref[...].astype(f32) for ref in received)).astype(bf16)
    value = apply_inverse(split(inverse[...], 2), out[...])
    total = jnp.sum(value * value, axis=1, keepdims=True)
    squares[...] = jnp.transpose(jnp.broadcast_to(total, (total.shape[0], 128)))[:8, :]


def share_of(inverse, own, received):
    r = own.shape[0]
    return pl.pallas_call(
        share_kernel,
        out_shape=(shape(own.shape, bf16), shape((8, r), f32)),
        in_specs=[VMEM] * (2 + len(received)),
        out_specs=(VMEM, VMEM),
        compiler_params=params(8),
        name="share",
    )(inverse, own, *received)


def result_kernel(d, factor, buf0, buf1, ortho_ref, inverse, squares, block0, block1, weight, *rest):
    new_weight, new_momentum, basis, mbuf, wbuf, vbuf, nbuf, in_sems, out_sems = rest[-9:]
    m = ortho_ref.shape[0]
    r, width = block0.shape
    half = width * (lax.axis_size("row") // 2)
    row = lax.axis_index("row")
    core = lax.bitwise_and(row, jnp.int32(1))
    chip = flip(lax.div(row, jnp.int32(2)), d)
    starts = [core * half + chip * width, (1 - core) * half + chip * width]
    cols = [pl.ds(pl.multiple_of(start, 128), width) for start in starts]
    loads = [pltpu.make_async_copy(weight.at[:, cols[b]], wbuf.at[b], in_sems.at[b]) for b in range(2)]
    stores = [
        pltpu.make_async_copy(src.at[b], dst.at[:, cols[b]], out_sems.at[k, b])
        for b in range(2)
        for k, (src, dst) in enumerate(((mbuf, new_momentum), (vbuf, new_weight), (nbuf, basis)))
    ]
    for load in loads:
        load.start()
    scale = lax.rsqrt(squares[...] / FF + epsilon)
    scale = jnp.transpose(jnp.concatenate([scale] * 16, axis=0))[:, :1]
    parts = split(inverse[...], 2)
    lows = []
    for b, block in enumerate((block0, block1)):
        right = apply_inverse(parts, block[...])
        lows.append(right.astype(bf16))
        nbuf[b] = (right * scale).astype(bf16)
    depth = lax.axis_size("col")
    size = m // (2 * depth)
    for b in range(2):
        loads[b].wait()

        def step(k, carry, b=b):
            for part, buf in enumerate((buf0, buf1)):
                here = pl.ds(pl.multiple_of(k * size, size), size)
                rows = pl.ds(pl.multiple_of((2 * k + part) * size, size), size)
                correction = dot(ortho_ref[rows, :], lows[b])
                mbuf[b, rows, :] = buf[here, cols[b]] - (1.0 - momentum_decay) * correction
                change = dot(ortho_ref[rows, :], nbuf[b])
                vbuf[b, rows, :] = (wbuf[b, rows, :].astype(f32) - factor * change).astype(bf16)
            return carry

        lax.fori_loop(0, depth, step, 0, unroll=2)
        for store in stores[3 * b : 3 * b + 3]:
            store.start()
    for store in stores:
        store.wait()


def results(d, factor, bufs, ortho_bf, inverse, squares, blocks, weight, before):
    m, n = weight.shape
    r, width = blocks[0].shape
    ins = [*map(keep, bufs), ortho_bf, inverse, squares, *blocks, stay(weight), *map(stay, before)]
    return pl.pallas_call(
        functools.partial(result_kernel, d, factor),
        out_shape=(shape((m, n), bf16), shape((m, n), f32), shape((r, n), bf16)),
        in_specs=[VMEM] * 7 + [ANY] * (1 + len(before)),
        out_specs=[ANY] * 3,
        input_output_aliases={8 + k: k for k in range(len(before))},
        scratch_shapes=[
            pltpu.VMEM((2, m, width), f32),
            pltpu.VMEM((2, m, width), bf16),
            pltpu.VMEM((2, m, width), bf16),
            pltpu.VMEM((2, r, width), bf16),
            pltpu.SemaphoreType.DMA((2,)),
            pltpu.SemaphoreType.DMA((3, 2)),
        ],
        compiler_params=params(20),
        name="results",
    )(*ins)


def pair_up(terms):
    while len(terms) > 1:
        terms = [terms[2 * i] + terms[2 * i + 1] for i in range(len(terms) // 2)]
    return terms[0]


def exchange(x, axis, count, unit=1):
    return [x] + [swap(x, axis, unit * d) for d in range(1, count)]


def per_device(weight, gradient, momentum, old_basis):
    depth, rows = lax.axis_size("col"), lax.axis_size("row")
    chips = rows // 2
    m, n = momentum.shape
    width = n // rows

    bufs, lefts, after = [], [], ()
    for part in range(2):
        buf, own, *sent = project(momentum, gradient, old_basis, depth, part, after)
        after = (sent[0],)
        low = share_sum(own, [swap(x, "col", d + 1) for d, x in enumerate(sent)])
        bufs.append(buf)
        lefts.append(exchange(low, "col", depth))

    other, mine, gram = first_product(bufs[0], lefts[0], width)
    other, g_mine, g_other = other_product(bufs[1], other, gram, lefts[1], width)
    received = swap(other, "row", 1)
    g_mine = g_mine + swap(g_other, "row", 1)
    mine = mine_product(bufs[1], mine, lefts[1], width, other)
    own, *sent = pair_sum(mine, received, chips, g_mine)
    g_mine = pair_up(exchange(g_mine, "row", chips, 2))
    got = [swap(x, "row", 2 * (d + 1)) for d, x in enumerate(sent)]

    inverse = chol_inverse(g_mine, swap(g_mine, "row", 1))
    ortho_bf = ortho(inverse, lefts[0] + lefts[1])

    share, squares = share_of(inverse, own, got)
    blocks = exchange(share, "row", chips, 2)
    squares = squares + swap(squares, "row", 1)
    squares = pair_up(exchange(squares, "row", chips, 2))
    squares = pair_up(exchange(squares, "col", depth))
    factor = step_rate * math.sqrt(D / RANK)
    outs = ()
    for d, block in enumerate(blocks):
        pair = (block, swap(block, "row", 1))
        outs = results(d, factor, bufs, ortho_bf, inverse, squares, pair, weight, outs)
    return tuple(outs)


def plain_per_device(weight, gradient, momentum, old_basis):
    buffer = momentum + gradient.astype(f32)
    buffer_low = buffer.astype(bf16)
    left_factor = lax.psum(dot(buffer_low, old_basis, ((1,), (1,))), "col")
    gram_share = lax.dot_general(
        left_factor,
        left_factor,
        (((0,), (0,)), ((), ())),
        precision=lax.Precision.HIGHEST,
        preferred_element_type=f32,
    )
    chol_factor = jnp.linalg.cholesky(lax.psum(gram_share, "row"))
    orthonormal = lax.linalg.triangular_solve(
        chol_factor, left_factor, left_side=False, lower=True, transpose_a=True
    ).astype(bf16)
    right_share = lax.psum_scatter(
        dot(orthonormal, buffer_low, ((0,), (0,))), "row", scatter_dimension=0, tiled=True
    )
    sum_squares = lax.psum(jnp.sum(right_share * right_share, axis=1), "col")
    scale_share = jnp.sqrt(sum_squares / FF + epsilon)
    basis_share = (right_share / scale_share[:, None]).astype(bf16)
    new_basis = lax.all_gather(basis_share, "row", axis=0, tiled=True)
    col_scale = lax.all_gather(scale_share, "row", axis=0, tiled=True)
    scaled = (orthonormal.astype(f32) * col_scale[None, :]).astype(bf16)
    new_momentum = buffer - (1.0 - momentum_decay) * dot(scaled, new_basis)
    factor = step_rate * math.sqrt(D / RANK)
    new_weight = (weight.astype(f32) - factor * dot(orthonormal, new_basis)).astype(bf16)
    return (new_weight, new_momentum, new_basis)


def power_of_two(k):
    return k > 1 and k & (k - 1) == 0


def solution(mesh):
    rows, depth = mesh.shape["row"], mesh.shape["col"]
    tiled = (
        power_of_two(rows)
        and power_of_two(depth)
        and D % (rows * depth * 128) == 0
        and FF % (rows * depth * 256) == 0
    )
    return jax.shard_map(
        per_device if tiled else plain_per_device,
        mesh=mesh,
        in_specs=(P("row", "col"), P("row", "col"), P("row", "col"), P(None, "col")),
        out_specs=(P("row", "col"), P("row", "col"), P(None, "col")),
        check_vma=False,
    )
```

```python
import functools
import math

import jax
import jax.numpy as jnp
from jax import lax
from jax.experimental import pallas as pl
from jax.experimental.pallas import tpu as pltpu
from jax.sharding import PartitionSpec as P

D = 8192
FF = 24576
RANK = 256

epsilon = 1e-06
momentum_decay = 0.6
step_rate = 0.5

bf16, f32 = jnp.bfloat16, jnp.float32
VMEM = pl.BlockSpec(memory_space=pltpu.VMEM)
ANY = pl.BlockSpec(memory_space=pl.ANY)
MIB = 1 << 20


def shape(dims, kind):
    return jax.ShapeDtypeStruct(dims, kind)


def params(mib):
    return pltpu.CompilerParams(vmem_limit_bytes=mib * MIB)


def dot(a, b, dims=((1,), (0,))):
    return lax.dot_general(a, b, (dims, ((), ())), preferred_element_type=f32)


def split(x, terms):
    parts = []
    for _ in range(terms):
        part = x.astype(bf16)
        parts.append(part)
        x = x - part.astype(f32)
    return parts


def flip(i, d):
    return lax.bitwise_xor(i, jnp.int32(d))


def swap(x, axis, d):
    return lax.ppermute(x, axis, [(i, i ^ d) for i in range(lax.axis_size(axis))])


def block_copies(part, d, mom, grad, buf, gbuf, slot, sems):
    half = gbuf.shape[1]
    block = flip(lax.axis_index("col"), d)
    there = pl.ds(pl.multiple_of((2 * block + part) * half, half), half)
    here = pl.ds(pl.multiple_of(block * half, half), half)
    return (
        pltpu.make_async_copy(mom.at[there, :], buf.at[here, :], sems.at[0, d]),
        pltpu.make_async_copy(grad.at[there, :], gbuf.at[slot], sems.at[1, d]),
    )


def project_block(d, buf, gref, basis, left):
    half, n = gref.shape
    rows = pl.ds(pl.multiple_of(flip(lax.axis_index("col"), d) * half, half), half)
    chunk = 1536 if n % 1536 == 0 else n

    def step(k, acc):
        cols = pl.ds(pl.multiple_of(k * chunk, 128), chunk)
        total = buf[rows, cols] + gref[:, cols].astype(f32)
        buf[rows, cols] = total
        return acc + dot(basis[:, cols], total.astype(bf16), ((1,), (1,)))

    acc = lax.fori_loop(0, n // chunk, step, jnp.zeros((basis.shape[0], half), f32))
    left[...] = acc.astype(left.dtype)


def project_kernel(part, depth, mom, grad, basis, *rest):
    if part == 0:
        (buf, kept), rest = rest[:2], rest[2:]
    else:
        kept, buf, rest = basis, rest[1], rest[2:]
    lefts, (gbuf, sems, basis_sem) = rest[:depth], rest[depth:]
    order = list(reversed(range(depth)))
    copies = [block_copies(part, d, mom, grad, buf, gbuf, d, sems) for d in range(depth)]
    load_basis = pltpu.make_async_copy(basis, kept, basis_sem) if part == 0 else None
    for k, d in enumerate(order):
        for copy in copies[d]:
            copy.start()
        if k == 0 and part == 0:
            load_basis.start()
    for k, d in enumerate(order):
        for copy in copies[d]:
            copy.wait()
        if k == 0 and part == 0:
            load_basis.wait()
        project_block(d, buf, gbuf.at[d], kept, lefts[d])


def project(momentum, gradient, basis, depth, part, after=()):
    m, n = momentum.shape
    r = basis.shape[0]
    half = m // 2 // depth
    kinds = [f32] + [bf16] * (depth - 1)
    kept = [] if part else [pltpu.VMEM((r, n), bf16)]
    return pl.pallas_call(
        functools.partial(project_kernel, part, depth),
        out_shape=(pltpu.VMEM((m // 2, n), f32), *kept, *[shape((r, half), k) for k in kinds]),
        in_specs=[ANY, ANY] + [VMEM if part else ANY] + [ANY] * len(after),
        out_specs=(VMEM,) * (depth + 1 + len(kept)),
        scratch_shapes=[
            pltpu.VMEM((depth, half, n), bf16),
            pltpu.SemaphoreType.DMA((2, depth)),
            pltpu.SemaphoreType.DMA,
        ],
        compiler_params=params(10),
        name="project",
    )(stay(momentum), stay(gradient), keep(basis) if part else stay(basis), *after)


def keep(x):
    return pltpu.with_memory_space_constraint(x, pltpu.VMEM)


def stay(x):
    return pltpu.with_memory_space_constraint(x, pltpu.HBM)


def gather_left(lefts, whole):
    half = lefts[0].shape[1]
    me = lax.axis_index("col")
    for d, ref in enumerate(lefts):
        whole[:, pl.ds(pl.multiple_of(flip(me, d) * half, half), half)] = ref[...]
    return whole


def gram_kernel(*refs):
    lefts, (g_mine, g_other, total) = refs[:-3], refs[-3:]
    core = lax.bitwise_and(lax.axis_index("row"), jnp.int32(1))
    total[...] = sum(dot(ref[...], ref[...], ((1,), (1,))) for ref in lefts)
    h = g_mine.shape[0]
    g_mine[...] = total[pl.ds(pl.multiple_of(core * h, h), h), :]
    g_other[...] = total[pl.ds(pl.multiple_of((1 - core) * h, h), h), :]


def gram(lefts):
    r = lefts[0].shape[0]
    return pl.pallas_call(
        gram_kernel,
        out_shape=[shape((r // 2, r), f32)] * 2,
        in_specs=[VMEM] * len(lefts),
        out_specs=[VMEM] * 2,
        scratch_shapes=[pltpu.VMEM((r, r), f32)],
        compiler_params=params(8),
        name="gram",
    )(*lefts)


def first_kernel(depth, width, buf, *rest):
    lefts, (other, mine, whole) = rest[:depth], rest[depth:]
    core = lax.bitwise_and(lax.axis_index("row"), jnp.int32(1))
    size = other.shape[1]
    gather_left(lefts, whole)
    for out, half in ((other, 1 - core), (mine, core)):

        def step(k, carry, out=out, half=half):
            cols = pl.ds(pl.multiple_of(half * size + k * width, 128), width)
            out[:, pl.ds(pl.multiple_of(k * width, 128), width)] = dot(whole[...], buf[:, cols].astype(bf16))
            return carry

        lax.fori_loop(0, size // width, step, 0)


def first_product(buf, lefts, width):
    m, n = buf.shape
    r = lefts[0].shape[0]
    return pl.pallas_call(
        functools.partial(first_kernel, len(lefts), width),
        out_shape=(shape((r, n // 2), f32), shape((r, n // 2), f32)),
        in_specs=[VMEM] * (1 + len(lefts)),
        out_specs=[VMEM] * 2,
        scratch_shapes=[pltpu.VMEM((r, m), bf16)],
        compiler_params=params(8),
        name="first_product",
    )(keep(buf), *lefts)


def other_kernel(depth, width, buf, sums, *rest):
    lefts, (out, whole) = rest[:depth], rest[-2:]
    core = lax.bitwise_and(lax.axis_index("row"), jnp.int32(1))
    size = out.shape[1]
    gather_left(lefts, whole)

    def step(k, carry):
        cols = pl.ds(pl.multiple_of((1 - core) * size + k * width, 128), width)
        at = pl.ds(pl.multiple_of(k * width, 128), width)
        out[:, at] = (sums[:, at] + dot(whole[...], buf[:, cols].astype(bf16))).astype(bf16)
        return carry

    lax.fori_loop(0, size // width, step, 0)


def other_product(buf, sums, lefts, width, after):
    m, n = buf.shape
    r = lefts[0].shape[0]
    return pl.pallas_call(
        functools.partial(other_kernel, len(lefts), width),
        out_shape=shape((r, n // 2), bf16),
        in_specs=[VMEM] * (2 + len(lefts)) + [ANY],
        out_specs=VMEM,
        scratch_shapes=[pltpu.VMEM((r, m), bf16)],
        compiler_params=params(8),
        name="other_product",
    )(keep(buf), sums, *lefts, after)


def mine_kernel(depth, width, buf, sums, *rest):
    lefts, (out, whole) = rest[:depth], rest[-2:]
    core = lax.bitwise_and(lax.axis_index("row"), jnp.int32(1))
    size = out.shape[1]
    gather_left(lefts, whole)

    def step(k, carry):
        cols = pl.ds(pl.multiple_of(core * size + k * width, 128), width)
        at = pl.ds(pl.multiple_of(k * width, 128), width)
        out[:, at] = sums[:, at] + dot(whole[...], buf[:, cols].astype(bf16))
        return carry

    lax.fori_loop(0, size // width, step, 0)


def mine_product(buf, sums, lefts, width, after):
    m, n = buf.shape
    r = lefts[0].shape[0]
    return pl.pallas_call(
        functools.partial(mine_kernel, len(lefts), width),
        out_shape=shape((r, n // 2), f32),
        in_specs=[VMEM] * (2 + len(lefts)) + [ANY],
        out_specs=VMEM,
        scratch_shapes=[pltpu.VMEM((r, m), bf16)],
        compiler_params=params(8),
        name="mine_product",
    )(keep(buf), sums, *lefts, after)


def pair_sum_kernel(chips, mine, received, _, *outs):
    me = lax.div(lax.axis_index("row"), jnp.int32(2))
    width = outs[0].shape[1]
    for d in range(chips):
        cols = pl.ds(pl.multiple_of(flip(me, d) * width, 128), width)
        outs[d][...] = (mine[:, cols] + received[:, cols].astype(f32)).astype(outs[d].dtype)


def pair_sum(mine, received, chips, after):
    r, n = mine.shape
    kinds = [f32] + [bf16] * (chips - 1)
    return pl.pallas_call(
        functools.partial(pair_sum_kernel, chips),
        out_shape=[shape((r, n // chips), k) for k in kinds],
        in_specs=[VMEM, VMEM, ANY],
        out_specs=[VMEM] * chips,
        compiler_params=params(8),
        name="pair_sum",
    )(mine, received, after)


def share_sum_kernel(own, *refs):
    received, out = refs[:-1], refs[-1]
    out[...] = (own[...] + sum(ref[...].astype(f32) for ref in received)).astype(bf16)


def share_sum(own, received):
    return pl.pallas_call(
        share_sum_kernel,
        out_shape=shape(own.shape, bf16),
        in_specs=[VMEM] * (1 + len(received)),
        out_specs=VMEM,
        compiler_params=params(8),
        name="share_sum",
    )(own, *received)


def eliminate(tiles, at, nb, group):
    sub = lax.broadcasted_iota(jnp.int32, (nb, 128), 0)
    scale = jnp.zeros((nb, 128), f32)
    for g in range(0, nb, group):
        cols = [
            jnp.broadcast_to(tiles[0][:, at + g + j : at + g + j + 1], (nb, 128)) for j in range(group)
        ]
        for j in range(group):
            t = g + j
            pivot = cols[j][t : t + 1, :]
            factor = jnp.where(sub > t, cols[j], 0.0) * (1.0 / pivot)
            scale = jnp.where(sub == t, lax.rsqrt(pivot), scale)
            for l in range(j + 1, group):
                cols[l] = cols[l] - factor * cols[l][t : t + 1, :]
            tiles = [x - factor * x[t : t + 1, :] for x in tiles]
    return [x * scale for x in tiles]


def chol_inverse_kernel(mine, other, out, work):
    n = out.shape[0]
    h = n // 2
    core = lax.bitwise_and(lax.axis_index("row"), jnp.int32(1))
    work[pl.ds(pl.multiple_of(core * h, h), h), :n] = mine[...]
    work[pl.ds(pl.multiple_of((1 - core) * h, h), h), :n] = other[...]
    r_id = lax.broadcasted_iota(jnp.int32, (n, n), 0)
    c_id = lax.broadcasted_iota(jnp.int32, (n, n), 1)
    work[:, n:] = jnp.where(r_id == c_id, 1.0, 0.0).astype(f32)
    nb = 32
    for p in range(n // nb):
        lo = p * nb
        left = (lo // 128) * 128
        right = n + ((lo + nb + 127) // 128) * 128
        tiles = [work[lo : lo + nb, c : c + 128] for c in range(left, right, 128)]
        s = jnp.concatenate(eliminate(tiles, lo - left, nb, 8), axis=1)
        work[lo : lo + nb, left:right] = s
        if lo + nb < n:
            lead = s[:, lo + nb - left : n - left]
            work[lo + nb :, left:right] -= lax.dot_general(
                lead, s, (((0,), (0,)), ((), ())), precision=lax.Precision.HIGHEST, preferred_element_type=f32
            )
    out[...] = jnp.where(r_id >= c_id, work[:, n:], 0.0)


def chol_inverse(mine, other):
    n = mine.shape[1]
    return pl.pallas_call(
        chol_inverse_kernel,
        out_shape=shape((n, n), f32),
        in_specs=[VMEM, VMEM],
        out_specs=VMEM,
        scratch_shapes=[pltpu.VMEM((n, 2 * n), f32)],
        compiler_params=params(8),
        name="chol_inverse",
    )(mine, other)


def ortho_kernel(depth, inverse, *refs):
    lefts, out = refs[: 2 * depth], refs[2 * depth]
    half = lefts[0].shape[1]
    me = lax.axis_index("col")
    parts = split(inverse[...], 3)
    for k, ref in enumerate(lefts):
        part, d = divmod(k, depth)
        rows = pl.ds(pl.multiple_of((2 * flip(me, d) + part) * half, half), half)
        out[rows, :] = sum(dot(ref[...], x, ((0,), (1,))) for x in reversed(parts)).astype(bf16)


def ortho(inverse, lefts):
    r, half = lefts[0].shape
    return pl.pallas_call(
        functools.partial(ortho_kernel, len(lefts) // 2),
        out_shape=shape((half * len(lefts), r), bf16),
        in_specs=[VMEM] * (1 + len(lefts)),
        out_specs=VMEM,
        compiler_params=params(8),
        name="ortho",
    )(inverse, *lefts)


def hand_on(x, *earlier):
    return pl.pallas_call(
        lambda *refs: None,
        out_shape=shape(x.shape, x.dtype),
        in_specs=[ANY] * (1 + len(earlier)),
        out_specs=ANY,
        input_output_aliases={0: 0},
        compiler_params=params(1),
        name="hand_on",
    )(x, *earlier)


def apply_inverse(parts, block):
    return sum(dot(x, block) for x in reversed(parts))


def share_kernel(inverse, own, *refs):
    received, (out, squares) = refs[:-2], refs[-2:]
    out[...] = (own[...] + sum(ref[...].astype(f32) for ref in received)).astype(bf16)
    value = apply_inverse(split(inverse[...], 2), out[...])
    total = jnp.sum(value * value, axis=1, keepdims=True)
    squares[...] = jnp.transpose(jnp.broadcast_to(total, (total.shape[0], 128)))[:8, :]


def share_of(inverse, own, received):
    r = own.shape[0]
    return pl.pallas_call(
        share_kernel,
        out_shape=(shape(own.shape, bf16), shape((8, r), f32)),
        in_specs=[VMEM] * (2 + len(received)),
        out_specs=(VMEM, VMEM),
        compiler_params=params(8),
        name="share",
    )(inverse, own, *received)


def result_kernel(d, factor, buf0, buf1, ortho_ref, inverse, squares, block0, block1, weight, *rest):
    new_weight, new_momentum, basis, mbuf, wbuf, vbuf, nbuf, lbuf, in_sems, out_sems, basis_sems = rest[-11:]
    r, width = block0.shape
    tile = 256
    tiles = width // tile
    half = width * (lax.axis_size("row") // 2)
    row = lax.axis_index("row")
    core = lax.bitwise_and(row, jnp.int32(1))
    chip = flip(lax.div(row, jnp.int32(2)), d)
    starts = [core * half + chip * width, (1 - core) * half + chip * width]
    cols = [pl.ds(pl.multiple_of(start, 128), width) for start in starts]
    loads = [pltpu.make_async_copy(weight.at[:, cols[b]], wbuf.at[b], in_sems.at[b]) for b in range(2)]
    basis_stores = [pltpu.make_async_copy(nbuf.at[b], basis.at[:, cols[b]], basis_sems.at[b]) for b in range(2)]

    def stores(b, t):
        at = pl.ds(pl.multiple_of(t * tile, tile), tile)
        there = pl.ds(pl.multiple_of(starts[b] + t * tile, 128), tile)
        return (
            pltpu.make_async_copy(mbuf.at[b, :, at], new_momentum.at[:, there], out_sems.at[0, b, t]),
            pltpu.make_async_copy(vbuf.at[b, :, at], new_weight.at[:, there], out_sems.at[1, b, t]),
        )

    for load in loads:
        load.start()
    scale = lax.rsqrt(squares[...] / FF + epsilon)
    scale = jnp.transpose(jnp.concatenate([scale] * 16, axis=0))[:, :1]
    parts = split(inverse[...], 2)
    depth = lax.axis_size("col")
    size = buf0.shape[0] // depth
    for b, block in enumerate((block0, block1)):
        right = apply_inverse(parts, block[...])
        lbuf[b] = right.astype(bf16)
        nbuf[b] = (right * scale).astype(bf16)
        basis_stores[b].start()
        loads[b].wait()

        def step(t, carry, b=b):
            at = pl.ds(pl.multiple_of(t * tile, tile), tile)
            there = pl.ds(pl.multiple_of(starts[b] + t * tile, 128), tile)
            correction = dot(ortho_ref[...], lbuf[b, :, at])
            for k in range(2 * depth):
                rows = slice(k * size, (k + 1) * size)
                here = slice(k // 2 * size, (k // 2 + 1) * size)
                old = (buf0, buf1)[k % 2][here, there]
                mbuf[b, rows, at] = old - (1.0 - momentum_decay) * correction[rows]
            change = dot(ortho_ref[...], nbuf[b, :, at])
            vbuf[b, :, at] = (wbuf[b, :, at].astype(f32) - factor * change).astype(bf16)
            for store in stores(b, t):
                store.start()
            return carry

        lax.fori_loop(0, tiles, step, 0)
    for b in range(2):
        basis_stores[b].wait()
        for t in range(tiles):
            for store in stores(b, t):
                store.wait()


def results(d, factor, bufs, ortho_bf, inverse, squares, blocks, weight, before):
    m, n = weight.shape
    r, width = blocks[0].shape
    ins = [*map(keep, bufs), ortho_bf, inverse, squares, *blocks, stay(weight), *map(stay, before)]
    return pl.pallas_call(
        functools.partial(result_kernel, d, factor),
        out_shape=(shape((m, n), bf16), shape((m, n), f32), shape((r, n), bf16)),
        in_specs=[VMEM] * 7 + [ANY] * (1 + len(before)),
        out_specs=[ANY] * 3,
        input_output_aliases={8 + k: k for k in range(len(before))},
        scratch_shapes=[
            pltpu.VMEM((2, m, width), f32),
            pltpu.VMEM((2, m, width), bf16),
            pltpu.VMEM((2, m, width), bf16),
            pltpu.VMEM((2, r, width), bf16),
            pltpu.VMEM((2, r, width), bf16),
            pltpu.SemaphoreType.DMA((2,)),
            pltpu.SemaphoreType.DMA((2, 2, width // 256)),
            pltpu.SemaphoreType.DMA((2,)),
        ],
        compiler_params=params(20),
        name="results",
    )(*ins)


def sum_over(x, axis, least=1):
    d = least
    while d < lax.axis_size(axis):
        x = x + swap(x, axis, d)
        d *= 2
    return x


def exchange(x, axis, count, unit=1):
    return [x] + [swap(x, axis, unit * d) for d in range(1, count)]


def per_device(weight, gradient, momentum, old_basis):
    depth, rows = lax.axis_size("col"), lax.axis_size("row")
    chips = rows // 2
    m, n = momentum.shape
    width = n // rows

    def sum_over_col(own, *sent):
        low = share_sum(own, [swap(x, "col", d + 1) for d, x in enumerate(sent)])
        return exchange(low, "col", depth)

    buf0, kept, *outs = project(momentum, gradient, old_basis, depth, 0)
    left0 = sum_over_col(*outs)
    buf1, *outs = project(momentum, gradient, kept, depth, 1, (outs[1],))
    left1 = sum_over_col(*outs)
    bufs = (buf0, buf1)

    other, mine = first_product(buf0, left0, width)
    g_mine, g_other = gram(left0 + left1)
    other = other_product(buf1, other, left1, width, g_mine)
    g_mine = g_mine + swap(g_other, "row", 1)
    received = swap(other, "row", 1)
    mine = mine_product(buf1, mine, left1, width, other)
    own, *sent = pair_sum(mine, received, chips, g_mine)
    g_mine = sum_over(g_mine, "row", 2)
    got = [swap(x, "row", 2 * (d + 1)) for d, x in enumerate(sent)]
    inverse = chol_inverse(g_mine, swap(g_mine, "row", 1))

    share, squares = share_of(inverse, own, got)
    ortho_bf = ortho(inverse, left0 + left1)
    squares = sum_over(squares, "row", 2)
    share = hand_on(share, squares)
    squares = sum_over(squares + swap(squares, "row", 1), "col")

    factor = step_rate * math.sqrt(D / RANK)
    outs, blocks = (), [share]
    for d in range(1, chips):
        source = share if d < 3 else hand_on(share, blocks[d - 2])
        blocks.append(swap(source, "row", 2 * d))
    for d, block in enumerate(blocks):
        if d > 2:
            block = hand_on(block, outs[2])
        pair = (block, swap(block, "row", 1))
        outs = results(d, factor, bufs, ortho_bf, inverse, squares, pair, weight, outs)
    return tuple(outs)


def plain_per_device(weight, gradient, momentum, old_basis):
    buffer = momentum + gradient.astype(f32)
    buffer_low = buffer.astype(bf16)
    left_factor = lax.psum(dot(buffer_low, old_basis, ((1,), (1,))), "col")
    gram_share = lax.dot_general(
        left_factor,
        left_factor,
        (((0,), (0,)), ((), ())),
        precision=lax.Precision.HIGHEST,
        preferred_element_type=f32,
    )
    chol_factor = jnp.linalg.cholesky(lax.psum(gram_share, "row"))
    orthonormal = lax.linalg.triangular_solve(
        chol_factor, left_factor, left_side=False, lower=True, transpose_a=True
    ).astype(bf16)
    right_share = lax.psum_scatter(
        dot(orthonormal, buffer_low, ((0,), (0,))), "row", scatter_dimension=0, tiled=True
    )
    sum_squares = lax.psum(jnp.sum(right_share * right_share, axis=1), "col")
    scale_share = jnp.sqrt(sum_squares / FF + epsilon)
    basis_share = (right_share / scale_share[:, None]).astype(bf16)
    new_basis = lax.all_gather(basis_share, "row", axis=0, tiled=True)
    col_scale = lax.all_gather(scale_share, "row", axis=0, tiled=True)
    scaled = (orthonormal.astype(f32) * col_scale[None, :]).astype(bf16)
    new_momentum = buffer - (1.0 - momentum_decay) * dot(scaled, new_basis)
    factor = step_rate * math.sqrt(D / RANK)
    new_weight = (weight.astype(f32) - factor * dot(orthonormal, new_basis)).astype(bf16)
    return (new_weight, new_momentum, new_basis)


def power_of_two(k):
    return k > 1 and k & (k - 1) == 0


def solution(mesh):
    rows, depth = mesh.shape["row"], mesh.shape["col"]
    tiled = (
        power_of_two(rows)
        and power_of_two(depth)
        and D % (rows * depth * 128) == 0
        and FF % (rows * depth * 256) == 0
    )
    return jax.shard_map(
        per_device if tiled else plain_per_device,
        mesh=mesh,
        in_specs=(P("row", "col"), P("row", "col"), P("row", "col"), P(None, "col")),
        out_specs=(P("row", "col"), P("row", "col"), P(None, "col")),
        check_vma=False,
    )
```

```python
import functools
import math

import jax
import jax.numpy as jnp
from jax import lax
from jax.experimental import pallas as pl
from jax.experimental.pallas import tpu as pltpu
from jax.sharding import PartitionSpec as P

D = 8192
FF = 24576
RANK = 256

epsilon = 1e-06
momentum_decay = 0.6
step_rate = 0.5

bf16, f32 = jnp.bfloat16, jnp.float32
VMEM = pl.BlockSpec(memory_space=pltpu.VMEM)
ANY = pl.BlockSpec(memory_space=pl.ANY)
MIB = 1 << 20


def shape(dims, kind):
    return jax.ShapeDtypeStruct(dims, kind)


def params(mib):
    return pltpu.CompilerParams(vmem_limit_bytes=mib * MIB)


def dot(a, b, dims=((1,), (0,))):
    return lax.dot_general(a, b, (dims, ((), ())), preferred_element_type=f32)


def split(x, terms):
    parts = []
    for _ in range(terms):
        part = x.astype(bf16)
        parts.append(part)
        x = x - part.astype(f32)
    return parts


def flip(i, d):
    return lax.bitwise_xor(i, jnp.int32(d))


def swap(x, axis, d):
    return lax.ppermute(x, axis, [(i, i ^ d) for i in range(lax.axis_size(axis))])


def block_copies(part, d, mom, grad, buf, gbuf, slot, sems):
    half = gbuf.shape[1]
    block = flip(lax.axis_index("col"), d)
    there = pl.ds(pl.multiple_of((2 * block + part) * half, half), half)
    here = pl.ds(pl.multiple_of(block * half, half), half)
    return (
        pltpu.make_async_copy(mom.at[there, :], buf.at[here, :], sems.at[0, d]),
        pltpu.make_async_copy(grad.at[there, :], gbuf.at[slot], sems.at[1, d]),
    )


def project_block(d, buf, gref, basis, left):
    half, n = gref.shape
    rows = pl.ds(pl.multiple_of(flip(lax.axis_index("col"), d) * half, half), half)
    chunk = 1536 if n % 1536 == 0 else n

    def step(k, acc):
        cols = pl.ds(pl.multiple_of(k * chunk, 128), chunk)
        total = buf[rows, cols] + gref[:, cols].astype(f32)
        buf[rows, cols] = total
        return acc + dot(basis[:, cols], total.astype(bf16), ((1,), (1,)))

    acc = lax.fori_loop(0, n // chunk, step, jnp.zeros((basis.shape[0], half), f32))
    left[...] = acc.astype(left.dtype)


def project_kernel(part, depth, mom, grad, basis, *rest):
    if part == 0:
        (buf, kept), rest = rest[:2], rest[2:]
    else:
        kept, buf, rest = basis, rest[1], rest[2:]
    lefts, (gbuf, sems, basis_sem) = rest[:depth], rest[depth:]
    order = list(reversed(range(depth)))
    copies = [block_copies(part, d, mom, grad, buf, gbuf, d, sems) for d in range(depth)]
    load_basis = pltpu.make_async_copy(basis, kept, basis_sem) if part == 0 else None
    for k, d in enumerate(order):
        for copy in copies[d]:
            copy.start()
        if k == 0 and part == 0:
            load_basis.start()
    for k, d in enumerate(order):
        for copy in copies[d]:
            copy.wait()
        if k == 0 and part == 0:
            load_basis.wait()
        project_block(d, buf, gbuf.at[d], kept, lefts[d])


def project(momentum, gradient, basis, depth, part, after=()):
    m, n = momentum.shape
    r = basis.shape[0]
    half = m // 2 // depth
    kinds = [f32] + [bf16] * (depth - 1)
    kept = [] if part else [pltpu.VMEM((r, n), bf16)]
    return pl.pallas_call(
        functools.partial(project_kernel, part, depth),
        out_shape=(pltpu.VMEM((m // 2, n), f32), *kept, *[shape((r, half), k) for k in kinds]),
        in_specs=[ANY, ANY] + [VMEM if part else ANY] + [ANY] * len(after),
        out_specs=(VMEM,) * (depth + 1 + len(kept)),
        scratch_shapes=[
            pltpu.VMEM((depth, half, n), bf16),
            pltpu.SemaphoreType.DMA((2, depth)),
            pltpu.SemaphoreType.DMA,
        ],
        compiler_params=params(10),
        cost_estimate=cost(momentum, gradient),
        name="project",
    )(stay(momentum), stay(gradient), keep(basis) if part else stay(basis), *after)


def cost(*arrays):
    size = sum(math.prod(x.shape) * x.dtype.itemsize for x in arrays)
    return pl.CostEstimate(flops=0, bytes_accessed=size, transcendentals=0)


def keep(x):
    return pltpu.with_memory_space_constraint(x, pltpu.VMEM)


def stay(x):
    return pltpu.with_memory_space_constraint(x, pltpu.HBM)


def gather_left(lefts, whole):
    half = lefts[0].shape[1]
    me = lax.axis_index("col")
    for d, ref in enumerate(lefts):
        whole[:, pl.ds(pl.multiple_of(flip(me, d) * half, half), half)] = ref[...]
    return whole


def gram_kernel(*refs):
    lefts, (_, g_mine, g_other, total) = refs[:-4], refs[-4:]
    core = lax.bitwise_and(lax.axis_index("row"), jnp.int32(1))
    total[...] = sum(dot(ref[...], ref[...], ((1,), (1,))) for ref in lefts)
    h = g_mine.shape[0]
    g_mine[...] = total[pl.ds(pl.multiple_of(core * h, h), h), :]
    g_other[...] = total[pl.ds(pl.multiple_of((1 - core) * h, h), h), :]


def gram(lefts, after):
    r = lefts[0].shape[0]
    return pl.pallas_call(
        gram_kernel,
        out_shape=[shape((r // 2, r), f32)] * 2,
        in_specs=[VMEM] * len(lefts) + [ANY],
        out_specs=[VMEM] * 2,
        scratch_shapes=[pltpu.VMEM((r, r), f32)],
        compiler_params=params(8),
        name="gram",
    )(*lefts, after)


def first_kernel(depth, width, buf, *rest):
    lefts, (other, mine, whole) = rest[:depth], rest[depth:]
    core = lax.bitwise_and(lax.axis_index("row"), jnp.int32(1))
    size = other.shape[1]
    gather_left(lefts, whole)
    for out, half in ((other, 1 - core), (mine, core)):

        def step(k, carry, out=out, half=half):
            cols = pl.ds(pl.multiple_of(half * size + k * width, 128), width)
            out[:, pl.ds(pl.multiple_of(k * width, 128), width)] = dot(whole[...], buf[:, cols].astype(bf16))
            return carry

        lax.fori_loop(0, size // width, step, 0)


def first_product(buf, lefts, width):
    m, n = buf.shape
    r = lefts[0].shape[0]
    return pl.pallas_call(
        functools.partial(first_kernel, len(lefts), width),
        out_shape=(shape((r, n // 2), f32), shape((r, n // 2), f32)),
        in_specs=[VMEM] * (1 + len(lefts)),
        out_specs=[VMEM] * 2,
        scratch_shapes=[pltpu.VMEM((r, m), bf16)],
        compiler_params=params(8),
        cost_estimate=cost(buf, shape((r, n), f32)),
        name="first_product",
    )(keep(buf), *lefts)


def other_kernel(depth, width, buf, sums, *rest):
    lefts, (out, whole) = rest[:depth], rest[-2:]
    core = lax.bitwise_and(lax.axis_index("row"), jnp.int32(1))
    size = out.shape[1]
    gather_left(lefts, whole)

    def step(k, carry):
        cols = pl.ds(pl.multiple_of((1 - core) * size + k * width, 128), width)
        at = pl.ds(pl.multiple_of(k * width, 128), width)
        out[:, at] = (sums[:, at] + dot(whole[...], buf[:, cols].astype(bf16))).astype(bf16)
        return carry

    lax.fori_loop(0, size // width, step, 0)


def other_product(buf, sums, lefts, width, after):
    m, n = buf.shape
    r = lefts[0].shape[0]
    return pl.pallas_call(
        functools.partial(other_kernel, len(lefts), width),
        out_shape=shape((r, n // 2), bf16),
        in_specs=[VMEM] * (2 + len(lefts)) + [ANY],
        out_specs=VMEM,
        scratch_shapes=[pltpu.VMEM((r, m), bf16)],
        compiler_params=params(8),
        cost_estimate=cost(buf, sums),
        name="other_product",
    )(keep(buf), sums, *lefts, after)


def mine_kernel(depth, width, buf, sums, *rest):
    lefts, (out, whole) = rest[:depth], rest[-2:]
    core = lax.bitwise_and(lax.axis_index("row"), jnp.int32(1))
    size = out.shape[1]
    gather_left(lefts, whole)

    def step(k, carry):
        cols = pl.ds(pl.multiple_of(core * size + k * width, 128), width)
        at = pl.ds(pl.multiple_of(k * width, 128), width)
        out[:, at] = sums[:, at] + dot(whole[...], buf[:, cols].astype(bf16))
        return carry

    lax.fori_loop(0, size // width, step, 0)


def mine_product(buf, sums, lefts, width, *after):
    m, n = buf.shape
    r = lefts[0].shape[0]
    return pl.pallas_call(
        functools.partial(mine_kernel, len(lefts), width),
        out_shape=shape((r, n // 2), f32),
        in_specs=[VMEM] * (2 + len(lefts)) + [ANY] * len(after),
        out_specs=VMEM,
        scratch_shapes=[pltpu.VMEM((r, m), bf16)],
        compiler_params=params(8),
        cost_estimate=cost(buf, sums),
        name="mine_product",
    )(keep(buf), sums, *lefts, *after)


def pair_sum_kernel(chips, mine, received, _, *outs):
    me = lax.div(lax.axis_index("row"), jnp.int32(2))
    width = outs[0].shape[1]
    for d in range(chips):
        cols = pl.ds(pl.multiple_of(flip(me, d) * width, 128), width)
        outs[d][...] = (mine[:, cols] + received[:, cols].astype(f32)).astype(outs[d].dtype)


def pair_sum(mine, received, chips, after):
    r, n = mine.shape
    kinds = [f32] + [bf16] * (chips - 1)
    return pl.pallas_call(
        functools.partial(pair_sum_kernel, chips),
        out_shape=[shape((r, n // chips), k) for k in kinds],
        in_specs=[VMEM, VMEM, ANY],
        out_specs=[VMEM] * chips,
        compiler_params=params(8),
        name="pair_sum",
    )(mine, received, after)


def share_sum_kernel(own, *refs):
    received, out = refs[:-1], refs[-1]
    out[...] = (own[...] + sum(ref[...].astype(f32) for ref in received)).astype(bf16)


def share_sum(own, received):
    return pl.pallas_call(
        share_sum_kernel,
        out_shape=shape(own.shape, bf16),
        in_specs=[VMEM] * (1 + len(received)),
        out_specs=VMEM,
        compiler_params=params(8),
        name="share_sum",
    )(own, *received)


def eliminate(tiles, at, nb, group):
    sub = lax.broadcasted_iota(jnp.int32, (nb, 128), 0)
    scale = jnp.zeros((nb, 128), f32)
    for g in range(0, nb, group):
        cols = [
            jnp.broadcast_to(tiles[0][:, at + g + j : at + g + j + 1], (nb, 128)) for j in range(group)
        ]
        for j in range(group):
            t = g + j
            pivot = cols[j][t : t + 1, :]
            factor = jnp.where(sub > t, cols[j], 0.0) * (1.0 / pivot)
            scale = jnp.where(sub == t, lax.rsqrt(pivot), scale)
            for l in range(j + 1, group):
                cols[l] = cols[l] - factor * cols[l][t : t + 1, :]
            tiles = [x - factor * x[t : t + 1, :] for x in tiles]
    return [x * scale for x in tiles]


def chol_inverse_kernel(mine, other, out, work):
    n = out.shape[0]
    h = n // 2
    core = lax.bitwise_and(lax.axis_index("row"), jnp.int32(1))
    work[pl.ds(pl.multiple_of(core * h, h), h), :n] = mine[...]
    work[pl.ds(pl.multiple_of((1 - core) * h, h), h), :n] = other[...]
    r_id = lax.broadcasted_iota(jnp.int32, (n, n), 0)
    c_id = lax.broadcasted_iota(jnp.int32, (n, n), 1)
    work[:, n:] = jnp.where(r_id == c_id, 1.0, 0.0).astype(f32)
    nb = 32
    for p in range(n // nb):
        lo = p * nb
        left = (lo // 128) * 128
        right = n + ((lo + nb + 127) // 128) * 128
        tiles = [work[lo : lo + nb, c : c + 128] for c in range(left, right, 128)]
        s = jnp.concatenate(eliminate(tiles, lo - left, nb, 8), axis=1)
        work[lo : lo + nb, left:right] = s
        if lo + nb < n:
            lead = s[:, lo + nb - left : n - left]
            work[lo + nb :, left:right] -= lax.dot_general(
                lead, s, (((0,), (0,)), ((), ())), precision=lax.Precision.HIGHEST, preferred_element_type=f32
            )
    out[...] = jnp.where(r_id >= c_id, work[:, n:], 0.0)


def chol_inverse(mine, other):
    n = mine.shape[1]
    return pl.pallas_call(
        chol_inverse_kernel,
        out_shape=shape((n, n), f32),
        in_specs=[VMEM, VMEM],
        out_specs=VMEM,
        scratch_shapes=[pltpu.VMEM((n, 2 * n), f32)],
        compiler_params=params(8),
        cost_estimate=cost(*[mine] * 256),
        name="chol_inverse",
    )(mine, other)


def ortho_kernel(depth, inverse, *refs):
    lefts, out = refs[: 2 * depth], refs[2 * depth]
    half = lefts[0].shape[1]
    me = lax.axis_index("col")
    parts = split(inverse[...], 3)
    for k, ref in enumerate(lefts):
        part, d = divmod(k, depth)
        rows = pl.ds(pl.multiple_of((2 * flip(me, d) + part) * half, half), half)
        out[rows, :] = sum(dot(ref[...], x, ((0,), (1,))) for x in reversed(parts)).astype(bf16)


def ortho(inverse, lefts):
    r, half = lefts[0].shape
    return pl.pallas_call(
        functools.partial(ortho_kernel, len(lefts) // 2),
        out_shape=shape((half * len(lefts), r), bf16),
        in_specs=[VMEM] * (1 + len(lefts)),
        out_specs=VMEM,
        compiler_params=params(8),
        cost_estimate=cost(*[shape((half * len(lefts), r), bf16)] * 8),
        name="ortho",
    )(inverse, *lefts)


def hand_on(x, *earlier):
    return pl.pallas_call(
        lambda *refs: None,
        out_shape=shape(x.shape, x.dtype),
        in_specs=[ANY] * (1 + len(earlier)),
        out_specs=ANY,
        input_output_aliases={0: 0},
        compiler_params=params(1),
        name="hand_on",
    )(x, *earlier)


def apply_inverse(parts, block):
    return sum(dot(x, block) for x in reversed(parts))


def share_kernel(inverse, own, *refs):
    received, (out, squares) = refs[:-2], refs[-2:]
    out[...] = (own[...] + sum(ref[...].astype(f32) for ref in received)).astype(bf16)
    value = apply_inverse(split(inverse[...], 2), out[...])
    total = jnp.sum(value * value, axis=1, keepdims=True)
    squares[...] = jnp.transpose(jnp.broadcast_to(total, (total.shape[0], 128)))[:8, :]


def share_of(inverse, own, received):
    r = own.shape[0]
    return pl.pallas_call(
        share_kernel,
        out_shape=(shape(own.shape, bf16), shape((8, r), f32)),
        in_specs=[VMEM] * (2 + len(received)),
        out_specs=(VMEM, VMEM),
        compiler_params=params(8),
        name="share",
    )(inverse, own, *received)


def result_kernel(pairs, factor, buf0, buf1, ortho_ref, inverse, squares, *refs):
    blocks, (weight, *rest) = refs[: 2 * len(pairs)], refs[2 * len(pairs) :]
    *_, new_weight, new_momentum, basis, token, mbuf, wbuf, vbuf, nbuf, lbuf, in_sems, out_sems, basis_sems = rest
    r, width = blocks[0].shape
    tile = 256
    tiles = width // tile
    count = len(blocks)
    half = width * (lax.axis_size("row") // 2)
    row = lax.axis_index("row")
    core = lax.bitwise_and(row, jnp.int32(1))
    chip = lax.div(row, jnp.int32(2))
    starts = []
    for d in pairs:
        starts += [core * half + flip(chip, d) * width, (1 - core) * half + flip(chip, d) * width]

    def cols(b):
        return pl.ds(pl.multiple_of(starts[b], 128), width)

    def load(b):
        return pltpu.make_async_copy(weight.at[:, cols(b)], wbuf.at[b % 2], in_sems.at[b % 2])

    def store_basis(b):
        return pltpu.make_async_copy(nbuf.at[b % 2], basis.at[:, cols(b)], basis_sems.at[b % 2])

    def stores(b, t):
        at = pl.ds(t * tile, tile)
        there = pl.ds(pl.multiple_of(starts[b] + t * tile, 128), tile)
        return (
            pltpu.make_async_copy(mbuf.at[b % 2, :, at], new_momentum.at[:, there], out_sems.at[0, b % 2, t]),
            pltpu.make_async_copy(vbuf.at[b % 2, :, at], new_weight.at[:, there], out_sems.at[1, b % 2, t]),
        )

    def finish(b):
        store_basis(b).wait()
        for t in range(tiles):
            for store in stores(b, t):
                store.wait()

    for b in range(2):
        load(b).start()
    scale = lax.rsqrt(squares[...] / FF + epsilon)
    scale = jnp.transpose(jnp.concatenate([scale] * 16, axis=0))[:, :1]
    token[...] = jnp.zeros_like(token)
    parts = split(inverse[...], 2)
    depth = lax.axis_size("col")
    size = buf0.shape[0] // depth
    for b in range(count):
        k = b % 2
        if b >= 2:
            finish(b - 2)
        right = apply_inverse(parts, blocks[b][...])
        lbuf[k] = ((1.0 - momentum_decay) * right).astype(bf16)
        nbuf[k] = (right * scale).astype(bf16)
        store_basis(b).start()
        load(b).wait()
        for t in range(tiles):
            at = slice(t * tile, (t + 1) * tile)
            there = pl.ds(pl.multiple_of(starts[b] + t * tile, 128), tile)
            correction = dot(ortho_ref[...], lbuf[k, :, at])
            for j in range(2 * depth):
                rows = slice(j * size, (j + 1) * size)
                here = slice(j // 2 * size, (j // 2 + 1) * size)
                mbuf[k, rows, at] = (buf0, buf1)[j % 2][here, there] - correction[rows]
            change = dot(ortho_ref[...], nbuf[k, :, at])
            vbuf[k, :, at] = (wbuf[k, :, at].astype(f32) - factor * change).astype(bf16)
            for store in stores(b, t):
                store.start()
        if b + 2 < count:
            load(b + 2).start()
    for b in range(count - 2, count):
        finish(b)


def results(pairs, factor, bufs, ortho_bf, inverse, squares, blocks, weight, outs):
    m, n = weight.shape
    r, width = blocks[0].shape
    ins = [*map(keep, bufs), ortho_bf, inverse, squares, *blocks, stay(weight), *map(stay, outs)]
    at = len(ins) - len(outs)
    *outs, token = pl.pallas_call(
        functools.partial(result_kernel, pairs, factor),
        out_shape=[shape((m, n), bf16), shape((m, n), f32), shape((r, n), bf16), shape((8, 128), f32)],
        in_specs=[VMEM] * (5 + len(blocks)) + [ANY] * (1 + len(outs)),
        out_specs=[ANY] * 3 + [VMEM],
        input_output_aliases={at + k: k for k in range(len(outs))},
        scratch_shapes=[
            pltpu.VMEM((2, m, width), f32),
            pltpu.VMEM((2, m, width), bf16),
            pltpu.VMEM((2, m, width), bf16),
            pltpu.VMEM((2, r, width), bf16),
            pltpu.VMEM((2, r, width), bf16),
            pltpu.SemaphoreType.DMA((2,)),
            pltpu.SemaphoreType.DMA((2, 2, width // 256)),
            pltpu.SemaphoreType.DMA((2,)),
        ],
        compiler_params=params(20),
        cost_estimate=cost(*[shape((m, width), f32)] * (2 * len(blocks))),
        name="results",
    )(*ins)
    return outs, token


def sum_over(x, axis, least=1):
    d = least
    while d < lax.axis_size(axis):
        x = x + swap(x, axis, d)
        d *= 2
    return x


def exchange(x, axis, count, unit=1):
    return [x] + [swap(x, axis, unit * d) for d in range(1, count)]


def pair_up(terms):
    while len(terms) > 1:
        terms = [terms[2 * i] + terms[2 * i + 1] for i in range(len(terms) // 2)]
    return terms[0]


def gather(x, axis):
    blocks = [x]
    size = lax.axis_size(axis)
    for d in range(1, size):
        low = d & -d
        blocks.append(swap(blocks[d - low] if d != low else x, axis, low))
    return blocks


def per_device(weight, gradient, momentum, old_basis):
    depth, rows = lax.axis_size("col"), lax.axis_size("row")
    chips = rows // 2
    m, n = momentum.shape
    width = n // rows

    def sum_over_col(own, *sent):
        return gather(share_sum(own, [swap(x, "col", d + 1) for d, x in enumerate(sent)]), "col")

    buf0, kept, *outs = project(momentum, gradient, old_basis, depth, 0)
    left0 = sum_over_col(*outs)
    buf1, *outs = project(momentum, gradient, kept, depth, 1, (outs[1],))
    left1 = sum_over_col(*outs)
    bufs = (buf0, buf1)

    other, mine = first_product(buf0, left0, width)
    g_mine, g_other = gram(left0 + left1, other)
    other = other_product(buf1, other, left1, width, g_mine)
    g_mine = g_mine + swap(g_other, "row", 1)
    received = swap(hand_on(other, g_mine), "row", 1)
    mine = mine_product(buf1, mine, left1, width, g_mine, other)
    g_mine = sum_over(g_mine, "row", 2)
    own, *sent = pair_sum(mine, received, chips, g_mine)
    got = [swap(x, "row", 2 * (d + 1)) for d, x in enumerate(sent)]
    inverse = chol_inverse(g_mine, swap(g_mine, "row", 1))

    share, squares = share_of(inverse, own, got)
    ortho_bf = ortho(inverse, left0 + left1)
    squares = pair_up(exchange(squares, "row", chips, 2))
    share = hand_on(share, squares)
    squares = pair_up(exchange(squares + swap(squares, "row", 1), "col", depth))

    factor = step_rate * math.sqrt(D / RANK)
    near = min(3, chips)
    blocks = [share] + [swap(share, "row", 2 * d) for d in range(1, near)]
    blocks = [share] + [hand_on(x, squares) for x in blocks[1:]]
    for d in range(near, chips):
        share = hand_on(share, blocks[d - 2])
        blocks.append(swap(share, "row", 2 * d))
    blocks[0] = share
    pairs = [x for block in blocks[:near] for x in (block, swap(block, "row", 1))]
    common = (factor, bufs, ortho_bf, inverse, squares)
    outs, token = results(tuple(range(near)), *common, pairs, weight, [])
    for d in range(near, chips):
        block = hand_on(blocks[d], token)
        outs, token = results((d,), *common, (block, swap(block, "row", 1)), weight, outs)
    return tuple(outs)


def plain_per_device(weight, gradient, momentum, old_basis):
    buffer = momentum + gradient.astype(f32)
    buffer_low = buffer.astype(bf16)
    left_factor = lax.psum(dot(buffer_low, old_basis, ((1,), (1,))), "col")
    gram_share = lax.dot_general(
        left_factor,
        left_factor,
        (((0,), (0,)), ((), ())),
        precision=lax.Precision.HIGHEST,
        preferred_element_type=f32,
    )
    chol_factor = jnp.linalg.cholesky(lax.psum(gram_share, "row"))
    orthonormal = lax.linalg.triangular_solve(
        chol_factor, left_factor, left_side=False, lower=True, transpose_a=True
    ).astype(bf16)
    right_share = lax.psum_scatter(
        dot(orthonormal, buffer_low, ((0,), (0,))), "row", scatter_dimension=0, tiled=True
    )
    sum_squares = lax.psum(jnp.sum(right_share * right_share, axis=1), "col")
    scale_share = jnp.sqrt(sum_squares / FF + epsilon)
    basis_share = (right_share / scale_share[:, None]).astype(bf16)
    new_basis = lax.all_gather(basis_share, "row", axis=0, tiled=True)
    col_scale = lax.all_gather(scale_share, "row", axis=0, tiled=True)
    scaled = (orthonormal.astype(f32) * col_scale[None, :]).astype(bf16)
    new_momentum = buffer - (1.0 - momentum_decay) * dot(scaled, new_basis)
    factor = step_rate * math.sqrt(D / RANK)
    new_weight = (weight.astype(f32) - factor * dot(orthonormal, new_basis)).astype(bf16)
    return (new_weight, new_momentum, new_basis)


def power_of_two(k):
    return k > 1 and k & (k - 1) == 0


def solution(mesh):
    rows, depth = mesh.shape["row"], mesh.shape["col"]
    tiled = (
        power_of_two(rows)
        and power_of_two(depth)
        and D % (rows * depth * 128) == 0
        and FF % (rows * depth * 256) == 0
    )
    return jax.shard_map(
        per_device if tiled else plain_per_device,
        mesh=mesh,
        in_specs=(P("row", "col"), P("row", "col"), P("row", "col"), P(None, "col")),
        out_specs=(P("row", "col"), P("row", "col"), P(None, "col")),
        check_vma=False,
    )
```

```python
import functools
import math

import jax
import jax.numpy as jnp
from jax import lax
from jax.experimental import pallas as pl
from jax.experimental.pallas import tpu as pltpu
from jax.sharding import PartitionSpec as P

D = 8192
FF = 24576
RANK = 256

epsilon = 1e-06
momentum_decay = 0.6
step_rate = 0.5

bf16, f32 = jnp.bfloat16, jnp.float32
VMEM = pl.BlockSpec(memory_space=pltpu.VMEM)
ANY = pl.BlockSpec(memory_space=pl.ANY)
MIB = 1 << 20


def shape(dims, kind):
    return jax.ShapeDtypeStruct(dims, kind)


def params(mib):
    return pltpu.CompilerParams(vmem_limit_bytes=mib * MIB)


def dot(a, b, dims=((1,), (0,))):
    return lax.dot_general(a, b, (dims, ((), ())), preferred_element_type=f32)


def split(x, terms):
    parts = []
    for _ in range(terms):
        part = x.astype(bf16)
        parts.append(part)
        x = x - part.astype(f32)
    return parts


def flip(i, d):
    return lax.bitwise_xor(i, jnp.int32(d))


def swap(x, axis, d):
    return lax.ppermute(x, axis, [(i, i ^ d) for i in range(lax.axis_size(axis))])


def project_kernel(part, depth, width, mom, grad, basis, *rest):
    if part == 0:
        (buf, kept), rest = rest[:2], rest[2:]
    else:
        kept, buf, rest = basis, rest[1], rest[2:]
    held, sent, gbuf, total, sems, basis_sem = rest
    m, n = buf.shape
    half = m // depth

    def copies(c):
        cols = pl.ds(pl.multiple_of(c * width, 128), width)
        pairs = []
        for k in range(depth):
            there = pl.ds((2 * k + part) * half, half)
            here = pl.ds(k * half, half)
            pairs.append(pltpu.make_async_copy(mom.at[there, cols], buf.at[here, cols], sems.at[0, k, c]))
            pairs.append(pltpu.make_async_copy(grad.at[there, cols], gbuf.at[here, cols], sems.at[1, k, c]))
        if part == 0:
            pairs.append(pltpu.make_async_copy(basis.at[:, cols], kept.at[:, cols], basis_sem.at[c]))
        return pairs

    def start(c, carry):
        for copy in copies(c):
            copy.start()
        return carry

    def step(c, carry):
        for copy in copies(c):
            copy.wait()
        cols = pl.ds(pl.multiple_of(c * width, 128), width)
        added = buf[:, cols] + gbuf[:, cols].astype(f32)
        buf[:, cols] = added
        total[...] += dot(added.astype(bf16), kept[:, cols], ((1,), (1,)))
        return carry

    total[...] = jnp.zeros_like(total)
    lax.fori_loop(0, n // width, start, 0)
    lax.fori_loop(0, n // width, step, 0)
    me = lax.axis_index("col")
    for out, odd in ((held, 0), (sent, 1)):
        for j in range(depth // 2):
            rows = pl.ds(pl.multiple_of(flip(me, 2 * j + odd) * half, half), half)
            out[:, j * half : (j + 1) * half] = jnp.transpose(total[rows, :]).astype(out.dtype)


def project(momentum, gradient, basis, depth, width, part, after=()):
    m, n = momentum.shape
    m = m // 2
    r = basis.shape[0]
    kept = [] if part else [pltpu.VMEM((r, n), bf16)]
    return pl.pallas_call(
        functools.partial(project_kernel, part, depth, width),
        out_shape=(pltpu.VMEM((m, n), f32), *kept, shape((r, m // 2), f32), shape((r, m // 2), bf16)),
        in_specs=[ANY, ANY] + [VMEM if part else ANY] + [ANY] * len(after),
        out_specs=(VMEM,) * (3 + len(kept)),
        scratch_shapes=[
            pltpu.VMEM((m, n), bf16),
            pltpu.VMEM((m, r), f32),
            pltpu.SemaphoreType.DMA((2, depth, n // width)),
            pltpu.SemaphoreType.DMA((n // width,)),
        ],
        compiler_params=params(14),
        cost_estimate=cost(momentum, gradient),
        name="project",
    )(stay(momentum), stay(gradient), keep(basis) if part else stay(basis), *after)


def fold_kernel(half, held, received, held_out, sent_out):
    added = held[...] + received[...].astype(f32)
    for j in range(held_out.shape[1] // half):
        at = slice(j * half, (j + 1) * half)
        held_out[:, at] = added[:, 2 * j * half : (2 * j + 1) * half]
        sent_out[:, at] = added[:, (2 * j + 1) * half : (2 * j + 2) * half].astype(bf16)


def fold(held, received, half):
    r, size = held.shape
    return pl.pallas_call(
        functools.partial(fold_kernel, half),
        out_shape=(shape((r, size // 2), f32), shape((r, size // 2), bf16)),
        in_specs=[VMEM, VMEM],
        out_specs=(VMEM, VMEM),
        compiler_params=params(8),
        name="fold",
    )(held, received)


def fold_last_kernel(held, received, *rest):
    before, out = rest[:-1], rest[-1]
    half = held.shape[1]
    for k, ref in enumerate(before):
        out[:, k * half : (k + 1) * half] = ref[...]
    out[:, len(before) * half :] = (held[...] + received[...].astype(f32)).astype(bf16)


def fold_last(held, received, *before):
    r, half = held.shape
    return pl.pallas_call(
        fold_last_kernel,
        out_shape=shape((r, half * (1 + len(before))), bf16),
        in_specs=[VMEM] * (2 + len(before)),
        out_specs=VMEM,
        compiler_params=params(8),
        name="fold_last",
    )(held, received, *before)


def cost(*arrays):
    size = sum(math.prod(x.shape) * x.dtype.itemsize for x in arrays)
    return pl.CostEstimate(flops=0, bytes_accessed=size, transcendentals=0)


def keep(x):
    return pltpu.with_memory_space_constraint(x, pltpu.VMEM)


def stay(x):
    return pltpu.with_memory_space_constraint(x, pltpu.HBM)


def buffer_rows(bufs, ds, depth, cols):
    half = bufs[0].shape[0] // depth
    me = lax.axis_index("col")
    rows = [pl.ds(pl.multiple_of(flip(me, d) * half, half), half) for d in ds]
    return jnp.concatenate([buf[at, cols].astype(bf16) for at in rows for buf in bufs], axis=0)


def first_kernel(depth, width, buf0, buf1, *rest):
    lefts, (other, mine, gram, whole) = rest[:-4], rest[-4:]
    core = lax.bitwise_and(lax.axis_index("row"), jnp.int32(1))
    size = other.shape[1]
    block = lefts[0].shape[1]
    for d, ref in enumerate(lefts):
        whole[:, d * block : (d + 1) * block] = ref[...]
    gram[...] = dot(whole[...], whole[...], ((1,), (1,)))
    for out, half in ((other, 1 - core), (mine, core)):

        def step(k, carry, out=out, half=half):
            cols = pl.ds(pl.multiple_of(half * size + k * width, 128), width)
            b = buffer_rows((buf0, buf1), range(len(lefts)), depth, cols)
            out[:, pl.ds(pl.multiple_of(k * width, 128), width)] = dot(whole[...], b)
            return carry

        lax.fori_loop(0, size // width, step, 0)


def first_product(bufs, lefts, depth, width):
    m, n = bufs[0].shape
    r, block = lefts[0].shape
    return pl.pallas_call(
        functools.partial(first_kernel, depth, width),
        out_shape=(shape((r, n // 2), f32), shape((r, n // 2), f32), shape((r, r), f32)),
        in_specs=[VMEM] * (2 + len(lefts)),
        out_specs=[VMEM] * 3,
        scratch_shapes=[pltpu.VMEM((r, block * len(lefts)), bf16)],
        compiler_params=params(10),
        cost_estimate=cost(*bufs, shape((r, n), f32)),
        name="first_product",
    )(*map(keep, bufs), *lefts)


def gram_kernel(left, sums, g_mine, g_other, total):
    core = lax.bitwise_and(lax.axis_index("row"), jnp.int32(1))
    total[...] = sums[...] + dot(left[...], left[...], ((1,), (1,)))
    h = g_mine.shape[0]
    g_mine[...] = total[pl.ds(pl.multiple_of(core * h, h), h), :]
    g_other[...] = total[pl.ds(pl.multiple_of((1 - core) * h, h), h), :]


def gram(left, sums):
    r = left.shape[0]
    return pl.pallas_call(
        gram_kernel,
        out_shape=[shape((r // 2, r), f32)] * 2,
        in_specs=[VMEM, VMEM],
        out_specs=[VMEM] * 2,
        scratch_shapes=[pltpu.VMEM((r, r), f32)],
        compiler_params=params(8),
        name="gram",
    )(left, sums)


def last_kernel(depth, width, mine, buf0, buf1, sums, left, *rest):
    out = rest[-1]
    core = lax.bitwise_and(lax.axis_index("row"), jnp.int32(1))
    half = core if mine else 1 - core
    size = out.shape[1]

    def step(k, carry):
        cols = pl.ds(pl.multiple_of(half * size + k * width, 128), width)
        at = pl.ds(pl.multiple_of(k * width, 128), width)
        b = buffer_rows((buf0, buf1), [depth - 1], depth, cols)
        out[:, at] = (sums[:, at] + dot(left[...], b)).astype(out.dtype)
        return carry

    lax.fori_loop(0, size // width, step, 0)


def last_product(bufs, sums, left, depth, width, mine, *after):
    return pl.pallas_call(
        functools.partial(last_kernel, depth, width, mine),
        out_shape=shape(sums.shape, f32 if mine else bf16),
        in_specs=[VMEM] * 4 + [ANY] * len(after),
        out_specs=VMEM,
        compiler_params=params(8),
        cost_estimate=cost(*bufs[:1], sums),
        name="mine_product" if mine else "other_product",
    )(*map(keep, bufs), sums, left, *after)


def pair_sum_kernel(chips, mine, received, _, *outs):
    me = lax.div(lax.axis_index("row"), jnp.int32(2))
    width = outs[0].shape[1]
    for d in range(chips):
        cols = pl.ds(pl.multiple_of(flip(me, d) * width, 128), width)
        outs[d][...] = (mine[:, cols] + received[:, cols].astype(f32)).astype(outs[d].dtype)


def pair_sum(mine, received, chips, after):
    r, n = mine.shape
    kinds = [f32] + [bf16] * (chips - 1)
    return pl.pallas_call(
        functools.partial(pair_sum_kernel, chips),
        out_shape=[shape((r, n // chips), k) for k in kinds],
        in_specs=[VMEM, VMEM, ANY],
        out_specs=[VMEM] * chips,
        compiler_params=params(8),
        name="pair_sum",
    )(mine, received, after)


def eliminate(tiles, at, nb, group):
    sub = lax.broadcasted_iota(jnp.int32, (nb, 128), 0)
    scale = jnp.zeros((nb, 128), f32)
    for g in range(0, nb, group):
        cols = [
            jnp.broadcast_to(tiles[0][:, at + g + j : at + g + j + 1], (nb, 128)) for j in range(group)
        ]
        for j in range(group):
            t = g + j
            pivot = cols[j][t : t + 1, :]
            factor = jnp.where(sub > t, cols[j], 0.0) * (1.0 / pivot)
            scale = jnp.where(sub == t, lax.rsqrt(pivot), scale)
            for l in range(j + 1, group):
                cols[l] = cols[l] - factor * cols[l][t : t + 1, :]
            tiles = [x - factor * x[t : t + 1, :] for x in tiles]
    return [x * scale for x in tiles]


def chol_inverse_kernel(mine, other, out, work):
    n = out.shape[0]
    h = n // 2
    core = lax.bitwise_and(lax.axis_index("row"), jnp.int32(1))
    work[pl.ds(pl.multiple_of(core * h, h), h), :n] = mine[...]
    work[pl.ds(pl.multiple_of((1 - core) * h, h), h), :n] = other[...]
    r_id = lax.broadcasted_iota(jnp.int32, (n, n), 0)
    c_id = lax.broadcasted_iota(jnp.int32, (n, n), 1)
    work[:, n:] = jnp.where(r_id == c_id, 1.0, 0.0).astype(f32)
    nb = 32
    for p in range(n // nb):
        lo = p * nb
        left = (lo // 128) * 128
        right = n + ((lo + nb + 127) // 128) * 128
        tiles = [work[lo : lo + nb, c : c + 128] for c in range(left, right, 128)]
        s = jnp.concatenate(eliminate(tiles, lo - left, nb, 8), axis=1)
        work[lo : lo + nb, left:right] = s
        if lo + nb < n:
            lead = s[:, lo + nb - left : n - left]
            work[lo + nb :, left:right] -= lax.dot_general(
                lead, s, (((0,), (0,)), ((), ())), precision=lax.Precision.HIGHEST, preferred_element_type=f32
            )
    out[...] = jnp.where(r_id >= c_id, work[:, n:], 0.0)


def chol_inverse(mine, other):
    n = mine.shape[1]
    return pl.pallas_call(
        chol_inverse_kernel,
        out_shape=shape((n, n), f32),
        in_specs=[VMEM, VMEM],
        out_specs=VMEM,
        scratch_shapes=[pltpu.VMEM((n, 2 * n), f32)],
        compiler_params=params(8),
        cost_estimate=cost(*[mine] * 256),
        name="chol_inverse",
    )(mine, other)


def ortho_kernel(inverse, *refs):
    lefts, out = refs[:-1], refs[-1]
    block = lefts[0].shape[1]
    me = lax.axis_index("col")
    parts = split(inverse[...], 3)
    for d, ref in enumerate(lefts):
        rows = pl.ds(pl.multiple_of(flip(me, d) * block, block), block)
        out[rows, :] = sum(dot(ref[...], x, ((0,), (1,))) for x in reversed(parts)).astype(bf16)


def ortho(inverse, lefts):
    r, block = lefts[0].shape
    return pl.pallas_call(
        ortho_kernel,
        out_shape=shape((block * len(lefts), r), bf16),
        in_specs=[VMEM] * (1 + len(lefts)),
        out_specs=VMEM,
        compiler_params=params(8),
        cost_estimate=cost(*[shape((block * len(lefts), r), bf16)] * 8),
        name="ortho",
    )(inverse, *lefts)


def hand_on(x, *earlier):
    return pl.pallas_call(
        lambda *refs: None,
        out_shape=shape(x.shape, x.dtype),
        in_specs=[ANY] * (1 + len(earlier)),
        out_specs=ANY,
        input_output_aliases={0: 0},
        compiler_params=params(1),
        name="hand_on",
    )(x, *earlier)


def apply_inverse(parts, block):
    return sum(dot(x, block) for x in reversed(parts))


def share_kernel(inverse, own, *refs):
    received, (out, squares) = refs[:-2], refs[-2:]
    out[...] = (own[...] + sum(ref[...].astype(f32) for ref in received)).astype(bf16)
    value = apply_inverse(split(inverse[...], 2), out[...])
    total = jnp.sum(value * value, axis=1, keepdims=True)
    squares[...] = jnp.transpose(jnp.broadcast_to(total, (total.shape[0], 128)))[:8, :]


def share_of(inverse, own, received):
    r = own.shape[0]
    return pl.pallas_call(
        share_kernel,
        out_shape=(shape(own.shape, bf16), shape((8, r), f32)),
        in_specs=[VMEM] * (2 + len(received)),
        out_specs=(VMEM, VMEM),
        compiler_params=params(8),
        name="share",
    )(inverse, own, *received)


def result_kernel(pairs, factor, buf0, buf1, ortho_ref, inverse, squares, weight, *refs):
    blocks, rest = refs[: 2 * len(pairs)], refs[2 * len(pairs) :]
    *_, new_weight, new_momentum, basis, token, mbuf, wbuf, vbuf, nbuf, lbuf, in_sems, out_sems, basis_sems = rest
    r, width = blocks[0].shape
    tile = 256
    tiles = width // tile
    count = len(blocks)
    half = width * (lax.axis_size("row") // 2)
    row = lax.axis_index("row")
    core = lax.bitwise_and(row, jnp.int32(1))
    chip = lax.div(row, jnp.int32(2))
    starts = []
    for d in pairs:
        starts += [core * half + flip(chip, d) * width, (1 - core) * half + flip(chip, d) * width]

    def load(b):
        cols = pl.ds(pl.multiple_of(starts[b], 128), width)
        return pltpu.make_async_copy(weight.at[:, cols], wbuf.at[b % 2], in_sems.at[b % 2])

    def store_basis(b):
        cols = pl.ds(pl.multiple_of(starts[b], 128), width)
        return pltpu.make_async_copy(nbuf.at[b % 2], basis.at[:, cols], basis_sems.at[b % 2])

    def place(b, t):
        return pl.ds(t * tile, tile), pl.ds(pl.multiple_of(starts[b] + t * tile, 128), tile)

    def store_momentum(b, t):
        at, there = place(b, t)
        return pltpu.make_async_copy(mbuf.at[b % 2, :, at], new_momentum.at[:, there], out_sems.at[0, b % 2, t])

    def store_weight(b, t):
        at, there = place(b, t)
        return pltpu.make_async_copy(vbuf.at[b % 2, :, at], new_weight.at[:, there], out_sems.at[1, b % 2, t])

    def finish(b):
        store_basis(b).wait()
        for t in range(tiles):
            store_momentum(b, t).wait()
            store_weight(b, t).wait()

    for b in range(2):
        load(b).start()
    scale = lax.rsqrt(squares[...] / FF + epsilon)
    scale = jnp.transpose(jnp.concatenate([scale] * 16, axis=0))[:, :1]
    token[...] = jnp.zeros_like(token)
    parts = split(inverse[...], 2)
    depth = lax.axis_size("col")
    size = buf0.shape[0] // depth
    for b in range(count):
        k = b % 2
        if b >= 2:
            finish(b - 2)
        right = apply_inverse(parts, blocks[b][...])
        lbuf[k] = ((1.0 - momentum_decay) * right).astype(bf16)
        nbuf[k] = (right * scale).astype(bf16)
        store_basis(b).start()
        for t in range(tiles):
            at, there = place(b, t)
            correction = dot(ortho_ref[...], lbuf[k, :, at])
            for j in range(2 * depth):
                rows = slice(j * size, (j + 1) * size)
                here = slice(j // 2 * size, (j // 2 + 1) * size)
                mbuf[k, rows, at] = (buf0, buf1)[j % 2][here, there] - correction[rows]
            store_momentum(b, t).start()
        load(b).wait()
        for t in range(tiles):
            at, there = place(b, t)
            change = dot(ortho_ref[...], nbuf[k, :, at])
            vbuf[k, :, at] = (wbuf[k, :, at].astype(f32) - factor * change).astype(bf16)
            store_weight(b, t).start()
        if b + 2 < count:
            load(b + 2).start()
    for b in range(count - 2, count):
        finish(b)


def results(pairs, factor, bufs, ortho_bf, inverse, squares, weight, blocks, outs):
    m, n = weight.shape
    r, width = blocks[0].shape
    ins = [*map(keep, bufs), ortho_bf, inverse, squares, stay(weight), *blocks, *map(stay, outs)]
    at = len(ins) - len(outs)
    *outs, token = pl.pallas_call(
        functools.partial(result_kernel, pairs, factor),
        out_shape=[shape((m, n), bf16), shape((m, n), f32), shape((r, n), bf16), shape((8, 128), f32)],
        in_specs=[VMEM] * 5 + [ANY] + [VMEM] * len(blocks) + [ANY] * len(outs),
        out_specs=[ANY] * 3 + [VMEM],
        input_output_aliases={at + k: k for k in range(len(outs))},
        scratch_shapes=[
            pltpu.VMEM((2, m, width), f32),
            pltpu.VMEM((2, m, width), bf16),
            pltpu.VMEM((2, m, width), bf16),
            pltpu.VMEM((2, r, width), bf16),
            pltpu.VMEM((2, r, width), bf16),
            pltpu.SemaphoreType.DMA((2,)),
            pltpu.SemaphoreType.DMA((2, 2, width // 256)),
            pltpu.SemaphoreType.DMA((2,)),
        ],
        compiler_params=params(15),
        cost_estimate=cost(*[shape((m, width), f32)] * (2 * len(blocks))),
        name="results",
    )(*ins)
    return outs, token


def sum_over(x, axis, least=1):
    d = least
    while d < lax.axis_size(axis):
        x = x + swap(x, axis, d)
        d *= 2
    return x


def exchange(x, axis, count, unit=1):
    return [x] + [swap(x, axis, unit * d) for d in range(1, count)]


def pair_up(terms):
    while len(terms) > 1:
        terms = [terms[2 * i] + terms[2 * i + 1] for i in range(len(terms) // 2)]
    return terms[0]


def gather(x, axis):
    blocks = [x]
    size = lax.axis_size(axis)
    for d in range(1, size):
        low = d & -d
        blocks.append(swap(blocks[d - low] if d != low else x, axis, low))
    return blocks


def per_device(weight, gradient, momentum, old_basis):
    depth, rows = lax.axis_size("col"), lax.axis_size("row")
    chips = rows // 2
    m, n = momentum.shape
    width = n // rows

    def sum_over_col(held, sent, *before):
        half = m // 2 // depth
        d = 1
        while held.shape[1] > half:
            held, sent = fold(held, swap(sent, "col", d), half)
            d *= 2
        return fold_last(held, swap(sent, "col", d), *before)

    buf0, kept, *outs = project(momentum, gradient, old_basis, depth, width, 0)
    low = sum_over_col(*outs)
    buf1, *outs = project(momentum, gradient, kept, depth, width, 1, (outs[1],))
    lefts = gather(sum_over_col(*outs, low), "col")
    bufs = (buf0, buf1)

    other, mine, g_sums = first_product(bufs, lefts[:-1], depth, width)
    g_mine, g_other = gram(lefts[-1], g_sums)
    other = last_product(bufs, other, lefts[-1], depth, width, False, g_mine)
    g_mine = g_mine + swap(g_other, "row", 1)
    other = hand_on(other, g_mine)
    received = swap(other, "row", 1)
    mine = last_product(bufs, mine, lefts[-1], depth, width, True, g_mine, other)
    own, *sent = pair_sum(mine, received, chips, g_mine)
    g_mine = pair_up(exchange(g_mine, "row", chips, 2))
    got = [swap(x, "row", 2 * (d + 1)) for d, x in enumerate(sent)]
    inverse = chol_inverse(g_mine, swap(g_mine, "row", 1))

    share, squares = share_of(inverse, own, got)
    ortho_bf = ortho(inverse, lefts)
    squares = pair_up(exchange(squares, "row", chips, 2))
    share = hand_on(share, squares)
    squares = pair_up(exchange(squares + swap(squares, "row", 1), "col", depth))

    factor = step_rate * math.sqrt(D / RANK)
    near = min(3, chips)
    blocks = [share] + [swap(share, "row", 2 * d) for d in range(1, near)]
    blocks = [share] + [hand_on(x, squares) for x in blocks[1:]]
    for d in range(near, chips):
        share = hand_on(share, blocks[d - 2])
        blocks.append(swap(share, "row", 2 * d))
    blocks[0] = share
    pairs = [x for block in blocks[:near] for x in (block, swap(block, "row", 1))]
    common = (factor, bufs, ortho_bf, inverse, squares, weight)
    outs, token = results(tuple(range(near)), *common, pairs, [])
    for d in range(near, chips):
        block = hand_on(blocks[d], token)
        outs, token = results((d,), *common, (block, swap(block, "row", 1)), outs)
    return tuple(outs)


def plain_per_device(weight, gradient, momentum, old_basis):
    buffer = momentum + gradient.astype(f32)
    buffer_low = buffer.astype(bf16)
    left_factor = lax.psum(dot(buffer_low, old_basis, ((1,), (1,))), "col")
    gram_share = lax.dot_general(
        left_factor,
        left_factor,
        (((0,), (0,)), ((), ())),
        precision=lax.Precision.HIGHEST,
        preferred_element_type=f32,
    )
    chol_factor = jnp.linalg.cholesky(lax.psum(gram_share, "row"))
    orthonormal = lax.linalg.triangular_solve(
        chol_factor, left_factor, left_side=False, lower=True, transpose_a=True
    ).astype(bf16)
    right_share = lax.psum_scatter(
        dot(orthonormal, buffer_low, ((0,), (0,))), "row", scatter_dimension=0, tiled=True
    )
    sum_squares = lax.psum(jnp.sum(right_share * right_share, axis=1), "col")
    scale_share = jnp.sqrt(sum_squares / FF + epsilon)
    basis_share = (right_share / scale_share[:, None]).astype(bf16)
    new_basis = lax.all_gather(basis_share, "row", axis=0, tiled=True)
    col_scale = lax.all_gather(scale_share, "row", axis=0, tiled=True)
    scaled = (orthonormal.astype(f32) * col_scale[None, :]).astype(bf16)
    new_momentum = buffer - (1.0 - momentum_decay) * dot(scaled, new_basis)
    factor = step_rate * math.sqrt(D / RANK)
    new_weight = (weight.astype(f32) - factor * dot(orthonormal, new_basis)).astype(bf16)
    return (new_weight, new_momentum, new_basis)


def power_of_two(k):
    return k > 1 and k & (k - 1) == 0


def solution(mesh):
    rows, depth = mesh.shape["row"], mesh.shape["col"]
    tiled = (
        power_of_two(rows)
        and power_of_two(depth)
        and D % (rows * depth * 128) == 0
        and FF % (rows * depth * 256) == 0
    )
    return jax.shard_map(
        per_device if tiled else plain_per_device,
        mesh=mesh,
        in_specs=(P("row", "col"), P("row", "col"), P("row", "col"), P(None, "col")),
        out_specs=(P("row", "col"), P("row", "col"), P(None, "col")),
        check_vma=False,
    )
```

```python
import functools
import math

import jax
import jax.numpy as jnp
from jax import lax
from jax.experimental import pallas as pl
from jax.experimental.pallas import tpu as pltpu
from jax.sharding import PartitionSpec as P

D = 8192
FF = 24576
RANK = 256

epsilon = 1e-06
momentum_decay = 0.6
step_rate = 0.5

bf16, f32 = jnp.bfloat16, jnp.float32
VMEM = pl.BlockSpec(memory_space=pltpu.VMEM)
ANY = pl.BlockSpec(memory_space=pl.ANY)
MIB = 1 << 20


def shape(dims, kind):
    return jax.ShapeDtypeStruct(dims, kind)


def params(mib):
    return pltpu.CompilerParams(vmem_limit_bytes=mib * MIB)


def dot(a, b, dims=((1,), (0,))):
    return lax.dot_general(a, b, (dims, ((), ())), preferred_element_type=f32)


def split(x, terms):
    parts = []
    for _ in range(terms):
        part = x.astype(bf16)
        parts.append(part)
        x = x - part.astype(f32)
    return parts


def flip(i, d):
    return lax.bitwise_xor(i, jnp.int32(d))


def swap(x, axis, d):
    return lax.ppermute(x, axis, [(i, i ^ d) for i in range(lax.axis_size(axis))])


def project_kernel(part, depth, width, mom, grad, basis, *rest):
    if part == 0:
        (buf, kept), rest = rest[:2], rest[2:]
    else:
        kept, buf, rest = basis, rest[1], rest[2:]
    held, sent, gbuf, total, sems, basis_sem = rest
    m, n = buf.shape
    half = m // depth

    def copies(c):
        cols = pl.ds(pl.multiple_of(c * width, 128), width)
        pairs = []
        for k in range(depth):
            there = pl.ds((2 * k + part) * half, half)
            here = pl.ds(k * half, half)
            pairs.append(pltpu.make_async_copy(mom.at[there, cols], buf.at[here, cols], sems.at[0, k, c]))
            pairs.append(pltpu.make_async_copy(grad.at[there, cols], gbuf.at[here, cols], sems.at[1, k, c]))
        if part == 0:
            pairs.append(pltpu.make_async_copy(basis.at[:, cols], kept.at[:, cols], basis_sem.at[c]))
        return pairs

    def start(c, carry):
        for copy in copies(c):
            copy.start()
        return carry

    def step(c, carry):
        for copy in copies(c):
            copy.wait()
        cols = pl.ds(pl.multiple_of(c * width, 128), width)
        added = buf[:, cols] + gbuf[:, cols].astype(f32)
        buf[:, cols] = added
        total[...] += dot(added.astype(bf16), kept[:, cols], ((1,), (1,)))
        return carry

    total[...] = jnp.zeros_like(total)
    lax.fori_loop(0, n // width, start, 0)
    lax.fori_loop(0, n // width, step, 0)
    me = lax.axis_index("col")
    for out, odd in ((held, 0), (sent, 1)):
        for j in range(depth // 2):
            rows = pl.ds(pl.multiple_of(flip(me, 2 * j + odd) * half, half), half)
            out[:, j * half : (j + 1) * half] = jnp.transpose(total[rows, :]).astype(out.dtype)


def project(momentum, gradient, basis, depth, width, part, after=()):
    m, n = momentum.shape
    m = m // 2
    r = basis.shape[0]
    kept = [] if part else [pltpu.VMEM((r, n), bf16)]
    return pl.pallas_call(
        functools.partial(project_kernel, part, depth, width),
        out_shape=(pltpu.VMEM((m, n), f32), *kept, shape((r, m // 2), f32), shape((r, m // 2), bf16)),
        in_specs=[ANY, ANY] + [VMEM if part else ANY] + [ANY] * len(after),
        out_specs=(VMEM,) * (3 + len(kept)),
        scratch_shapes=[
            pltpu.VMEM((m, n), bf16),
            pltpu.VMEM((m, r), f32),
            pltpu.SemaphoreType.DMA((2, depth, n // width)),
            pltpu.SemaphoreType.DMA((n // width,)),
        ],
        compiler_params=params(14),
        cost_estimate=cost(momentum, gradient),
        name="project",
    )(stay(momentum), stay(gradient), keep(basis) if part else stay(basis), *after)


def fold_kernel(half, held, received, held_out, sent_out):
    added = held[...] + received[...].astype(f32)
    for j in range(held_out.shape[1] // half):
        at = slice(j * half, (j + 1) * half)
        held_out[:, at] = added[:, 2 * j * half : (2 * j + 1) * half]
        sent_out[:, at] = added[:, (2 * j + 1) * half : (2 * j + 2) * half].astype(bf16)


def fold(held, received, half):
    r, size = held.shape
    return pl.pallas_call(
        functools.partial(fold_kernel, half),
        out_shape=(shape((r, size // 2), f32), shape((r, size // 2), bf16)),
        in_specs=[VMEM, VMEM],
        out_specs=(VMEM, VMEM),
        compiler_params=params(8),
        name="fold",
    )(held, received)


def fold_last_kernel(held, received, *rest):
    before, out = rest[:-1], rest[-1]
    half = held.shape[1]
    for k, ref in enumerate(before):
        out[:, k * half : (k + 1) * half] = ref[...]
    out[:, len(before) * half :] = (held[...] + received[...].astype(f32)).astype(bf16)


def fold_last(held, received, *before):
    r, half = held.shape
    return pl.pallas_call(
        fold_last_kernel,
        out_shape=shape((r, half * (1 + len(before))), bf16),
        in_specs=[VMEM] * (2 + len(before)),
        out_specs=VMEM,
        compiler_params=params(8),
        name="fold_last",
    )(held, received, *before)


def cost(*arrays):
    size = sum(math.prod(x.shape) * x.dtype.itemsize for x in arrays)
    return pl.CostEstimate(flops=0, bytes_accessed=size, transcendentals=0)


def keep(x):
    return pltpu.with_memory_space_constraint(x, pltpu.VMEM)


def stay(x):
    return pltpu.with_memory_space_constraint(x, pltpu.HBM)


def buffer_rows(bufs, ds, depth, cols):
    half = bufs[0].shape[0] // depth
    me = lax.axis_index("col")
    rows = [pl.ds(pl.multiple_of(flip(me, d) * half, half), half) for d in ds]
    return jnp.concatenate([buf[at, cols].astype(bf16) for at in rows for buf in bufs], axis=0)


def first_kernel(depth, width, buf0, buf1, *rest):
    lefts, (other, mine, gram, whole) = rest[:-4], rest[-4:]
    core = lax.bitwise_and(lax.axis_index("row"), jnp.int32(1))
    size = other.shape[1]
    block = lefts[0].shape[1]
    for d, ref in enumerate(lefts):
        whole[:, d * block : (d + 1) * block] = ref[...]
    gram[...] = dot(whole[...], whole[...], ((1,), (1,)))
    for out, half in ((other, 1 - core), (mine, core)):

        def step(k, carry, out=out, half=half):
            cols = pl.ds(pl.multiple_of(half * size + k * width, 128), width)
            b = buffer_rows((buf0, buf1), range(len(lefts)), depth, cols)
            out[:, pl.ds(pl.multiple_of(k * width, 128), width)] = dot(whole[...], b)
            return carry

        lax.fori_loop(0, size // width, step, 0)


def first_product(bufs, lefts, depth, width):
    m, n = bufs[0].shape
    r, block = lefts[0].shape
    return pl.pallas_call(
        functools.partial(first_kernel, depth, width),
        out_shape=(shape((r, n // 2), f32), shape((r, n // 2), f32), shape((r, r), f32)),
        in_specs=[VMEM] * (2 + len(lefts)),
        out_specs=[VMEM] * 3,
        scratch_shapes=[pltpu.VMEM((r, block * len(lefts)), bf16)],
        compiler_params=params(10),
        cost_estimate=cost(*bufs, shape((r, n), f32)),
        name="first_product",
    )(*map(keep, bufs), *lefts)


def gram_kernel(left, sums, g_mine, g_other, total):
    core = lax.bitwise_and(lax.axis_index("row"), jnp.int32(1))
    total[...] = sums[...] + dot(left[...], left[...], ((1,), (1,)))
    h = g_mine.shape[0]
    g_mine[...] = total[pl.ds(pl.multiple_of(core * h, h), h), :]
    g_other[...] = total[pl.ds(pl.multiple_of((1 - core) * h, h), h), :]


def gram(left, sums):
    r = left.shape[0]
    return pl.pallas_call(
        gram_kernel,
        out_shape=[shape((r // 2, r), f32)] * 2,
        in_specs=[VMEM, VMEM],
        out_specs=[VMEM] * 2,
        scratch_shapes=[pltpu.VMEM((r, r), f32)],
        compiler_params=params(8),
        name="gram",
    )(left, sums)


def last_kernel(depth, width, mine, buf0, buf1, sums, left, *rest):
    out = rest[-1]
    core = lax.bitwise_and(lax.axis_index("row"), jnp.int32(1))
    half = core if mine else 1 - core
    size = out.shape[1]

    def step(k, carry):
        cols = pl.ds(pl.multiple_of(half * size + k * width, 128), width)
        at = pl.ds(pl.multiple_of(k * width, 128), width)
        b = buffer_rows((buf0, buf1), [depth - 1], depth, cols)
        out[:, at] = (sums[:, at] + dot(left[...], b)).astype(out.dtype)
        return carry

    lax.fori_loop(0, size // width, step, 0)


def last_product(bufs, sums, left, depth, width, mine, *after):
    return pl.pallas_call(
        functools.partial(last_kernel, depth, width, mine),
        out_shape=shape(sums.shape, f32 if mine else bf16),
        in_specs=[VMEM] * 4 + [ANY] * len(after),
        out_specs=VMEM,
        compiler_params=params(8),
        cost_estimate=cost(*bufs[:1], sums),
        name="mine_product" if mine else "other_product",
    )(*map(keep, bufs), sums, left, *after)


def pair_sum_kernel(chips, mine, received, _, *outs):
    me = lax.div(lax.axis_index("row"), jnp.int32(2))
    width = outs[0].shape[1]
    for d in range(chips):
        cols = pl.ds(pl.multiple_of(flip(me, d) * width, 128), width)
        outs[d][...] = (mine[:, cols] + received[:, cols].astype(f32)).astype(outs[d].dtype)


def pair_sum(mine, received, chips, after):
    r, n = mine.shape
    kinds = [f32] + [bf16] * (chips - 1)
    return pl.pallas_call(
        functools.partial(pair_sum_kernel, chips),
        out_shape=[shape((r, n // chips), k) for k in kinds],
        in_specs=[VMEM, VMEM, ANY],
        out_specs=[VMEM] * chips,
        compiler_params=params(8),
        name="pair_sum",
    )(mine, received, after)


def eliminate(tiles, at, nb, group):
    sub = lax.broadcasted_iota(jnp.int32, (nb, 128), 0)
    scale = jnp.zeros((nb, 128), f32)
    for g in range(0, nb, group):
        cols = [
            jnp.broadcast_to(tiles[0][:, at + g + j : at + g + j + 1], (nb, 128)) for j in range(group)
        ]
        for j in range(group):
            t = g + j
            pivot = cols[j][t : t + 1, :]
            factor = jnp.where(sub > t, cols[j], 0.0) * (1.0 / pivot)
            scale = jnp.where(sub == t, lax.rsqrt(pivot), scale)
            for l in range(j + 1, group):
                cols[l] = cols[l] - factor * cols[l][t : t + 1, :]
            tiles = [x - factor * x[t : t + 1, :] for x in tiles]
    return [x * scale for x in tiles]


def chol_inverse_kernel(mine, other, out, work):
    n = out.shape[0]
    h = n // 2
    core = lax.bitwise_and(lax.axis_index("row"), jnp.int32(1))
    work[pl.ds(pl.multiple_of(core * h, h), h), :n] = mine[...]
    work[pl.ds(pl.multiple_of((1 - core) * h, h), h), :n] = other[...]
    r_id = lax.broadcasted_iota(jnp.int32, (n, n), 0)
    c_id = lax.broadcasted_iota(jnp.int32, (n, n), 1)
    work[:, n:] = jnp.where(r_id == c_id, 1.0, 0.0).astype(f32)
    nb = 32
    for p in range(n // nb):
        lo = p * nb
        left = (lo // 128) * 128
        right = n + ((lo + nb + 127) // 128) * 128
        tiles = [work[lo : lo + nb, c : c + 128] for c in range(left, right, 128)]
        s = jnp.concatenate(eliminate(tiles, lo - left, nb, 8), axis=1)
        work[lo : lo + nb, left:right] = s
        if lo + nb < n:
            lead = s[:, lo + nb - left : n - left]
            work[lo + nb :, left:right] -= lax.dot_general(
                lead, s, (((0,), (0,)), ((), ())), precision=lax.Precision.HIGHEST, preferred_element_type=f32
            )
    out[...] = jnp.where(r_id >= c_id, work[:, n:], 0.0)


def chol_inverse(mine, other):
    n = mine.shape[1]
    return pl.pallas_call(
        chol_inverse_kernel,
        out_shape=shape((n, n), f32),
        in_specs=[VMEM, VMEM],
        out_specs=VMEM,
        scratch_shapes=[pltpu.VMEM((n, 2 * n), f32)],
        compiler_params=params(8),
        cost_estimate=cost(*[mine] * 256),
        name="chol_inverse",
    )(mine, other)


def ortho_kernel(inverse, *refs):
    lefts, out = refs[:-1], refs[-1]
    block = lefts[0].shape[1]
    me = lax.axis_index("col")
    parts = split(inverse[...], 3)
    for d, ref in enumerate(lefts):
        rows = pl.ds(pl.multiple_of(flip(me, d) * block, block), block)
        out[rows, :] = sum(dot(ref[...], x, ((0,), (1,))) for x in reversed(parts)).astype(bf16)


def ortho(inverse, lefts):
    r, block = lefts[0].shape
    return pl.pallas_call(
        ortho_kernel,
        out_shape=shape((block * len(lefts), r), bf16),
        in_specs=[VMEM] * (1 + len(lefts)),
        out_specs=VMEM,
        compiler_params=params(8),
        cost_estimate=cost(*[shape((block * len(lefts), r), bf16)] * 8),
        name="ortho",
    )(inverse, *lefts)


def hand_on(x, *earlier):
    return pl.pallas_call(
        lambda *refs: None,
        out_shape=shape(x.shape, x.dtype),
        in_specs=[ANY] * (1 + len(earlier)),
        out_specs=ANY,
        input_output_aliases={0: 0},
        compiler_params=params(1),
        name="hand_on",
    )(x, *earlier)


def apply_inverse(parts, block):
    return sum(dot(x, block) for x in reversed(parts))


def share_kernel(own, *refs):
    received, (_, out) = refs[:-2], refs[-2:]
    out[...] = (own[...] + sum(ref[...].astype(f32) for ref in received)).astype(bf16)


def share_of(own, received, after):
    return pl.pallas_call(
        share_kernel,
        out_shape=shape(own.shape, bf16),
        in_specs=[VMEM] * (1 + len(received)) + [ANY],
        out_specs=VMEM,
        compiler_params=params(8),
        name="share",
    )(own, *received, after)


def result_kernel(pairs, factor, momentum_too, weight_too, terms, buf0, buf1, ortho_ref, inverse, weight, *refs):
    squares, refs = refs[:terms], refs[terms:]
    blocks, rest = refs[: 2 * len(pairs)], refs[2 * len(pairs) :]
    *outs, sums, mbuf, wbuf, vbuf, nbuf, lbuf, in_sems, out_sems, basis_sems = rest
    new_momentum = outs[-1] if momentum_too else None
    new_weight, basis = outs[-2 - momentum_too : len(outs) - momentum_too] if weight_too else (None, None)
    r, width = blocks[0].shape
    tile = 256
    tiles = width // tile
    count = len(blocks)
    half = width * (lax.axis_size("row") // 2)
    row = lax.axis_index("row")
    core = lax.bitwise_and(row, jnp.int32(1))
    chip = lax.div(row, jnp.int32(2))
    starts = []
    for d in pairs:
        starts += [core * half + flip(chip, d) * width, (1 - core) * half + flip(chip, d) * width]

    def load(b):
        cols = pl.ds(pl.multiple_of(starts[b], 128), width)
        return pltpu.make_async_copy(weight.at[:, cols], wbuf.at[b % 2], in_sems.at[b % 2])

    def store_basis(b):
        cols = pl.ds(pl.multiple_of(starts[b], 128), width)
        return pltpu.make_async_copy(nbuf.at[b % 2], basis.at[:, cols], basis_sems.at[b % 2])

    def place(b, t):
        return pl.ds(t * tile, tile), pl.ds(pl.multiple_of(starts[b] + t * tile, 128), tile)

    def store_momentum(b, t):
        at, there = place(b, t)
        return pltpu.make_async_copy(mbuf.at[b % 2, :, at], new_momentum.at[:, there], out_sems.at[0, b % 2, t])

    def store_weight(b, t):
        at, there = place(b, t)
        return pltpu.make_async_copy(vbuf.at[b % 2, :, at], new_weight.at[:, there], out_sems.at[1, b % 2, t])

    def finish(b):
        if weight_too:
            store_basis(b).wait()
        for t in range(tiles):
            if momentum_too:
                store_momentum(b, t).wait()
            if weight_too:
                store_weight(b, t).wait()

    if weight_too:
        for b in range(2):
            load(b).start()
        total = jnp.sum(pair_up([ref[...] for ref in squares]), axis=0, keepdims=True)
        scale = lax.rsqrt(total / FF + epsilon)
        scale = jnp.transpose(jnp.broadcast_to(scale, (128, r)))[:, :1]
    sums[...] = jnp.zeros_like(sums)
    block_id = lax.broadcasted_iota(jnp.int32, sums.shape, 0)
    parts = split(inverse[...], 2)
    depth = lax.axis_size("col")
    size = buf0.shape[0] // depth
    for b in range(count):
        k = b % 2
        if b >= 2:
            finish(b - 2)
        right = apply_inverse(parts, blocks[b][...])
        if momentum_too:
            lbuf[k] = ((1.0 - momentum_decay) * right).astype(bf16)
            total = jnp.sum(right * right, axis=1, keepdims=True)
            total = jnp.transpose(jnp.broadcast_to(total, (r, 128)))[: sums.shape[0], :]
            sums[...] += jnp.where(block_id == lax.div(starts[b], jnp.int32(width)), total, 0.0)
        if weight_too:
            nbuf[k] = (right * scale).astype(bf16)
            store_basis(b).start()
            load(b).wait()
        for t in range(tiles):
            at, there = place(b, t)
            if momentum_too:
                correction = dot(ortho_ref[...], lbuf[k, :, at])
                for j in range(2 * depth):
                    rows = slice(j * size, (j + 1) * size)
                    here = slice(j // 2 * size, (j // 2 + 1) * size)
                    mbuf[k, rows, at] = (buf0, buf1)[j % 2][here, there] - correction[rows]
                store_momentum(b, t).start()
            if weight_too:
                change = dot(ortho_ref[...], nbuf[k, :, at])
                vbuf[k, :, at] = (wbuf[k, :, at].astype(f32) - factor * change).astype(bf16)
                store_weight(b, t).start()
        if weight_too and b + 2 < count:
            load(b + 2).start()
    for b in range(count - 2, count):
        finish(b)


def results(pairs, kinds, factor, bufs, ortho_bf, inverse, weight, squares, blocks, outs=(), after=()):
    momentum_too, weight_too = kinds
    m, n = weight.shape
    r, width = blocks[0].shape
    ins = [*map(keep, bufs), ortho_bf, inverse, stay(weight), *squares, *blocks, *after, *map(stay, outs)]
    at = len(ins) - len(outs)
    out_shape = []
    if weight_too:
        out_shape += [shape((m, n), bf16), shape((r, n), bf16)]
    if momentum_too:
        out_shape += [shape((m, n), f32)]
    m_slots, w_slots = (m if momentum_too else 8), (m if weight_too else 16)
    return pl.pallas_call(
        functools.partial(result_kernel, pairs, factor, momentum_too, weight_too, len(squares)),
        out_shape=[*out_shape, shape((max(8, n // width), r), f32)],
        in_specs=[VMEM] * 4 + [ANY] + [VMEM] * (len(squares) + len(blocks)) + [ANY] * (len(after) + len(outs)),
        out_specs=[ANY] * len(out_shape) + [VMEM],
        input_output_aliases={at + k: k for k in range(len(outs))},
        scratch_shapes=[
            pltpu.VMEM((2, m_slots, width), f32),
            pltpu.VMEM((2, w_slots, width), bf16),
            pltpu.VMEM((2, w_slots, width), bf16),
            pltpu.VMEM((2, r, width), bf16),
            pltpu.VMEM((2, r, width), bf16),
            pltpu.SemaphoreType.DMA((2,)),
            pltpu.SemaphoreType.DMA((2, 2, width // 256)),
            pltpu.SemaphoreType.DMA((2,)),
        ],
        compiler_params=params(15),
        cost_estimate=cost(*[shape((m, width), f32)] * len(blocks) * (momentum_too + weight_too)),
        name="results",
    )(*ins)


def sum_over(x, axis, least=1):
    d = least
    while d < lax.axis_size(axis):
        x = x + swap(x, axis, d)
        d *= 2
    return x


def exchange(x, axis, count, unit=1):
    return [x] + [swap(x, axis, unit * d) for d in range(1, count)]


def pair_up(terms):
    while len(terms) > 1:
        terms = [terms[2 * i] + terms[2 * i + 1] for i in range(len(terms) // 2)]
    return terms[0]


def gather(x, axis):
    blocks = [x]
    size = lax.axis_size(axis)
    for d in range(1, size):
        low = d & -d
        blocks.append(swap(blocks[d - low] if d != low else x, axis, low))
    return blocks


def per_device(weight, gradient, momentum, old_basis):
    depth, rows = lax.axis_size("col"), lax.axis_size("row")
    chips = rows // 2
    m, n = momentum.shape
    width = n // rows

    def sum_over_col(held, sent, *before):
        half = m // 2 // depth
        d = 1
        while held.shape[1] > half:
            held, sent = fold(held, swap(sent, "col", d), half)
            d *= 2
        return fold_last(held, swap(sent, "col", d), *before)

    buf0, kept, *outs = project(momentum, gradient, old_basis, depth, width, 0)
    low = sum_over_col(*outs)
    buf1, *outs = project(momentum, gradient, kept, depth, width, 1, (outs[1],))
    lefts = gather(sum_over_col(*outs, low), "col")
    bufs = (buf0, buf1)

    other, mine, g_sums = first_product(bufs, lefts[:-1], depth, width)
    g_mine, g_other = gram(lefts[-1], g_sums)
    other = last_product(bufs, other, lefts[-1], depth, width, False, g_mine)
    g_mine = g_mine + swap(g_other, "row", 1)
    other = hand_on(other, g_mine)
    received = swap(other, "row", 1)
    mine = last_product(bufs, mine, lefts[-1], depth, width, True, g_mine, other)
    own, *sent = pair_sum(mine, received, chips, g_mine)
    g_mine = pair_up(exchange(g_mine, "row", chips, 2))
    got = [swap(x, "row", 2 * (d + 1)) for d, x in enumerate(sent)]
    inverse = chol_inverse(g_mine, swap(g_mine, "row", 1))

    share = share_of(own, got, inverse)
    ortho_bf = ortho(inverse, lefts)

    factor = step_rate * math.sqrt(D / RANK)
    common = (factor, bufs, ortho_bf, inverse, weight)
    blocks = {0: share}
    for d in range(1, chips):
        if d & (d - 1) == 0:
            blocks[d] = swap(share, "row", 2 * d)
    near = sorted(blocks)
    pairs = {0: (share, swap(share, "row", 1))}
    momentum, sums = results((0,), (True, False), *common, (), pairs[0])
    for d in near[1:]:
        blocks[d] = hand_on(blocks[d], sums)
        pairs[d] = (blocks[d], swap(blocks[d], "row", 1))
    far = [d for d in range(chips) if d not in blocks]
    h = share.shape[0] // 2
    halves = {}
    for d in far:
        least, most = d & -d, 1 << (d.bit_length() - 1)
        halves[d] = (
            swap(blocks[d ^ most][:h], "row", 2 * most),
            swap(blocks[d ^ least][h:], "row", 2 * least),
        )
        blocks[d] = jnp.concatenate(halves[d], axis=0)
    squares = [sums]
    rest = [x for d in near[1:] for x in pairs[d]]
    momentum, sums = results(tuple(near[1:]), (True, False), *common, (), rest, [momentum])
    squares.append(sums)
    for d in far:
        top, bottom = halves[d]
        block = jnp.concatenate([hand_on(top, sums), bottom], axis=0)
        pairs[d] = (block, swap(block, "row", 1))
        momentum, sums = results((d,), (True, False), *common, (), pairs[d], [momentum])
        squares.append(sums)
    scales = exchange(sum(squares), "col", depth)
    order = near + far
    rest = [x for d in order for x in pairs[d]]
    new_weight, new_basis, _ = results(tuple(order), (False, True), *common, scales, rest)
    return (new_weight, momentum, new_basis)


def plain_per_device(weight, gradient, momentum, old_basis):
    buffer = momentum + gradient.astype(f32)
    buffer_low = buffer.astype(bf16)
    left_factor = lax.psum(dot(buffer_low, old_basis, ((1,), (1,))), "col")
    gram_share = lax.dot_general(
        left_factor,
        left_factor,
        (((0,), (0,)), ((), ())),
        precision=lax.Precision.HIGHEST,
        preferred_element_type=f32,
    )
    chol_factor = jnp.linalg.cholesky(lax.psum(gram_share, "row"))
    orthonormal = lax.linalg.triangular_solve(
        chol_factor, left_factor, left_side=False, lower=True, transpose_a=True
    ).astype(bf16)
    right_share = lax.psum_scatter(
        dot(orthonormal, buffer_low, ((0,), (0,))), "row", scatter_dimension=0, tiled=True
    )
    sum_squares = lax.psum(jnp.sum(right_share * right_share, axis=1), "col")
    scale_share = jnp.sqrt(sum_squares / FF + epsilon)
    basis_share = (right_share / scale_share[:, None]).astype(bf16)
    new_basis = lax.all_gather(basis_share, "row", axis=0, tiled=True)
    col_scale = lax.all_gather(scale_share, "row", axis=0, tiled=True)
    scaled = (orthonormal.astype(f32) * col_scale[None, :]).astype(bf16)
    new_momentum = buffer - (1.0 - momentum_decay) * dot(scaled, new_basis)
    factor = step_rate * math.sqrt(D / RANK)
    new_weight = (weight.astype(f32) - factor * dot(orthonormal, new_basis)).astype(bf16)
    return (new_weight, new_momentum, new_basis)


def power_of_two(k):
    return k > 1 and k & (k - 1) == 0


def solution(mesh):
    rows, depth = mesh.shape["row"], mesh.shape["col"]
    tiled = (
        power_of_two(rows // 2)
        and power_of_two(depth)
        and D % (rows * depth * 128) == 0
        and FF % (rows * depth * 256) == 0
    )
    return jax.shard_map(
        per_device if tiled else plain_per_device,
        mesh=mesh,
        in_specs=(P("row", "col"), P("row", "col"), P("row", "col"), P(None, "col")),
        out_specs=(P("row", "col"), P("row", "col"), P(None, "col")),
        check_vma=False,
    )
```

```python
import functools
import math

import jax
import jax.numpy as jnp
from jax import lax
from jax.experimental import pallas as pl
from jax.experimental.pallas import tpu as pltpu
from jax.sharding import PartitionSpec as P

D = 8192
FF = 24576
RANK = 256

epsilon = 1e-06
momentum_decay = 0.6
step_rate = 0.5

bf16, f32 = jnp.bfloat16, jnp.float32
VMEM = pl.BlockSpec(memory_space=pltpu.VMEM)
ANY = pl.BlockSpec(memory_space=pl.ANY)
MIB = 1 << 20


def shape(dims, kind):
    return jax.ShapeDtypeStruct(dims, kind)


def params(mib):
    return pltpu.CompilerParams(vmem_limit_bytes=mib * MIB)


def dot(a, b, dims=((1,), (0,))):
    return lax.dot_general(a, b, (dims, ((), ())), preferred_element_type=f32)


def split(x, terms):
    parts = []
    for _ in range(terms):
        part = x.astype(bf16)
        parts.append(part)
        x = x - part.astype(f32)
    return parts


def flip(i, d):
    return lax.bitwise_xor(i, jnp.int32(d))


def swap(x, axis, d):
    return lax.ppermute(x, axis, [(i, i ^ d) for i in range(lax.axis_size(axis))])


def project_kernel(part, depth, width, mom, grad, basis, *rest):
    if part == 0:
        (buf, kept), rest = rest[:2], rest[2:]
    else:
        kept, buf, rest = basis, rest[1], rest[2:]
    held, sent, gbuf, total, sems, basis_sem = rest
    m, n = buf.shape
    half = m // depth

    def copies(c):
        cols = pl.ds(pl.multiple_of(c * width, 128), width)
        pairs = []
        for k in range(depth):
            there = pl.ds((2 * k + part) * half, half)
            here = pl.ds(k * half, half)
            pairs.append(pltpu.make_async_copy(mom.at[there, cols], buf.at[here, cols], sems.at[0, k, c]))
            pairs.append(pltpu.make_async_copy(grad.at[there, cols], gbuf.at[here, cols], sems.at[1, k, c]))
        if part == 0:
            pairs.append(pltpu.make_async_copy(basis.at[:, cols], kept.at[:, cols], basis_sem.at[c]))
        return pairs

    def start(c, carry):
        for copy in copies(c):
            copy.start()
        return carry

    def step(c, carry):
        for copy in copies(c):
            copy.wait()
        cols = pl.ds(pl.multiple_of(c * width, 128), width)
        added = buf[:, cols] + gbuf[:, cols].astype(f32)
        buf[:, cols] = added
        total[...] += dot(added.astype(bf16), kept[:, cols], ((1,), (1,)))
        return carry

    total[...] = jnp.zeros_like(total)
    lax.fori_loop(0, n // width, start, 0)
    lax.fori_loop(0, n // width, step, 0)
    me = lax.axis_index("col")
    for out, odd in ((held, 0), (sent, 1)):
        for j in range(depth // 2):
            rows = pl.ds(pl.multiple_of(flip(me, 2 * j + odd) * half, half), half)
            out[:, j * half : (j + 1) * half] = jnp.transpose(total[rows, :]).astype(out.dtype)


def project(momentum, gradient, basis, depth, width, part, after=()):
    m, n = momentum.shape
    m = m // 2
    r = basis.shape[0]
    kept = [] if part else [pltpu.VMEM((r, n), bf16)]
    return pl.pallas_call(
        functools.partial(project_kernel, part, depth, width),
        out_shape=(pltpu.VMEM((m, n), f32), *kept, shape((r, m // 2), f32), shape((r, m // 2), bf16)),
        in_specs=[ANY, ANY] + [VMEM if part else ANY] + [ANY] * len(after),
        out_specs=(VMEM,) * (3 + len(kept)),
        scratch_shapes=[
            pltpu.VMEM((m, n), bf16),
            pltpu.VMEM((m, r), f32),
            pltpu.SemaphoreType.DMA((2, depth, n // width)),
            pltpu.SemaphoreType.DMA((n // width,)),
        ],
        compiler_params=params(14),
        cost_estimate=cost(momentum, gradient),
        name="project",
    )(stay(momentum), stay(gradient), keep(basis) if part else stay(basis), *after)


def fold_kernel(half, held, received, held_out, sent_out):
    added = held[...] + received[...].astype(f32)
    for j in range(held_out.shape[1] // half):
        at = slice(j * half, (j + 1) * half)
        held_out[:, at] = added[:, 2 * j * half : (2 * j + 1) * half]
        sent_out[:, at] = added[:, (2 * j + 1) * half : (2 * j + 2) * half].astype(bf16)


def fold(held, received, half):
    r, size = held.shape
    return pl.pallas_call(
        functools.partial(fold_kernel, half),
        out_shape=(shape((r, size // 2), f32), shape((r, size // 2), bf16)),
        in_specs=[VMEM, VMEM],
        out_specs=(VMEM, VMEM),
        compiler_params=params(8),
        name="fold",
    )(held, received)


def fold_last_kernel(held, received, *rest):
    before, out = rest[:-1], rest[-1]
    half = held.shape[1]
    for k, ref in enumerate(before):
        out[:, k * half : (k + 1) * half] = ref[...]
    out[:, len(before) * half :] = (held[...] + received[...].astype(f32)).astype(bf16)


def fold_last(held, received, *before):
    r, half = held.shape
    return pl.pallas_call(
        fold_last_kernel,
        out_shape=shape((r, half * (1 + len(before))), bf16),
        in_specs=[VMEM] * (2 + len(before)),
        out_specs=VMEM,
        compiler_params=params(8),
        name="fold_last",
    )(held, received, *before)


def cost(*arrays):
    size = sum(math.prod(x.shape) * x.dtype.itemsize for x in arrays)
    return pl.CostEstimate(flops=0, bytes_accessed=size, transcendentals=0)


def keep(x):
    return pltpu.with_memory_space_constraint(x, pltpu.VMEM)


def stay(x):
    return pltpu.with_memory_space_constraint(x, pltpu.HBM)


def buffer_rows(bufs, ds, depth, cols):
    half = bufs[0].shape[0] // depth
    me = lax.axis_index("col")
    rows = [pl.ds(pl.multiple_of(flip(me, d) * half, half), half) for d in ds]
    return jnp.concatenate([buf[at, cols].astype(bf16) for at in rows for buf in bufs], axis=0)


def first_kernel(depth, width, buf0, buf1, *rest):
    lefts, (other, mine, gram, whole) = rest[:-4], rest[-4:]
    core = lax.bitwise_and(lax.axis_index("row"), jnp.int32(1))
    size = other.shape[1]
    block = lefts[0].shape[1]
    for d, ref in enumerate(lefts):
        whole[:, d * block : (d + 1) * block] = ref[...]
    gram[...] = dot(whole[...], whole[...], ((1,), (1,)))
    for out, half in ((other, 1 - core), (mine, core)):

        def step(k, carry, out=out, half=half):
            cols = pl.ds(pl.multiple_of(half * size + k * width, 128), width)
            b = buffer_rows((buf0, buf1), range(len(lefts)), depth, cols)
            out[:, pl.ds(pl.multiple_of(k * width, 128), width)] = dot(whole[...], b)
            return carry

        lax.fori_loop(0, size // width, step, 0)


def first_product(bufs, lefts, depth, width):
    m, n = bufs[0].shape
    r, block = lefts[0].shape
    return pl.pallas_call(
        functools.partial(first_kernel, depth, width),
        out_shape=(shape((r, n // 2), f32), shape((r, n // 2), f32), shape((r, r), f32)),
        in_specs=[VMEM] * (2 + len(lefts)),
        out_specs=[VMEM] * 3,
        scratch_shapes=[pltpu.VMEM((r, block * len(lefts)), bf16)],
        compiler_params=params(10),
        cost_estimate=cost(*bufs, shape((r, n), f32)),
        name="first_product",
    )(*map(keep, bufs), *lefts)


def gram_kernel(left, sums, g_mine, g_other, total):
    core = lax.bitwise_and(lax.axis_index("row"), jnp.int32(1))
    total[...] = sums[...] + dot(left[...], left[...], ((1,), (1,)))
    h = g_mine.shape[0]
    g_mine[...] = total[pl.ds(pl.multiple_of(core * h, h), h), :]
    g_other[...] = total[pl.ds(pl.multiple_of((1 - core) * h, h), h), :]


def gram(left, sums):
    r = left.shape[0]
    return pl.pallas_call(
        gram_kernel,
        out_shape=[shape((r // 2, r), f32)] * 2,
        in_specs=[VMEM, VMEM],
        out_specs=[VMEM] * 2,
        scratch_shapes=[pltpu.VMEM((r, r), f32)],
        compiler_params=params(8),
        name="gram",
    )(left, sums)


def last_kernel(depth, width, mine, buf0, buf1, sums, left, *rest):
    out = rest[-1]
    core = lax.bitwise_and(lax.axis_index("row"), jnp.int32(1))
    half = core if mine else 1 - core
    size = out.shape[1]

    def step(k, carry):
        cols = pl.ds(pl.multiple_of(half * size + k * width, 128), width)
        at = pl.ds(pl.multiple_of(k * width, 128), width)
        b = buffer_rows((buf0, buf1), [depth - 1], depth, cols)
        out[:, at] = (sums[:, at] + dot(left[...], b)).astype(out.dtype)
        return carry

    lax.fori_loop(0, size // width, step, 0)


def last_product(bufs, sums, left, depth, width, mine, *after):
    return pl.pallas_call(
        functools.partial(last_kernel, depth, width, mine),
        out_shape=shape(sums.shape, f32 if mine else bf16),
        in_specs=[VMEM] * 4 + [ANY] * len(after),
        out_specs=VMEM,
        compiler_params=params(8),
        cost_estimate=cost(*bufs[:1], sums),
        name="mine_product" if mine else "other_product",
    )(*map(keep, bufs), sums, left, *after)


def pair_sum_kernel(chips, mine, received, _, *outs):
    me = lax.div(lax.axis_index("row"), jnp.int32(2))
    width = outs[0].shape[1]
    for d in range(chips):
        cols = pl.ds(pl.multiple_of(flip(me, d) * width, 128), width)
        outs[d][...] = (mine[:, cols] + received[:, cols].astype(f32)).astype(outs[d].dtype)


def pair_sum(mine, received, chips, after):
    r, n = mine.shape
    kinds = [f32] + [bf16] * (chips - 1)
    return pl.pallas_call(
        functools.partial(pair_sum_kernel, chips),
        out_shape=[shape((r, n // chips), k) for k in kinds],
        in_specs=[VMEM, VMEM, ANY],
        out_specs=[VMEM] * chips,
        compiler_params=params(8),
        name="pair_sum",
    )(mine, received, after)


def eliminate(tiles, at, nb, group):
    sub = lax.broadcasted_iota(jnp.int32, (nb, 128), 0)
    scale = jnp.zeros((nb, 128), f32)
    for g in range(0, nb, group):
        cols = [
            jnp.broadcast_to(tiles[0][:, at + g + j : at + g + j + 1], (nb, 128)) for j in range(group)
        ]
        for j in range(group):
            t = g + j
            pivot = cols[j][t : t + 1, :]
            factor = jnp.where(sub > t, cols[j], 0.0) * (1.0 / pivot)
            scale = jnp.where(sub == t, lax.rsqrt(pivot), scale)
            for l in range(j + 1, group):
                cols[l] = cols[l] - factor * cols[l][t : t + 1, :]
            tiles = [x - factor * x[t : t + 1, :] for x in tiles]
    return [x * scale for x in tiles]


def chol_inverse_kernel(mine, other, out, work):
    n = out.shape[0]
    h = n // 2
    core = lax.bitwise_and(lax.axis_index("row"), jnp.int32(1))
    work[pl.ds(pl.multiple_of(core * h, h), h), :n] = mine[...]
    work[pl.ds(pl.multiple_of((1 - core) * h, h), h), :n] = other[...]
    r_id = lax.broadcasted_iota(jnp.int32, (n, n), 0)
    c_id = lax.broadcasted_iota(jnp.int32, (n, n), 1)
    work[:, n:] = jnp.where(r_id == c_id, 1.0, 0.0).astype(f32)
    nb = 32
    for p in range(n // nb):
        lo = p * nb
        left = (lo // 128) * 128
        right = n + ((lo + nb + 127) // 128) * 128
        tiles = [work[lo : lo + nb, c : c + 128] for c in range(left, right, 128)]
        s = jnp.concatenate(eliminate(tiles, lo - left, nb, 8), axis=1)
        work[lo : lo + nb, left:right] = s
        if lo + nb < n:
            lead = s[:, lo + nb - left : n - left]
            work[lo + nb :, left:right] -= lax.dot_general(
                lead, s, (((0,), (0,)), ((), ())), precision=lax.Precision.HIGHEST, preferred_element_type=f32
            )
    out[...] = jnp.where(r_id >= c_id, work[:, n:], 0.0)


def chol_inverse(mine, other):
    n = mine.shape[1]
    return pl.pallas_call(
        chol_inverse_kernel,
        out_shape=shape((n, n), f32),
        in_specs=[VMEM, VMEM],
        out_specs=VMEM,
        scratch_shapes=[pltpu.VMEM((n, 2 * n), f32)],
        compiler_params=params(8),
        cost_estimate=cost(*[mine] * 256),
        name="chol_inverse",
    )(mine, other)


def ortho_kernel(inverse, *refs):
    lefts, out = refs[:-1], refs[-1]
    block = lefts[0].shape[1]
    me = lax.axis_index("col")
    parts = split(inverse[...], 3)
    for d, ref in enumerate(lefts):
        rows = pl.ds(pl.multiple_of(flip(me, d) * block, block), block)
        out[rows, :] = sum(dot(ref[...], x, ((0,), (1,))) for x in reversed(parts)).astype(bf16)


def ortho(inverse, lefts):
    r, block = lefts[0].shape
    return pl.pallas_call(
        ortho_kernel,
        out_shape=shape((block * len(lefts), r), bf16),
        in_specs=[VMEM] * (1 + len(lefts)),
        out_specs=VMEM,
        compiler_params=params(8),
        cost_estimate=cost(*[shape((block * len(lefts), r), bf16)] * 8),
        name="ortho",
    )(inverse, *lefts)


def hand_on(x, *earlier):
    return pl.pallas_call(
        lambda *refs: None,
        out_shape=shape(x.shape, x.dtype),
        in_specs=[ANY] * (1 + len(earlier)),
        out_specs=ANY,
        input_output_aliases={0: 0},
        compiler_params=params(1),
        name="hand_on",
    )(x, *earlier)


def share_kernel(inverse, own, *refs):
    received, out = refs[:-1], refs[-1]
    total = own[...] + sum(ref[...].astype(f32) for ref in received)
    x_high, x_low = split(inverse[...], 2)
    high, low = split(total, 2)
    out[...] = (dot(x_high, low) + dot(x_low, high) + dot(x_high, high)).astype(bf16)


def share_of(inverse, own, received):
    return pl.pallas_call(
        share_kernel,
        out_shape=shape(own.shape, bf16),
        in_specs=[VMEM] * (2 + len(received)),
        out_specs=VMEM,
        compiler_params=params(8),
        name="share",
    )(inverse, own, *received)


def square_rows(blocks, ids, out_shape):
    rows, r = out_shape
    block_id = lax.broadcasted_iota(jnp.int32, out_shape, 0)
    sums = jnp.zeros(out_shape, f32)
    for block, i in zip(blocks, ids):
        value = block[...].astype(f32)
        total = jnp.sum(value * value, axis=1, keepdims=True)
        total = jnp.transpose(jnp.broadcast_to(total, (r, 128)))[:rows, :]
        sums = sums + jnp.where(block_id == i, total, 0.0)
    return sums


def block_ids(pairs):
    row = lax.axis_index("row")
    core = lax.bitwise_and(row, jnp.int32(1))
    chip = lax.div(row, jnp.int32(2))
    chips = lax.axis_size("row") // 2
    return [half * chips + flip(chip, d) for d in pairs for half in (core, 1 - core)]


def squares_kernel(pairs, before, *refs):
    blocks, earlier, out = refs[: 2 * len(pairs)], refs[2 * len(pairs) : -1], refs[-1]
    out[...] = square_rows(blocks, block_ids(pairs), out.shape) + sum(ref[...] for ref in earlier)


def squares_of(pairs, blocks, earlier):
    return pl.pallas_call(
        functools.partial(squares_kernel, pairs, len(earlier)),
        out_shape=shape(earlier[0].shape, f32),
        in_specs=[VMEM] * (len(blocks) + len(earlier)),
        out_specs=VMEM,
        compiler_params=params(8),
        name="squares",
    )(*blocks, *earlier)


def result_kernel(pairs, factor, momentum_too, weight_too, terms, buf0, buf1, ortho_ref, weight, *refs):
    squares, refs = refs[:terms], refs[terms:]
    blocks, rest = refs[: 2 * len(pairs)], refs[2 * len(pairs) :]
    *outs, sums, mbuf, wbuf, vbuf, nbuf, in_sems, out_sems = rest
    new_momentum = outs[-1] if momentum_too else None
    new_weight, basis = outs[-2 - momentum_too : len(outs) - momentum_too] if weight_too else (None, None)
    r, width = blocks[0].shape
    count = len(blocks)
    ids = block_ids(pairs)
    cols = [pl.ds(pl.multiple_of(i * width, 128), width) for i in ids]

    def load(b):
        return pltpu.make_async_copy(weight.at[:, cols[b]], wbuf.at[b % 2], in_sems.at[b % 2])

    def stores(b):
        copies = []
        if momentum_too:
            copies.append((mbuf, new_momentum))
        if weight_too:
            copies += [(vbuf, new_weight), (nbuf, basis)]
        return [
            pltpu.make_async_copy(src.at[b % 2], dst.at[:, cols[b]], out_sems.at[k, b % 2])
            for k, (src, dst) in enumerate(copies)
        ]

    if weight_too:
        for b in range(2):
            load(b).start()
        total = jnp.sum(pair_up([ref[...] for ref in squares]), axis=0, keepdims=True)
        scale = lax.rsqrt(total / FF + epsilon)
        scale = jnp.transpose(jnp.broadcast_to(scale, (128, r)))[:, :1]
    depth = lax.axis_size("col")
    size = buf0.shape[0] // depth
    m = ortho_ref.shape[0]
    step = m // 2
    for b in range(count):
        k = b % 2
        if b >= 2:
            for store in stores(b - 2):
                store.wait()
        if weight_too:
            nbuf[k] = (blocks[b][...].astype(f32) * scale).astype(bf16)
        if momentum_too:
            for lo in range(0, m, step):
                correction = dot(ortho_ref[lo : lo + step, :], blocks[b][...])
                for j in range(lo // size, (lo + step) // size):
                    here = slice(j // 2 * size, (j // 2 + 1) * size)
                    part = correction[j * size - lo : (j + 1) * size - lo]
                    old = (buf0, buf1)[j % 2][here, cols[b]]
                    mbuf[k, j * size : (j + 1) * size, :] = old - (1.0 - momentum_decay) * part
        if weight_too:
            load(b).wait()
            for lo in range(0, m, step):
                at = slice(lo, lo + step)
                change = dot(ortho_ref[at, :], nbuf[k])
                vbuf[k, at, :] = (wbuf[k, at, :].astype(f32) - factor * change).astype(bf16)
        for store in stores(b):
            store.start()
        if weight_too and b + 2 < count:
            load(b + 2).start()
    sums[...] = square_rows(blocks, ids, sums.shape) if momentum_too else jnp.zeros_like(sums)
    for b in range(count - 2, count):
        for store in stores(b):
            store.wait()


def results(pairs, kinds, factor, bufs, ortho_bf, weight, squares, blocks, outs=(), after=()):
    momentum_too, weight_too = kinds
    m, n = weight.shape
    r, width = blocks[0].shape
    ins = [*map(keep, bufs), ortho_bf, stay(weight), *squares, *blocks, *after, *map(stay, outs)]
    at = len(ins) - len(outs)
    out_shape = []
    if weight_too:
        out_shape += [shape((m, n), bf16), shape((r, n), bf16)]
    if momentum_too:
        out_shape += [shape((m, n), f32)]
    m_slots, w_slots = (m if momentum_too else 8), (m if weight_too else 16)
    return pl.pallas_call(
        functools.partial(result_kernel, pairs, factor, momentum_too, weight_too, len(squares)),
        out_shape=[*out_shape, shape((max(8, n // width), r), f32)],
        in_specs=[VMEM] * 3 + [ANY] + [VMEM] * (len(squares) + len(blocks)) + [ANY] * (len(after) + len(outs)),
        out_specs=[ANY] * len(out_shape) + [VMEM],
        input_output_aliases={at + k: k for k in range(len(outs))},
        scratch_shapes=[
            pltpu.VMEM((2, m_slots, width), f32),
            pltpu.VMEM((2, w_slots, width), bf16),
            pltpu.VMEM((2, w_slots, width), bf16),
            pltpu.VMEM((2, r, width), bf16),
            pltpu.SemaphoreType.DMA((2,)),
            pltpu.SemaphoreType.DMA((3, 2)),
        ],
        compiler_params=params(15),
        cost_estimate=cost(*[shape((m, width), f32)] * len(blocks) * (momentum_too + weight_too)),
        name="results",
    )(*ins)


def sum_over(x, axis, least=1):
    d = least
    while d < lax.axis_size(axis):
        x = x + swap(x, axis, d)
        d *= 2
    return x


def exchange(x, axis, count, unit=1):
    return [x] + [swap(x, axis, unit * d) for d in range(1, count)]


def pair_up(terms):
    while len(terms) > 1:
        terms = [terms[2 * i] + terms[2 * i + 1] for i in range(len(terms) // 2)]
    return terms[0]


def gather(x, axis):
    blocks = [x]
    size = lax.axis_size(axis)
    for d in range(1, size):
        low = d & -d
        blocks.append(swap(blocks[d - low] if d != low else x, axis, low))
    return blocks


def per_device(weight, gradient, momentum, old_basis):
    depth, rows = lax.axis_size("col"), lax.axis_size("row")
    chips = rows // 2
    m, n = momentum.shape
    width = n // rows

    def sum_over_col(held, sent, *before):
        half = m // 2 // depth
        d = 1
        while held.shape[1] > half:
            held, sent = fold(held, swap(sent, "col", d), half)
            d *= 2
        return fold_last(held, swap(sent, "col", d), *before)

    buf0, kept, *outs = project(momentum, gradient, old_basis, depth, width, 0)
    low = sum_over_col(*outs)
    buf1, *outs = project(momentum, gradient, kept, depth, width, 1, (outs[1],))
    lefts = gather(sum_over_col(*outs, low), "col")
    bufs = (buf0, buf1)

    other, mine, g_sums = first_product(bufs, lefts[:-1], depth, width)
    g_mine, g_other = gram(lefts[-1], g_sums)
    other = last_product(bufs, other, lefts[-1], depth, width, False, g_mine)
    g_mine = g_mine + swap(g_other, "row", 1)
    other = hand_on(other, g_mine)
    received = swap(other, "row", 1)
    mine = last_product(bufs, mine, lefts[-1], depth, width, True, g_mine, other)
    own, *sent = pair_sum(mine, received, chips, g_mine)
    g_mine = pair_up(exchange(g_mine, "row", chips, 2))
    got = [swap(x, "row", 2 * (d + 1)) for d, x in enumerate(sent)]
    inverse = chol_inverse(g_mine, swap(g_mine, "row", 1))

    share = share_of(inverse, own, got)
    ortho_bf = ortho(inverse, lefts)

    factor = step_rate * math.sqrt(D / RANK)
    common = (factor, bufs, ortho_bf, weight)
    blocks = {0: share}
    for d in range(1, chips):
        if d & (d - 1) == 0:
            blocks[d] = swap(share, "row", 2 * d)
    near = sorted(blocks)
    pairs = {0: (share, swap(share, "row", 1))}
    momentum, sums = results((0,), (True, False), *common, (), pairs[0])
    for d in near[1:]:
        blocks[d] = hand_on(blocks[d], sums)
        pairs[d] = (blocks[d], swap(blocks[d], "row", 1))
    far = [d for d in range(chips) if d not in blocks]
    h = share.shape[0] // 2
    halves = {}
    for d in far:
        least, most = d & -d, 1 << (d.bit_length() - 1)
        halves[d] = (
            swap(blocks[d ^ most][:h], "row", 2 * most),
            swap(blocks[d ^ least][h:], "row", 2 * least),
        )
        blocks[d] = jnp.concatenate(halves[d], axis=0)
    squares = [sums]
    rest = [x for d in near[1:] for x in pairs[d]]
    momentum, sums = results(tuple(near[1:]), (True, False), *common, (), rest, [momentum])
    squares.append(sums)
    for d in far:
        top, bottom = halves[d]
        block = jnp.concatenate([hand_on(top, sums), bottom], axis=0)
        pairs[d] = (block, swap(block, "row", 1))
    if far:
        rest = [x for d in far for x in pairs[d]]
        total = squares_of(tuple(far), rest, squares)
        momentum, _ = results(tuple(far), (True, False), *common, (), rest, [momentum], [total])
    else:
        total = sum(squares)
    scales = exchange(total, "col", depth)
    order = near + far
    rest = [x for d in order for x in pairs[d]]
    new_weight, new_basis, _ = results(tuple(order), (False, True), *common, scales, rest)
    return (new_weight, momentum, new_basis)


def plain_per_device(weight, gradient, momentum, old_basis):
    buffer = momentum + gradient.astype(f32)
    buffer_low = buffer.astype(bf16)
    left_factor = lax.psum(dot(buffer_low, old_basis, ((1,), (1,))), "col")
    gram_share = lax.dot_general(
        left_factor,
        left_factor,
        (((0,), (0,)), ((), ())),
        precision=lax.Precision.HIGHEST,
        preferred_element_type=f32,
    )
    chol_factor = jnp.linalg.cholesky(lax.psum(gram_share, "row"))
    orthonormal = lax.linalg.triangular_solve(
        chol_factor, left_factor, left_side=False, lower=True, transpose_a=True
    ).astype(bf16)
    right_share = lax.psum_scatter(
        dot(orthonormal, buffer_low, ((0,), (0,))), "row", scatter_dimension=0, tiled=True
    )
    sum_squares = lax.psum(jnp.sum(right_share * right_share, axis=1), "col")
    scale_share = jnp.sqrt(sum_squares / FF + epsilon)
    basis_share = (right_share / scale_share[:, None]).astype(bf16)
    new_basis = lax.all_gather(basis_share, "row", axis=0, tiled=True)
    col_scale = lax.all_gather(scale_share, "row", axis=0, tiled=True)
    scaled = (orthonormal.astype(f32) * col_scale[None, :]).astype(bf16)
    new_momentum = buffer - (1.0 - momentum_decay) * dot(scaled, new_basis)
    factor = step_rate * math.sqrt(D / RANK)
    new_weight = (weight.astype(f32) - factor * dot(orthonormal, new_basis)).astype(bf16)
    return (new_weight, new_momentum, new_basis)


def power_of_two(k):
    return k > 1 and k & (k - 1) == 0


def solution(mesh):
    rows, depth = mesh.shape["row"], mesh.shape["col"]
    tiled = (
        power_of_two(rows // 2)
        and power_of_two(depth)
        and D % (rows * depth * 128) == 0
        and FF % (rows * depth * 256) == 0
    )
    return jax.shard_map(
        per_device if tiled else plain_per_device,
        mesh=mesh,
        in_specs=(P("row", "col"), P("row", "col"), P("row", "col"), P(None, "col")),
        out_specs=(P("row", "col"), P("row", "col"), P(None, "col")),
        check_vma=False,
    )
```

```python
import functools
import math

import jax
import jax.numpy as jnp
from jax import lax
from jax.experimental import pallas as pl
from jax.experimental.pallas import tpu as pltpu
from jax.sharding import PartitionSpec as P

D = 8192
FF = 24576
RANK = 256

epsilon = 1e-06
momentum_decay = 0.6
step_rate = 0.5

bf16, f32 = jnp.bfloat16, jnp.float32
VMEM = pl.BlockSpec(memory_space=pltpu.VMEM)
ANY = pl.BlockSpec(memory_space=pl.ANY)
MIB = 1 << 20


def shape(dims, kind):
    return jax.ShapeDtypeStruct(dims, kind)


def params(mib):
    return pltpu.CompilerParams(vmem_limit_bytes=mib * MIB)


def dot(a, b, dims=((1,), (0,))):
    return lax.dot_general(a, b, (dims, ((), ())), preferred_element_type=f32)


def split(x, terms):
    parts = []
    for _ in range(terms):
        part = x.astype(bf16)
        parts.append(part)
        x = x - part.astype(f32)
    return parts


def flip(i, d):
    return lax.bitwise_xor(i, jnp.int32(d))


def swap(x, axis, d):
    return lax.ppermute(x, axis, [(i, i ^ d) for i in range(lax.axis_size(axis))])


def project_kernel(part, depth, width, mom, grad, basis, *rest):
    if part == 0:
        (buf, kept), rest = rest[:2], rest[2:]
    else:
        kept, buf, rest = basis, rest[1], rest[2:]
    held, sent, gbuf, total, sems, basis_sem = rest
    m, n = buf.shape
    half = m // depth

    def copies(c):
        cols = pl.ds(pl.multiple_of(c * width, 128), width)
        pairs = []
        for k in range(depth):
            there = pl.ds((2 * k + part) * half, half)
            here = pl.ds(k * half, half)
            pairs.append(pltpu.make_async_copy(mom.at[there, cols], buf.at[here, cols], sems.at[0, k, c]))
            pairs.append(pltpu.make_async_copy(grad.at[there, cols], gbuf.at[here, cols], sems.at[1, k, c]))
        if part == 0:
            pairs.append(pltpu.make_async_copy(basis.at[:, cols], kept.at[:, cols], basis_sem.at[c]))
        return pairs

    def start(c, carry):
        for copy in copies(c):
            copy.start()
        return carry

    def step(c, carry):
        for copy in copies(c):
            copy.wait()
        cols = pl.ds(pl.multiple_of(c * width, 128), width)
        added = buf[:, cols] + gbuf[:, cols].astype(f32)
        buf[:, cols] = added
        total[...] += dot(added.astype(bf16), kept[:, cols], ((1,), (1,)))
        return carry

    total[...] = jnp.zeros_like(total)
    lax.fori_loop(0, n // width, start, 0)
    lax.fori_loop(0, n // width, step, 0)
    me = lax.axis_index("col")
    for out, odd in ((held, 0), (sent, 1)):
        for j in range(depth // 2):
            rows = pl.ds(pl.multiple_of(flip(me, 2 * j + odd) * half, half), half)
            out[:, j * half : (j + 1) * half] = jnp.transpose(total[rows, :]).astype(out.dtype)


def project(momentum, gradient, basis, depth, width, part, after=()):
    m, n = momentum.shape
    m = m // 2
    r = basis.shape[0]
    kept = [] if part else [pltpu.VMEM((r, n), bf16)]
    return pl.pallas_call(
        functools.partial(project_kernel, part, depth, width),
        out_shape=(pltpu.VMEM((m, n), f32), *kept, shape((r, m // 2), f32), shape((r, m // 2), bf16)),
        in_specs=[ANY, ANY] + [VMEM if part else ANY] + [ANY] * len(after),
        out_specs=(VMEM,) * (3 + len(kept)),
        scratch_shapes=[
            pltpu.VMEM((m, n), bf16),
            pltpu.VMEM((m, r), f32),
            pltpu.SemaphoreType.DMA((2, depth, n // width)),
            pltpu.SemaphoreType.DMA((n // width,)),
        ],
        compiler_params=params(14),
        cost_estimate=cost(momentum, gradient),
        name="project",
    )(stay(momentum), stay(gradient), keep(basis) if part else stay(basis), *after)


def fold_kernel(half, held, received, held_out, sent_out):
    added = held[...] + received[...].astype(f32)
    for j in range(held_out.shape[1] // half):
        at = slice(j * half, (j + 1) * half)
        held_out[:, at] = added[:, 2 * j * half : (2 * j + 1) * half]
        sent_out[:, at] = added[:, (2 * j + 1) * half : (2 * j + 2) * half].astype(bf16)


def fold(held, received, half):
    r, size = held.shape
    return pl.pallas_call(
        functools.partial(fold_kernel, half),
        out_shape=(shape((r, size // 2), f32), shape((r, size // 2), bf16)),
        in_specs=[VMEM, VMEM],
        out_specs=(VMEM, VMEM),
        compiler_params=params(8),
        name="fold",
    )(held, received)


def fold_last_kernel(held, received, *rest):
    before, out = rest[:-1], rest[-1]
    half = held.shape[1]
    for k, ref in enumerate(before):
        out[:, k * half : (k + 1) * half] = ref[...]
    out[:, len(before) * half :] = (held[...] + received[...].astype(f32)).astype(bf16)


def fold_last(held, received, *before):
    r, half = held.shape
    return pl.pallas_call(
        fold_last_kernel,
        out_shape=shape((r, half * (1 + len(before))), bf16),
        in_specs=[VMEM] * (2 + len(before)),
        out_specs=VMEM,
        compiler_params=params(8),
        name="fold_last",
    )(held, received, *before)


def cost(*arrays):
    size = sum(math.prod(x.shape) * x.dtype.itemsize for x in arrays)
    return pl.CostEstimate(flops=0, bytes_accessed=size, transcendentals=0)


def keep(x):
    return pltpu.with_memory_space_constraint(x, pltpu.VMEM)


def stay(x):
    return pltpu.with_memory_space_constraint(x, pltpu.HBM)


def buffer_rows(bufs, ds, depth, cols):
    half = bufs[0].shape[0] // depth
    me = lax.axis_index("col")
    rows = [pl.ds(pl.multiple_of(flip(me, d) * half, half), half) for d in ds]
    return jnp.concatenate([buf[at, cols].astype(bf16) for at in rows for buf in bufs], axis=0)


def early(depth):
    return (0, depth // 2)


def late(depth):
    return tuple(d for d in range(depth) if d not in early(depth))


def first_kernel(depth, width, buf0, buf1, *rest):
    lefts, (other, mine, gram, whole) = rest[:-4], rest[-4:]
    core = lax.bitwise_and(lax.axis_index("row"), jnp.int32(1))
    size = other.shape[1]
    block = lefts[0].shape[1]
    for d, ref in enumerate(lefts):
        whole[:, d * block : (d + 1) * block] = ref[...]
    gram[...] = dot(whole[...], whole[...], ((1,), (1,)))
    for out, half in ((other, 1 - core), (mine, core)):

        def step(k, carry, out=out, half=half):
            cols = pl.ds(pl.multiple_of(half * size + k * width, 128), width)
            b = buffer_rows((buf0, buf1), early(depth), depth, cols)
            out[:, pl.ds(pl.multiple_of(k * width, 128), width)] = dot(whole[...], b)
            return carry

        lax.fori_loop(0, size // width, step, 0)


def first_product(bufs, lefts, depth, width):
    m, n = bufs[0].shape
    r, block = lefts[0].shape
    return pl.pallas_call(
        functools.partial(first_kernel, depth, width),
        out_shape=(shape((r, n // 2), f32), shape((r, n // 2), f32), shape((r, r), f32)),
        in_specs=[VMEM] * (2 + len(lefts)),
        out_specs=[VMEM] * 3,
        scratch_shapes=[pltpu.VMEM((r, block * len(lefts)), bf16)],
        compiler_params=params(10),
        cost_estimate=cost(*bufs, shape((r, n), f32)),
        name="first_product",
    )(*map(keep, bufs), *lefts)


def gram_kernel(sums, *rest):
    lefts, (g_mine, g_other, total) = rest[:-3], rest[-3:]
    core = lax.bitwise_and(lax.axis_index("row"), jnp.int32(1))
    total[...] = sums[...] + sum(dot(ref[...], ref[...], ((1,), (1,))) for ref in lefts)
    h = g_mine.shape[0]
    g_mine[...] = total[pl.ds(pl.multiple_of(core * h, h), h), :]
    g_other[...] = total[pl.ds(pl.multiple_of((1 - core) * h, h), h), :]


def gram(lefts, sums):
    r = lefts[0].shape[0]
    return pl.pallas_call(
        gram_kernel,
        out_shape=[shape((r // 2, r), f32)] * 2,
        in_specs=[VMEM] * (1 + len(lefts)),
        out_specs=[VMEM] * 2,
        scratch_shapes=[pltpu.VMEM((r, r), f32)],
        compiler_params=params(8),
        name="gram",
    )(sums, *lefts)


def last_kernel(depth, width, mine, buf0, buf1, sums, *rest):
    lefts, (*_, out, whole) = rest[: len(late(depth))], rest[len(late(depth)) :]
    core = lax.bitwise_and(lax.axis_index("row"), jnp.int32(1))
    half = core if mine else 1 - core
    size = out.shape[1]
    block = lefts[0].shape[1]
    for k, ref in enumerate(lefts):
        whole[:, k * block : (k + 1) * block] = ref[...]

    def step(k, carry):
        cols = pl.ds(pl.multiple_of(half * size + k * width, 128), width)
        at = pl.ds(pl.multiple_of(k * width, 128), width)
        b = buffer_rows((buf0, buf1), late(depth), depth, cols)
        out[:, at] = (sums[:, at] + dot(whole[...], b)).astype(out.dtype)
        return carry

    lax.fori_loop(0, size // width, step, 0)


def last_product(bufs, sums, lefts, depth, width, mine, *after):
    r, block = lefts[0].shape
    return pl.pallas_call(
        functools.partial(last_kernel, depth, width, mine),
        out_shape=shape(sums.shape, f32 if mine else bf16),
        in_specs=[VMEM] * (3 + len(lefts)) + [ANY] * len(after),
        out_specs=VMEM,
        scratch_shapes=[pltpu.VMEM((r, block * len(lefts)), bf16)],
        compiler_params=params(8),
        cost_estimate=cost(*bufs[:1], sums),
        name="mine_product" if mine else "other_product",
    )(*map(keep, bufs), sums, *lefts, *after)


def pair_sum_kernel(chips, mine, received, _, *outs):
    me = lax.div(lax.axis_index("row"), jnp.int32(2))
    width = outs[0].shape[1]
    for d in range(chips):
        cols = pl.ds(pl.multiple_of(flip(me, d) * width, 128), width)
        outs[d][...] = (mine[:, cols] + received[:, cols].astype(f32)).astype(outs[d].dtype)


def pair_sum(mine, received, chips, after):
    r, n = mine.shape
    kinds = [f32] + [bf16] * (chips - 1)
    return pl.pallas_call(
        functools.partial(pair_sum_kernel, chips),
        out_shape=[shape((r, n // chips), k) for k in kinds],
        in_specs=[VMEM, VMEM, ANY],
        out_specs=[VMEM] * chips,
        compiler_params=params(8),
        name="pair_sum",
    )(mine, received, after)


def eliminate(tiles, at, nb, group):
    sub = lax.broadcasted_iota(jnp.int32, (nb, 128), 0)
    scale = jnp.zeros((nb, 128), f32)
    for g in range(0, nb, group):
        cols = [
            jnp.broadcast_to(tiles[0][:, at + g + j : at + g + j + 1], (nb, 128)) for j in range(group)
        ]
        for j in range(group):
            t = g + j
            pivot = cols[j][t : t + 1, :]
            factor = jnp.where(sub > t, cols[j], 0.0) * (1.0 / pivot)
            scale = jnp.where(sub == t, lax.rsqrt(pivot), scale)
            for l in range(j + 1, group):
                cols[l] = cols[l] - factor * cols[l][t : t + 1, :]
            tiles = [x - factor * x[t : t + 1, :] for x in tiles]
    return [x * scale for x in tiles]


def chol_inverse_kernel(mine, other, out, work):
    n = out.shape[0]
    h = n // 2
    core = lax.bitwise_and(lax.axis_index("row"), jnp.int32(1))
    work[pl.ds(pl.multiple_of(core * h, h), h), :n] = mine[...]
    work[pl.ds(pl.multiple_of((1 - core) * h, h), h), :n] = other[...]
    r_id = lax.broadcasted_iota(jnp.int32, (n, n), 0)
    c_id = lax.broadcasted_iota(jnp.int32, (n, n), 1)
    work[:, n:] = jnp.where(r_id == c_id, 1.0, 0.0).astype(f32)
    nb = 32
    for p in range(n // nb):
        lo = p * nb
        left = (lo // 128) * 128
        right = n + ((lo + nb + 127) // 128) * 128
        tiles = [work[lo : lo + nb, c : c + 128] for c in range(left, right, 128)]
        s = jnp.concatenate(eliminate(tiles, lo - left, nb, 8), axis=1)
        work[lo : lo + nb, left:right] = s
        if lo + nb < n:
            lead = s[:, lo + nb - left : n - left]
            work[lo + nb :, left:right] -= lax.dot_general(
                lead, s, (((0,), (0,)), ((), ())), precision=lax.Precision.HIGHEST, preferred_element_type=f32
            )
    out[...] = jnp.where(r_id >= c_id, work[:, n:], 0.0)


def chol_inverse(mine, other):
    n = mine.shape[1]
    return pl.pallas_call(
        chol_inverse_kernel,
        out_shape=shape((n, n), f32),
        in_specs=[VMEM, VMEM],
        out_specs=VMEM,
        scratch_shapes=[pltpu.VMEM((n, 2 * n), f32)],
        compiler_params=params(8),
        cost_estimate=cost(*[mine] * 256),
        name="chol_inverse",
    )(mine, other)


def ortho_kernel(inverse, *refs):
    lefts, out = refs[:-1], refs[-1]
    block = lefts[0].shape[1]
    me = lax.axis_index("col")
    parts = split(inverse[...], 3)
    for d, ref in enumerate(lefts):
        rows = pl.ds(pl.multiple_of(flip(me, d) * block, block), block)
        out[rows, :] = sum(dot(ref[...], x, ((0,), (1,))) for x in reversed(parts)).astype(bf16)


def ortho(inverse, lefts):
    r, block = lefts[0].shape
    return pl.pallas_call(
        ortho_kernel,
        out_shape=shape((block * len(lefts), r), bf16),
        in_specs=[VMEM] * (1 + len(lefts)),
        out_specs=VMEM,
        compiler_params=params(8),
        cost_estimate=cost(*[shape((block * len(lefts), r), bf16)] * 8),
        name="ortho",
    )(inverse, *lefts)


def hand_on(x, *earlier):
    return pl.pallas_call(
        lambda *refs: None,
        out_shape=shape(x.shape, x.dtype),
        in_specs=[ANY] * (1 + len(earlier)),
        out_specs=ANY,
        input_output_aliases={0: 0},
        compiler_params=params(1),
        name="hand_on",
    )(x, *earlier)


def block_ids(pairs):
    row = lax.axis_index("row")
    core = lax.bitwise_and(row, jnp.int32(1))
    chip = lax.div(row, jnp.int32(2))
    chips = lax.axis_size("row") // 2
    return [half * chips + flip(chip, d) for d in pairs for half in (core, 1 - core)]


def share_kernel(inverse, own, *refs):
    received, (out, squares) = refs[:-2], refs[-2:]
    total = own[...] + sum(ref[...].astype(f32) for ref in received)
    x_high, x_low = split(inverse[...], 2)
    high, low = split(total, 2)
    right = dot(x_high, low) + dot(x_low, high) + dot(x_high, high)
    out[...] = right.astype(bf16)
    r = out.shape[0]
    sums = jnp.sum(right * right, axis=1, keepdims=True)
    sums = jnp.transpose(jnp.broadcast_to(sums, (r, 128)))[: squares.shape[0], :]
    block_id = lax.broadcasted_iota(jnp.int32, squares.shape, 0)
    squares[...] = jnp.where(block_id == block_ids((0,))[0], sums, 0.0)


def share_of(inverse, own, received):
    r, width = own.shape
    rows = max(8, lax.axis_size("row"))
    return pl.pallas_call(
        share_kernel,
        out_shape=(shape((r, width), bf16), shape((rows, r), f32)),
        in_specs=[VMEM] * (2 + len(received)),
        out_specs=(VMEM, VMEM),
        compiler_params=params(8),
        name="share",
    )(inverse, own, *received)


def result_kernel(pairs, factor, buf0, buf1, ortho_ref, squares, weight, *refs):
    blocks, rest = refs[: 2 * len(pairs)], refs[2 * len(pairs) :]
    *_, new_weight, new_momentum, basis, token, mbuf, wbuf, vbuf, nbuf, in_sems, out_sems, basis_sems = rest
    r, width = blocks[0].shape
    tile = 256
    tiles = width // tile
    count = len(blocks)
    starts = [i * width for i in block_ids(pairs)]

    def load(b):
        cols = pl.ds(pl.multiple_of(starts[b], 128), width)
        return pltpu.make_async_copy(weight.at[:, cols], wbuf.at[b % 2], in_sems.at[b % 2])

    def store_basis(b):
        cols = pl.ds(pl.multiple_of(starts[b], 128), width)
        return pltpu.make_async_copy(nbuf.at[b % 2], basis.at[:, cols], basis_sems.at[b % 2])

    def place(b, t):
        return pl.ds(t * tile, tile), pl.ds(pl.multiple_of(starts[b] + t * tile, 128), tile)

    def stores(b, t):
        at, there = place(b, t)
        return (
            pltpu.make_async_copy(mbuf.at[b % 2, :, at], new_momentum.at[:, there], out_sems.at[0, b % 2, t]),
            pltpu.make_async_copy(vbuf.at[b % 2, :, at], new_weight.at[:, there], out_sems.at[1, b % 2, t]),
        )

    def finish(b):
        store_basis(b).wait()
        for t in range(tiles):
            for store in stores(b, t):
                store.wait()

    for b in range(2):
        load(b).start()
    scale = lax.rsqrt(jnp.sum(squares[...], axis=0, keepdims=True) / FF + epsilon)
    scale = jnp.transpose(jnp.broadcast_to(scale, (128, r)))[:, :1]
    token[...] = jnp.zeros_like(token)
    depth = lax.axis_size("col")
    size = buf0.shape[0] // depth
    for b in range(count):
        k = b % 2
        if b >= 2:
            finish(b - 2)
        nbuf[k] = (blocks[b][...].astype(f32) * scale).astype(bf16)
        store_basis(b).start()
        load(b).wait()
        for t in range(tiles):
            at, there = place(b, t)
            correction = dot(ortho_ref[...], blocks[b][:, at])
            for j in range(2 * depth):
                rows = slice(j * size, (j + 1) * size)
                here = slice(j // 2 * size, (j // 2 + 1) * size)
                old = (buf0, buf1)[j % 2][here, there]
                mbuf[k, rows, at] = old - (1.0 - momentum_decay) * correction[rows]
            change = dot(ortho_ref[...], nbuf[k, :, at])
            vbuf[k, :, at] = (wbuf[k, :, at].astype(f32) - factor * change).astype(bf16)
            for store in stores(b, t):
                store.start()
        if b + 2 < count:
            load(b + 2).start()
    for b in range(count - 2, count):
        finish(b)


def results(pairs, factor, bufs, ortho_bf, squares, weight, blocks, outs=(), after=()):
    m, n = weight.shape
    r, width = blocks[0].shape
    ins = [*map(keep, bufs), ortho_bf, squares, stay(weight), *blocks, *after, *map(stay, outs)]
    at = len(ins) - len(outs)
    *outs, token = pl.pallas_call(
        functools.partial(result_kernel, pairs, factor),
        out_shape=[shape((m, n), bf16), shape((m, n), f32), shape((r, n), bf16), shape((8, 128), f32)],
        in_specs=[VMEM] * 4 + [ANY] + [VMEM] * len(blocks) + [ANY] * (len(after) + len(outs)),
        out_specs=[ANY] * 3 + [VMEM],
        input_output_aliases={at + k: k for k in range(len(outs))},
        scratch_shapes=[
            pltpu.VMEM((2, m, width), f32),
            pltpu.VMEM((2, m, width), bf16),
            pltpu.VMEM((2, m, width), bf16),
            pltpu.VMEM((2, r, width), bf16),
            pltpu.SemaphoreType.DMA((2,)),
            pltpu.SemaphoreType.DMA((2, 2, width // 256)),
            pltpu.SemaphoreType.DMA((2,)),
        ],
        compiler_params=params(15),
        cost_estimate=cost(*[shape((m, width), f32)] * (2 * len(blocks))),
        name="results",
    )(*ins)
    return outs, token


def sum_over(x, axis, least=1):
    d = least
    while d < lax.axis_size(axis):
        x = x + swap(x, axis, d)
        d *= 2
    return x


def exchange(x, axis, count, unit=1):
    return [x] + [swap(x, axis, unit * d) for d in range(1, count)]


def pair_up(terms):
    while len(terms) > 1:
        terms = [terms[2 * i] + terms[2 * i + 1] for i in range(len(terms) // 2)]
    return terms[0]


def gather(x, axis):
    blocks = [x]
    size = lax.axis_size(axis)
    for d in range(1, size):
        low = d & -d
        blocks.append(swap(blocks[d - low] if d != low else x, axis, low))
    return blocks


def per_device(weight, gradient, momentum, old_basis):
    depth, rows = lax.axis_size("col"), lax.axis_size("row")
    chips = rows // 2
    m, n = momentum.shape
    width = n // rows

    def sum_over_col(held, sent, *before):
        half = m // 2 // depth
        d = 1
        while held.shape[1] > half:
            held, sent = fold(held, swap(sent, "col", d), half)
            d *= 2
        return fold_last(held, swap(sent, "col", d), *before)

    buf0, kept, *outs = project(momentum, gradient, old_basis, depth, width, 0)
    low = sum_over_col(*outs)
    buf1, *outs = project(momentum, gradient, kept, depth, width, 1, (outs[1],))
    lefts = gather(sum_over_col(*outs, low), "col")
    bufs = (buf0, buf1)

    other, mine, g_sums = first_product(bufs, [lefts[d] for d in early(depth)], depth, width)
    lefts_late = [lefts[d] for d in late(depth)]
    g_mine, g_other = gram(lefts_late, g_sums)
    other = last_product(bufs, other, lefts_late, depth, width, False, g_mine)
    g_mine = g_mine + swap(g_other, "row", 1)
    other = hand_on(other, g_mine)
    received = swap(other, "row", 1)
    mine = last_product(bufs, mine, lefts_late, depth, width, True, g_mine, other)
    own, *sent = pair_sum(mine, received, chips, g_mine)
    g_mine = pair_up(exchange(g_mine, "row", chips, 2))
    got = [swap(x, "row", 2 * (d + 1)) for d, x in enumerate(sent)]
    inverse = chol_inverse(g_mine, swap(g_mine, "row", 1))

    share, squares = share_of(inverse, own, got)
    ortho_bf = ortho(inverse, lefts)

    near = [d for d in range(chips) if d & (d - 1) == 0]
    blocks = {d: swap(share, "row", 2 * d) for d in near[1:]}
    own_pair = swap(share, "row", 1)
    squares = pair_up(exchange(hand_on(squares, own_pair), "col", depth))
    squares = hand_on(squares, *blocks.values(), ortho_bf)
    squares = pair_up(exchange(squares, "row", chips, 2))
    pairs = {}
    for d in near[1:]:
        block = hand_on(blocks[d], squares)
        pairs[d] = (block, swap(block, "row", 1))
    squares = squares + swap(squares, "row", 1)
    share = hand_on(share, *[pair[0] for pair in pairs.values()])
    pairs[0] = (share, own_pair)
    far = [d for d in range(chips) if d not in near]
    blocks = {d: swap(share, "row", 2 * d) for d in far}

    factor = step_rate * math.sqrt(D / RANK)
    common = (factor, bufs, ortho_bf, squares, weight)
    outs, token = (), share
    if near[1:]:
        rest = [x for d in near[1:] for x in pairs[d]]
        outs, token = results(tuple(near[1:]), *common, rest, (), (share,))
    blocks = {d: hand_on(block, token) for d, block in blocks.items()}
    outs, token = results((0,), *common, pairs[0], outs)
    for d, block in blocks.items():
        outs, token = results((d,), *common, (block, swap(block, "row", 1)), outs)
    new_weight, new_momentum, new_basis = outs
    return (new_weight, new_momentum, new_basis)


def plain_per_device(weight, gradient, momentum, old_basis):
    buffer = momentum + gradient.astype(f32)
    buffer_low = buffer.astype(bf16)
    left_factor = lax.psum(dot(buffer_low, old_basis, ((1,), (1,))), "col")
    gram_share = lax.dot_general(
        left_factor,
        left_factor,
        (((0,), (0,)), ((), ())),
        precision=lax.Precision.HIGHEST,
        preferred_element_type=f32,
    )
    chol_factor = jnp.linalg.cholesky(lax.psum(gram_share, "row"))
    orthonormal = lax.linalg.triangular_solve(
        chol_factor, left_factor, left_side=False, lower=True, transpose_a=True
    ).astype(bf16)
    right_share = lax.psum_scatter(
        dot(orthonormal, buffer_low, ((0,), (0,))), "row", scatter_dimension=0, tiled=True
    )
    sum_squares = lax.psum(jnp.sum(right_share * right_share, axis=1), "col")
    scale_share = jnp.sqrt(sum_squares / FF + epsilon)
    basis_share = (right_share / scale_share[:, None]).astype(bf16)
    new_basis = lax.all_gather(basis_share, "row", axis=0, tiled=True)
    col_scale = lax.all_gather(scale_share, "row", axis=0, tiled=True)
    scaled = (orthonormal.astype(f32) * col_scale[None, :]).astype(bf16)
    new_momentum = buffer - (1.0 - momentum_decay) * dot(scaled, new_basis)
    factor = step_rate * math.sqrt(D / RANK)
    new_weight = (weight.astype(f32) - factor * dot(orthonormal, new_basis)).astype(bf16)
    return (new_weight, new_momentum, new_basis)


def power_of_two(k):
    return k > 1 and k & (k - 1) == 0


def solution(mesh):
    rows, depth = mesh.shape["row"], mesh.shape["col"]
    tiled = (
        power_of_two(rows // 2)
        and power_of_two(depth)
        and depth > 2
        and D % (rows * depth * 128) == 0
        and FF % (rows * depth * 256) == 0
    )
    return jax.shard_map(
        per_device if tiled else plain_per_device,
        mesh=mesh,
        in_specs=(P("row", "col"), P("row", "col"), P("row", "col"), P(None, "col")),
        out_specs=(P("row", "col"), P("row", "col"), P(None, "col")),
        check_vma=False,
    )
```

```python
import functools
import math

import jax
import jax.numpy as jnp
from jax import lax
from jax.experimental import pallas as pl
from jax.experimental.pallas import tpu as pltpu
from jax.sharding import PartitionSpec as P

D = 8192
FF = 24576
RANK = 256

epsilon = 1e-06
momentum_decay = 0.6
step_rate = 0.5

bf16, f32 = jnp.bfloat16, jnp.float32
VMEM = pl.BlockSpec(memory_space=pltpu.VMEM)
ANY = pl.BlockSpec(memory_space=pl.ANY)
MIB = 1 << 20


def shape(dims, kind):
    return jax.ShapeDtypeStruct(dims, kind)


def params(mib):
    return pltpu.CompilerParams(vmem_limit_bytes=mib * MIB)


def dot(a, b, dims=((1,), (0,))):
    return lax.dot_general(a, b, (dims, ((), ())), preferred_element_type=f32)


def split(x, terms):
    parts = []
    for _ in range(terms):
        part = x.astype(bf16)
        parts.append(part)
        x = x - part.astype(f32)
    return parts


def flip(i, d):
    return lax.bitwise_xor(i, jnp.int32(d))


def swap(x, axis, d):
    return lax.ppermute(x, axis, [(i, i ^ d) for i in range(lax.axis_size(axis))])


def project_kernel(part, depth, width, mom, grad, basis, *rest):
    if part == 0:
        (buf, kept), rest = rest[:2], rest[2:]
    else:
        kept, buf, rest = basis, rest[1], rest[2:]
    held, sent, gbuf, total, sems, basis_sem = rest
    m, n = buf.shape
    half = m // depth

    def copies(c):
        cols = pl.ds(pl.multiple_of(c * width, 128), width)
        pairs = []
        for k in range(depth):
            there = pl.ds((2 * k + part) * half, half)
            here = pl.ds(k * half, half)
            pairs.append(pltpu.make_async_copy(mom.at[there, cols], buf.at[here, cols], sems.at[0, k, c]))
            pairs.append(pltpu.make_async_copy(grad.at[there, cols], gbuf.at[here, cols], sems.at[1, k, c]))
        if part == 0:
            pairs.append(pltpu.make_async_copy(basis.at[:, cols], kept.at[:, cols], basis_sem.at[c]))
        return pairs

    def start(c, carry):
        for copy in copies(c):
            copy.start()
        return carry

    def step(c, carry):
        for copy in copies(c):
            copy.wait()
        cols = pl.ds(pl.multiple_of(c * width, 128), width)
        added = buf[:, cols] + gbuf[:, cols].astype(f32)
        buf[:, cols] = added
        total[...] += dot(added.astype(bf16), kept[:, cols], ((1,), (1,)))
        return carry

    total[...] = jnp.zeros_like(total)
    lax.fori_loop(0, n // width, start, 0)
    lax.fori_loop(0, n // width, step, 0)
    me = lax.axis_index("col")
    for out, odd in ((held, 0), (sent, 1)):
        for j in range(depth // 2):
            rows = pl.ds(pl.multiple_of(flip(me, 2 * j + odd) * half, half), half)
            out[:, j * half : (j + 1) * half] = jnp.transpose(total[rows, :]).astype(out.dtype)


def project(momentum, gradient, basis, depth, width, part, after=()):
    m, n = momentum.shape
    m = m // 2
    r = basis.shape[0]
    kept = [] if part else [pltpu.VMEM((r, n), bf16)]
    return pl.pallas_call(
        functools.partial(project_kernel, part, depth, width),
        out_shape=(pltpu.VMEM((m, n), f32), *kept, shape((r, m // 2), f32), shape((r, m // 2), bf16)),
        in_specs=[ANY, ANY] + [VMEM if part else ANY] + [ANY] * len(after),
        out_specs=(VMEM,) * (3 + len(kept)),
        scratch_shapes=[
            pltpu.VMEM((m, n), bf16),
            pltpu.VMEM((m, r), f32),
            pltpu.SemaphoreType.DMA((2, depth, n // width)),
            pltpu.SemaphoreType.DMA((n // width,)),
        ],
        compiler_params=params(14),
        cost_estimate=cost(momentum, gradient),
        name="project",
    )(stay(momentum), stay(gradient), keep(basis) if part else stay(basis), *after)


def fold_kernel(half, held, received, held_out, sent_out):
    added = held[...] + received[...].astype(f32)
    for j in range(held_out.shape[1] // half):
        at = slice(j * half, (j + 1) * half)
        held_out[:, at] = added[:, 2 * j * half : (2 * j + 1) * half]
        sent_out[:, at] = added[:, (2 * j + 1) * half : (2 * j + 2) * half].astype(bf16)


def fold(held, received, half):
    r, size = held.shape
    return pl.pallas_call(
        functools.partial(fold_kernel, half),
        out_shape=(shape((r, size // 2), f32), shape((r, size // 2), bf16)),
        in_specs=[VMEM, VMEM],
        out_specs=(VMEM, VMEM),
        compiler_params=params(8),
        name="fold",
    )(held, received)


def fold_last_kernel(held, received, *rest):
    before, out = rest[:-1], rest[-1]
    half = held.shape[1]
    for k, ref in enumerate(before):
        out[:, k * half : (k + 1) * half] = ref[...]
    out[:, len(before) * half :] = (held[...] + received[...].astype(f32)).astype(bf16)


def fold_last(held, received, *before):
    r, half = held.shape
    return pl.pallas_call(
        fold_last_kernel,
        out_shape=shape((r, half * (1 + len(before))), bf16),
        in_specs=[VMEM] * (2 + len(before)),
        out_specs=VMEM,
        compiler_params=params(8),
        name="fold_last",
    )(held, received, *before)


def cost(*arrays):
    size = sum(math.prod(x.shape) * x.dtype.itemsize for x in arrays)
    return pl.CostEstimate(flops=0, bytes_accessed=size, transcendentals=0)


def keep(x):
    return pltpu.with_memory_space_constraint(x, pltpu.VMEM)


def stay(x):
    return pltpu.with_memory_space_constraint(x, pltpu.HBM)


def buffer_rows(bufs, ds, depth, cols):
    half = bufs[0].shape[0] // depth
    me = lax.axis_index("col")
    rows = [pl.ds(pl.multiple_of(flip(me, d) * half, half), half) for d in ds]
    return jnp.concatenate([buf[at, cols].astype(bf16) for at in rows for buf in bufs], axis=0)


def early(depth):
    return (0, depth // 2)


def late(depth):
    return tuple(d for d in range(depth) if d not in early(depth))


def first_kernel(depth, width, buf0, buf1, *rest):
    lefts, (other, mine, gram, whole) = rest[:-4], rest[-4:]
    core = lax.bitwise_and(lax.axis_index("row"), jnp.int32(1))
    size = other.shape[1]
    block = lefts[0].shape[1]
    for d, ref in enumerate(lefts):
        whole[:, d * block : (d + 1) * block] = ref[...]
    gram[...] = dot(whole[...], whole[...], ((1,), (1,)))
    for out, half in ((other, 1 - core), (mine, core)):

        def step(k, carry, out=out, half=half):
            cols = pl.ds(pl.multiple_of(half * size + k * width, 128), width)
            b = buffer_rows((buf0, buf1), early(depth), depth, cols)
            out[:, pl.ds(pl.multiple_of(k * width, 128), width)] = dot(whole[...], b)
            return carry

        lax.fori_loop(0, size // width, step, 0)


def first_product(bufs, lefts, depth, width):
    m, n = bufs[0].shape
    r, block = lefts[0].shape
    return pl.pallas_call(
        functools.partial(first_kernel, depth, width),
        out_shape=(shape((r, n // 2), f32), shape((r, n // 2), f32), shape((r, r), f32)),
        in_specs=[VMEM] * (2 + len(lefts)),
        out_specs=[VMEM] * 3,
        scratch_shapes=[pltpu.VMEM((r, block * len(lefts)), bf16)],
        compiler_params=params(10),
        cost_estimate=cost(*bufs, shape((r, n), f32)),
        name="first_product",
    )(*map(keep, bufs), *lefts)


def gram_kernel(sums, *rest):
    lefts, (g_mine, g_other, total) = rest[:-3], rest[-3:]
    core = lax.bitwise_and(lax.axis_index("row"), jnp.int32(1))
    total[...] = sums[...] + sum(dot(ref[...], ref[...], ((1,), (1,))) for ref in lefts)
    h = g_mine.shape[0]
    g_mine[...] = total[pl.ds(pl.multiple_of(core * h, h), h), :]
    g_other[...] = total[pl.ds(pl.multiple_of((1 - core) * h, h), h), :]


def gram(lefts, sums):
    r = lefts[0].shape[0]
    return pl.pallas_call(
        gram_kernel,
        out_shape=[shape((r // 2, r), f32)] * 2,
        in_specs=[VMEM] * (1 + len(lefts)),
        out_specs=[VMEM] * 2,
        scratch_shapes=[pltpu.VMEM((r, r), f32)],
        compiler_params=params(8),
        name="gram",
    )(sums, *lefts)


def last_kernel(depth, width, mine, buf0, buf1, sums, *rest):
    lefts, (*_, out, whole) = rest[: len(late(depth))], rest[len(late(depth)) :]
    core = lax.bitwise_and(lax.axis_index("row"), jnp.int32(1))
    half = core if mine else 1 - core
    size = out.shape[1]
    block = lefts[0].shape[1]
    for k, ref in enumerate(lefts):
        whole[:, k * block : (k + 1) * block] = ref[...]

    def step(k, carry):
        cols = pl.ds(pl.multiple_of(half * size + k * width, 128), width)
        at = pl.ds(pl.multiple_of(k * width, 128), width)
        b = buffer_rows((buf0, buf1), late(depth), depth, cols)
        out[:, at] = (sums[:, at] + dot(whole[...], b)).astype(out.dtype)
        return carry

    lax.fori_loop(0, size // width, step, 0)


def last_product(bufs, sums, lefts, depth, width, mine, *after):
    r, block = lefts[0].shape
    return pl.pallas_call(
        functools.partial(last_kernel, depth, width, mine),
        out_shape=shape(sums.shape, f32 if mine else bf16),
        in_specs=[VMEM] * (3 + len(lefts)) + [ANY] * len(after),
        out_specs=VMEM,
        scratch_shapes=[pltpu.VMEM((r, block * len(lefts)), bf16)],
        compiler_params=params(8),
        cost_estimate=cost(*bufs[:1], sums),
        name="mine_product" if mine else "other_product",
    )(*map(keep, bufs), sums, *lefts, *after)


def pair_sum_kernel(chips, mine, received, _, *outs):
    me = lax.div(lax.axis_index("row"), jnp.int32(2))
    width = outs[0].shape[1]
    for d in range(chips):
        cols = pl.ds(pl.multiple_of(flip(me, d) * width, 128), width)
        outs[d][...] = (mine[:, cols] + received[:, cols].astype(f32)).astype(outs[d].dtype)


def pair_sum(mine, received, chips, after):
    r, n = mine.shape
    kinds = [f32] + [bf16] * (chips - 1)
    return pl.pallas_call(
        functools.partial(pair_sum_kernel, chips),
        out_shape=[shape((r, n // chips), k) for k in kinds],
        in_specs=[VMEM, VMEM, ANY],
        out_specs=[VMEM] * chips,
        compiler_params=params(8),
        name="pair_sum",
    )(mine, received, after)


def eliminate(tiles, at, nb, group):
    sub = lax.broadcasted_iota(jnp.int32, (nb, 128), 0)
    scale = jnp.zeros((nb, 128), f32)
    for g in range(0, nb, group):
        cols = [
            jnp.broadcast_to(tiles[0][:, at + g + j : at + g + j + 1], (nb, 128)) for j in range(group)
        ]
        for j in range(group):
            t = g + j
            pivot = cols[j][t : t + 1, :]
            factor = jnp.where(sub > t, cols[j], 0.0) * (1.0 / pivot)
            scale = jnp.where(sub == t, lax.rsqrt(pivot), scale)
            for l in range(j + 1, group):
                cols[l] = cols[l] - factor * cols[l][t : t + 1, :]
            tiles = [x - factor * x[t : t + 1, :] for x in tiles]
    return [x * scale for x in tiles]


def chol_inverse_kernel(mine, other, weight, out, fetched, work, sem):
    fetch = pltpu.make_async_copy(weight, fetched, sem)
    fetch.start()
    n = out.shape[0]
    h = n // 2
    core = lax.bitwise_and(lax.axis_index("row"), jnp.int32(1))
    work[pl.ds(pl.multiple_of(core * h, h), h), :n] = mine[...]
    work[pl.ds(pl.multiple_of((1 - core) * h, h), h), :n] = other[...]
    r_id = lax.broadcasted_iota(jnp.int32, (n, n), 0)
    c_id = lax.broadcasted_iota(jnp.int32, (n, n), 1)
    work[:, n:] = jnp.where(r_id == c_id, 1.0, 0.0).astype(f32)
    nb = 32
    for p in range(n // nb):
        lo = p * nb
        left = (lo // 128) * 128
        right = n + ((lo + nb + 127) // 128) * 128
        tiles = [work[lo : lo + nb, c : c + 128] for c in range(left, right, 128)]
        s = jnp.concatenate(eliminate(tiles, lo - left, nb, 8), axis=1)
        work[lo : lo + nb, left:right] = s
        if lo + nb < n:
            lead = s[:, lo + nb - left : n - left]
            work[lo + nb :, left:right] -= lax.dot_general(
                lead, s, (((0,), (0,)), ((), ())), precision=lax.Precision.HIGHEST, preferred_element_type=f32
            )
    out[...] = jnp.where(r_id >= c_id, work[:, n:], 0.0)
    fetch.wait()


def chol_inverse(mine, other, weight):
    n = mine.shape[1]
    return pl.pallas_call(
        chol_inverse_kernel,
        out_shape=(shape((n, n), f32), pltpu.VMEM(weight.shape, weight.dtype)),
        in_specs=[VMEM, VMEM, ANY],
        out_specs=(VMEM, VMEM),
        scratch_shapes=[pltpu.VMEM((n, 2 * n), f32), pltpu.SemaphoreType.DMA],
        compiler_params=params(8),
        cost_estimate=cost(*[mine] * 256),
        name="chol_inverse",
    )(mine, other, stay(weight))


def ortho_kernel(inverse, *refs):
    lefts, out = refs[:-1], refs[-1]
    block = lefts[0].shape[1]
    me = lax.axis_index("col")
    parts = split(inverse[...], 3)
    for d, ref in enumerate(lefts):
        rows = pl.ds(pl.multiple_of(flip(me, d) * block, block), block)
        out[rows, :] = sum(dot(ref[...], x, ((0,), (1,))) for x in reversed(parts)).astype(bf16)


def ortho(inverse, lefts):
    r, block = lefts[0].shape
    return pl.pallas_call(
        ortho_kernel,
        out_shape=shape((block * len(lefts), r), bf16),
        in_specs=[VMEM] * (1 + len(lefts)),
        out_specs=VMEM,
        compiler_params=params(8),
        cost_estimate=cost(*[shape((block * len(lefts), r), bf16)] * 8),
        name="ortho",
    )(inverse, *lefts)


def hand_on(x, *earlier):
    return pl.pallas_call(
        lambda *refs: None,
        out_shape=shape(x.shape, x.dtype),
        in_specs=[ANY] * (1 + len(earlier)),
        out_specs=ANY,
        input_output_aliases={0: 0},
        compiler_params=params(1),
        name="hand_on",
    )(x, *earlier)


def block_ids(pairs):
    row = lax.axis_index("row")
    core = lax.bitwise_and(row, jnp.int32(1))
    chip = lax.div(row, jnp.int32(2))
    chips = lax.axis_size("row") // 2
    return [half * chips + flip(chip, d) for d in pairs for half in (core, 1 - core)]


def share_kernel(inverse, own, *refs):
    received, (out, squares) = refs[:-2], refs[-2:]
    total = own[...] + sum(ref[...].astype(f32) for ref in received)
    x_high, x_low = split(inverse[...], 2)
    high, low = split(total, 2)
    right = dot(x_high, low) + dot(x_low, high) + dot(x_high, high)
    out[...] = right.astype(bf16)
    r = out.shape[0]
    sums = jnp.sum(right * right, axis=1, keepdims=True)
    sums = jnp.transpose(jnp.broadcast_to(sums, (r, 128)))[: squares.shape[0], :]
    block_id = lax.broadcasted_iota(jnp.int32, squares.shape, 0)
    squares[...] = jnp.where(block_id == block_ids((0,))[0], sums, 0.0)


def share_of(inverse, own, received):
    r, width = own.shape
    rows = max(8, lax.axis_size("row"))
    return pl.pallas_call(
        share_kernel,
        out_shape=(shape((r, width), bf16), shape((rows, r), f32)),
        in_specs=[VMEM] * (2 + len(received)),
        out_specs=(VMEM, VMEM),
        compiler_params=params(8),
        name="share",
    )(inverse, own, *received)


def result_kernel(pairs, momentum_too, weight_too, factor, buf0, buf1, ortho_ref, weight, squares, *refs):
    blocks, rest = refs[: 2 * len(pairs)], refs[2 * len(pairs) :]
    *outs, token, mbuf, vbuf, nbuf, out_sems, basis_sems = rest
    new_momentum = outs[-1] if momentum_too else None
    new_weight, basis = outs[-2 - momentum_too : len(outs) - momentum_too] if weight_too else (None, None)
    r, width = blocks[0].shape
    tile = 256
    tiles = width // tile
    count = len(blocks)
    starts = [i * width for i in block_ids(pairs)]

    def store_basis(b):
        cols = pl.ds(pl.multiple_of(starts[b], 128), width)
        return pltpu.make_async_copy(nbuf.at[b % 2], basis.at[:, cols], basis_sems.at[b % 2])

    def place(b, t):
        return pl.ds(t * tile, tile), pl.ds(pl.multiple_of(starts[b] + t * tile, 128), tile)

    def stores(b, t):
        at, there = place(b, t)
        copies = []
        if momentum_too:
            copies.append((mbuf, new_momentum))
        if weight_too:
            copies.append((vbuf, new_weight))
        return [
            pltpu.make_async_copy(src.at[b % 2, :, at], dst.at[:, there], out_sems.at[k, b % 2, t])
            for k, (src, dst) in enumerate(copies)
        ]

    def finish(b):
        if weight_too:
            store_basis(b).wait()
        for t in range(tiles):
            for store in stores(b, t):
                store.wait()

    if weight_too:
        scale = lax.rsqrt(jnp.sum(squares[...], axis=0, keepdims=True) / FF + epsilon)
        scale = jnp.transpose(jnp.broadcast_to(scale, (128, r)))[:, :1]
    token[...] = jnp.zeros_like(token)
    depth = lax.axis_size("col")
    size = buf0.shape[0] // depth
    for b in range(count):
        k = b % 2
        if b >= 2:
            finish(b - 2)
        if weight_too:
            nbuf[k] = (blocks[b][...].astype(f32) * scale).astype(bf16)
            store_basis(b).start()
        for t in range(tiles):
            at, there = place(b, t)
            if momentum_too:
                correction = dot(ortho_ref[...], blocks[b][:, at])
                for j in range(2 * depth):
                    rows = slice(j * size, (j + 1) * size)
                    here = slice(j // 2 * size, (j // 2 + 1) * size)
                    old = (buf0, buf1)[j % 2][here, there]
                    mbuf[k, rows, at] = old - (1.0 - momentum_decay) * correction[rows]
            if weight_too:
                change = dot(ortho_ref[...], nbuf[k, :, at])
                vbuf[k, :, at] = (weight[:, there].astype(f32) - factor * change).astype(bf16)
            for store in stores(b, t):
                store.start()
    for b in range(count - 2, count):
        finish(b)


def results(pairs, kinds, factor, bufs, ortho_bf, weight, squares, blocks, outs=(), after=(), last=()):
    momentum_too, weight_too = kinds
    m, n = weight.shape
    r, width = blocks[0].shape
    outs = [*outs, *last]
    ins = [*map(keep, bufs), ortho_bf, keep(weight), squares, *blocks, *after, *map(stay, outs)]
    at = len(ins) - len(outs)
    skipped = 2 * weight_too + momentum_too - len(outs) if last else 0
    out_shape = []
    if weight_too:
        out_shape += [shape((m, n), bf16), shape((r, n), bf16)]
    if momentum_too:
        out_shape += [shape((m, n), f32)]
    m_rows, w_rows = (m if momentum_too else 8), (m if weight_too else 16)
    *outs, token = pl.pallas_call(
        functools.partial(result_kernel, pairs, *kinds, factor),
        out_shape=[*out_shape, shape((8, 128), f32)],
        in_specs=[VMEM] * (5 + len(blocks)) + [ANY] * (len(after) + len(outs)),
        out_specs=[ANY] * len(out_shape) + [VMEM],
        input_output_aliases={at + k: skipped + k for k in range(len(outs))},
        scratch_shapes=[
            pltpu.VMEM((2, m_rows, width), f32),
            pltpu.VMEM((2, w_rows, width), bf16),
            pltpu.VMEM((2, r, width), bf16),
            pltpu.SemaphoreType.DMA((2, 2, width // 256)),
            pltpu.SemaphoreType.DMA((2,)),
        ],
        compiler_params=params(12),
        cost_estimate=cost(*[shape((m, width), f32)] * (len(blocks) * (momentum_too + weight_too))),
        name="results",
    )(*ins)
    return outs, token


def sum_over(x, axis, least=1):
    d = least
    while d < lax.axis_size(axis):
        x = x + swap(x, axis, d)
        d *= 2
    return x


def exchange(x, axis, count, unit=1):
    return [x] + [swap(x, axis, unit * d) for d in range(1, count)]


def pair_up(terms):
    while len(terms) > 1:
        terms = [terms[2 * i] + terms[2 * i + 1] for i in range(len(terms) // 2)]
    return terms[0]


def gather(x, axis):
    blocks = [x]
    size = lax.axis_size(axis)
    for d in range(1, size):
        low = d & -d
        blocks.append(swap(blocks[d - low] if d != low else x, axis, low))
    return blocks


def per_device(weight, gradient, momentum, old_basis):
    depth, rows = lax.axis_size("col"), lax.axis_size("row")
    chips = rows // 2
    m, n = momentum.shape
    width = n // rows

    def sum_over_col(held, sent, *before):
        half = m // 2 // depth
        d = 1
        while held.shape[1] > half:
            held, sent = fold(held, swap(sent, "col", d), half)
            d *= 2
        return fold_last(held, swap(sent, "col", d), *before)

    buf0, kept, *outs = project(momentum, gradient, old_basis, depth, width, 0)
    low = sum_over_col(*outs)
    buf1, *outs = project(momentum, gradient, kept, depth, width, 1, (outs[1],))
    lefts = gather(sum_over_col(*outs, low), "col")
    bufs = (buf0, buf1)

    other, mine, g_sums = first_product(bufs, [lefts[d] for d in early(depth)], depth, width)
    lefts_late = [lefts[d] for d in late(depth)]
    g_mine, g_other = gram(lefts_late, g_sums)
    other = last_product(bufs, other, lefts_late, depth, width, False, g_mine)
    g_mine = g_mine + swap(g_other, "row", 1)
    other = hand_on(other, g_mine)
    received = swap(other, "row", 1)
    mine = last_product(bufs, mine, lefts_late, depth, width, True, g_mine, other)
    own, *sent = pair_sum(mine, received, chips, g_mine)
    g_mine = pair_up(exchange(g_mine, "row", chips, 2))
    got = [swap(x, "row", 2 * (d + 1)) for d, x in enumerate(sent)]
    inverse, weight = chol_inverse(g_mine, swap(g_mine, "row", 1), weight)

    share, squares = share_of(inverse, own, got)
    ortho_bf = ortho(inverse, lefts)

    near = [d for d in range(chips) if d & (d - 1) == 0]
    blocks = {d: swap(share, "row", 2 * d) for d in near[1:]}
    own_pair = swap(share, "row", 1)
    factor = step_rate * math.sqrt(D / RANK)
    common = (factor, bufs, ortho_bf, weight)
    squares = exchange(hand_on(squares, own_pair), "col", depth)
    (momentum,), token = results((0,), (True, False), *common, squares[0], (share, own_pair))
    squares = hand_on(pair_up(squares), *blocks.values(), token)
    squares = pair_up(exchange(squares, "row", chips, 2))
    pairs = {}
    for d in near[1:]:
        block = hand_on(blocks[d], squares)
        pairs[d] = (block, swap(block, "row", 1))
    squares = squares + swap(squares, "row", 1)
    share = hand_on(share, *[pair[0] for pair in pairs.values()])
    pairs[0] = (share, own_pair)
    far = [d for d in range(chips) if d not in near]
    blocks = {d: swap(share, "row", 2 * d) for d in far}

    common = (*common, squares)
    weight_basis = ()
    if near[1:]:
        rest = [x for d in near[1:] for x in pairs[d]]
        (*weight_basis, momentum), token = results(
            tuple(near[1:]), (True, True), *common, rest, (), (share,), [momentum]
        )
    blocks = {d: hand_on(block, token) for d, block in blocks.items()}
    weight_basis, token = results((0,), (False, True), *common, pairs[0], weight_basis)
    outs = [*weight_basis, momentum]
    for d, block in blocks.items():
        outs, token = results((d,), (True, True), *common, (block, swap(block, "row", 1)), outs)
    new_weight, new_basis, new_momentum = outs
    return (new_weight, new_momentum, new_basis)


def plain_per_device(weight, gradient, momentum, old_basis):
    buffer = momentum + gradient.astype(f32)
    buffer_low = buffer.astype(bf16)
    left_factor = lax.psum(dot(buffer_low, old_basis, ((1,), (1,))), "col")
    gram_share = lax.dot_general(
        left_factor,
        left_factor,
        (((0,), (0,)), ((), ())),
        precision=lax.Precision.HIGHEST,
        preferred_element_type=f32,
    )
    chol_factor = jnp.linalg.cholesky(lax.psum(gram_share, "row"))
    orthonormal = lax.linalg.triangular_solve(
        chol_factor, left_factor, left_side=False, lower=True, transpose_a=True
    ).astype(bf16)
    right_share = lax.psum_scatter(
        dot(orthonormal, buffer_low, ((0,), (0,))), "row", scatter_dimension=0, tiled=True
    )
    sum_squares = lax.psum(jnp.sum(right_share * right_share, axis=1), "col")
    scale_share = jnp.sqrt(sum_squares / FF + epsilon)
    basis_share = (right_share / scale_share[:, None]).astype(bf16)
    new_basis = lax.all_gather(basis_share, "row", axis=0, tiled=True)
    col_scale = lax.all_gather(scale_share, "row", axis=0, tiled=True)
    scaled = (orthonormal.astype(f32) * col_scale[None, :]).astype(bf16)
    new_momentum = buffer - (1.0 - momentum_decay) * dot(scaled, new_basis)
    factor = step_rate * math.sqrt(D / RANK)
    new_weight = (weight.astype(f32) - factor * dot(orthonormal, new_basis)).astype(bf16)
    return (new_weight, new_momentum, new_basis)


def power_of_two(k):
    return k > 1 and k & (k - 1) == 0


def solution(mesh):
    rows, depth = mesh.shape["row"], mesh.shape["col"]
    tiled = (
        power_of_two(rows // 2)
        and power_of_two(depth)
        and depth > 2
        and D % (rows * depth * 128) == 0
        and FF % (rows * depth * 256) == 0
    )
    return jax.shard_map(
        per_device if tiled else plain_per_device,
        mesh=mesh,
        in_specs=(P("row", "col"), P("row", "col"), P("row", "col"), P(None, "col")),
        out_specs=(P("row", "col"), P("row", "col"), P(None, "col")),
        check_vma=False,
    )
```

```python
import functools
import math

import jax
import jax.numpy as jnp
from jax import lax
from jax.experimental import pallas as pl
from jax.experimental.pallas import tpu as pltpu
from jax.sharding import PartitionSpec as P

D = 8192
FF = 24576
RANK = 256

epsilon = 1e-06
momentum_decay = 0.6
step_rate = 0.5

bf16, f32 = jnp.bfloat16, jnp.float32
VMEM = pl.BlockSpec(memory_space=pltpu.VMEM)
ANY = pl.BlockSpec(memory_space=pl.ANY)
MIB = 1 << 20


def shape(dims, kind):
    return jax.ShapeDtypeStruct(dims, kind)


def params(mib):
    return pltpu.CompilerParams(vmem_limit_bytes=mib * MIB)


def dot(a, b, dims=((1,), (0,))):
    return lax.dot_general(a, b, (dims, ((), ())), preferred_element_type=f32)


def split(x, terms):
    parts = []
    for _ in range(terms):
        part = x.astype(bf16)
        parts.append(part)
        x = x - part.astype(f32)
    return parts


def flip(i, d):
    return lax.bitwise_xor(i, jnp.int32(d))


def swap(x, axis, d):
    return lax.ppermute(x, axis, [(i, i ^ d) for i in range(lax.axis_size(axis))])


def project_kernel(part, depth, width, mom, grad, basis, *rest):
    if part == 0:
        (buf, kept), rest = rest[:2], rest[2:]
    else:
        kept, buf, rest = basis, rest[1], rest[2:]
    held, sent, gbuf, total, sems, basis_sem = rest
    m, n = buf.shape
    half = m // depth

    def copies(c):
        cols = pl.ds(pl.multiple_of(c * width, 128), width)
        pairs = []
        for k in range(depth):
            there = pl.ds((2 * k + part) * half, half)
            here = pl.ds(k * half, half)
            pairs.append(pltpu.make_async_copy(mom.at[there, cols], buf.at[here, cols], sems.at[0, k, c]))
            pairs.append(pltpu.make_async_copy(grad.at[there, cols], gbuf.at[here, cols], sems.at[1, k, c]))
        if part == 0:
            pairs.append(pltpu.make_async_copy(basis.at[:, cols], kept.at[:, cols], basis_sem.at[c]))
        return pairs

    def start(c, carry):
        for copy in copies(c):
            copy.start()
        return carry

    def step(c, carry):
        for copy in copies(c):
            copy.wait()
        cols = pl.ds(pl.multiple_of(c * width, 128), width)
        added = buf[:, cols] + gbuf[:, cols].astype(f32)
        buf[:, cols] = added
        total[...] += dot(added.astype(bf16), kept[:, cols], ((1,), (1,)))
        return carry

    total[...] = jnp.zeros_like(total)
    lax.fori_loop(0, n // width, start, 0)
    lax.fori_loop(0, n // width, step, 0)
    me = lax.axis_index("col")
    for out, odd in ((held, 0), (sent, 1)):
        for j in range(depth // 2):
            rows = pl.ds(pl.multiple_of(flip(me, 2 * j + odd) * half, half), half)
            out[:, j * half : (j + 1) * half] = jnp.transpose(total[rows, :]).astype(out.dtype)


def project(momentum, gradient, basis, depth, width, part, after=()):
    m, n = momentum.shape
    m = m // 2
    r = basis.shape[0]
    kept = [] if part else [pltpu.VMEM((r, n), bf16)]
    return pl.pallas_call(
        functools.partial(project_kernel, part, depth, width),
        out_shape=(pltpu.VMEM((m, n), f32), *kept, shape((r, m // 2), f32), shape((r, m // 2), bf16)),
        in_specs=[ANY, ANY] + [VMEM if part else ANY] + [ANY] * len(after),
        out_specs=(VMEM,) * (3 + len(kept)),
        scratch_shapes=[
            pltpu.VMEM((m, n), bf16),
            pltpu.VMEM((m, r), f32),
            pltpu.SemaphoreType.DMA((2, depth, n // width)),
            pltpu.SemaphoreType.DMA((n // width,)),
        ],
        compiler_params=params(14),
        cost_estimate=cost(momentum, gradient),
        name="project",
    )(stay(momentum), stay(gradient), keep(basis) if part else stay(basis), *after)


def fold_kernel(half, held, received, held_out, sent_out):
    added = held[...] + received[...].astype(f32)
    for j in range(held_out.shape[1] // half):
        at = slice(j * half, (j + 1) * half)
        held_out[:, at] = added[:, 2 * j * half : (2 * j + 1) * half]
        sent_out[:, at] = added[:, (2 * j + 1) * half : (2 * j + 2) * half].astype(bf16)


def fold(held, received, half):
    r, size = held.shape
    return pl.pallas_call(
        functools.partial(fold_kernel, half),
        out_shape=(shape((r, size // 2), f32), shape((r, size // 2), bf16)),
        in_specs=[VMEM, VMEM],
        out_specs=(VMEM, VMEM),
        compiler_params=params(8),
        name="fold",
    )(held, received)


def fold_last_kernel(held, received, *rest):
    before, out = rest[:-1], rest[-1]
    half = held.shape[1]
    for k, ref in enumerate(before):
        out[:, k * half : (k + 1) * half] = ref[...]
    out[:, len(before) * half :] = (held[...] + received[...].astype(f32)).astype(bf16)


def fold_last(held, received, *before):
    r, half = held.shape
    return pl.pallas_call(
        fold_last_kernel,
        out_shape=shape((r, half * (1 + len(before))), bf16),
        in_specs=[VMEM] * (2 + len(before)),
        out_specs=VMEM,
        compiler_params=params(8),
        name="fold_last",
    )(held, received, *before)


def cost(*arrays):
    size = sum(math.prod(x.shape) * x.dtype.itemsize for x in arrays)
    return pl.CostEstimate(flops=0, bytes_accessed=size, transcendentals=0)


def keep(x):
    return pltpu.with_memory_space_constraint(x, pltpu.VMEM)


def stay(x):
    return pltpu.with_memory_space_constraint(x, pltpu.HBM)


def buffer_rows(bufs, ds, depth, cols):
    half = bufs[0].shape[0] // depth
    me = lax.axis_index("col")
    rows = [pl.ds(pl.multiple_of(flip(me, d) * half, half), half) for d in ds]
    return jnp.concatenate([buf[at, cols].astype(bf16) for at in rows for buf in bufs], axis=0)


def early(depth):
    return (0, depth // 2)


def late(depth):
    return tuple(d for d in range(depth) if d not in early(depth))


def first_kernel(depth, width, buf0, buf1, *rest):
    lefts, (other, mine, gram, whole) = rest[:-4], rest[-4:]
    core = lax.bitwise_and(lax.axis_index("row"), jnp.int32(1))
    size = other.shape[1]
    block = lefts[0].shape[1]
    for d, ref in enumerate(lefts):
        whole[:, d * block : (d + 1) * block] = ref[...]
    gram[...] = dot(whole[...], whole[...], ((1,), (1,)))
    for out, half in ((other, 1 - core), (mine, core)):

        def step(k, carry, out=out, half=half):
            cols = pl.ds(pl.multiple_of(half * size + k * width, 128), width)
            b = buffer_rows((buf0, buf1), early(depth), depth, cols)
            out[:, pl.ds(pl.multiple_of(k * width, 128), width)] = dot(whole[...], b)
            return carry

        lax.fori_loop(0, size // width, step, 0)


def first_product(bufs, lefts, depth, width):
    m, n = bufs[0].shape
    r, block = lefts[0].shape
    return pl.pallas_call(
        functools.partial(first_kernel, depth, width),
        out_shape=(shape((r, n // 2), f32), shape((r, n // 2), f32), shape((r, r), f32)),
        in_specs=[VMEM] * (2 + len(lefts)),
        out_specs=[VMEM] * 3,
        scratch_shapes=[pltpu.VMEM((r, block * len(lefts)), bf16)],
        compiler_params=params(10),
        cost_estimate=cost(*bufs, shape((r, n), f32)),
        name="first_product",
    )(*map(keep, bufs), *lefts)


def gram_kernel(sums, *rest):
    lefts, (g_mine, g_other, total) = rest[:-3], rest[-3:]
    core = lax.bitwise_and(lax.axis_index("row"), jnp.int32(1))
    total[...] = sums[...] + sum(dot(ref[...], ref[...], ((1,), (1,))) for ref in lefts)
    h = g_mine.shape[0]
    g_mine[...] = total[pl.ds(pl.multiple_of(core * h, h), h), :]
    g_other[...] = total[pl.ds(pl.multiple_of((1 - core) * h, h), h), :]


def gram(lefts, sums):
    r = lefts[0].shape[0]
    return pl.pallas_call(
        gram_kernel,
        out_shape=[shape((r // 2, r), f32)] * 2,
        in_specs=[VMEM] * (1 + len(lefts)),
        out_specs=[VMEM] * 2,
        scratch_shapes=[pltpu.VMEM((r, r), f32)],
        compiler_params=params(8),
        name="gram",
    )(sums, *lefts)


def last_kernel(depth, width, mine, buf0, buf1, sums, *rest):
    lefts, (*_, out, whole) = rest[: len(late(depth))], rest[len(late(depth)) :]
    core = lax.bitwise_and(lax.axis_index("row"), jnp.int32(1))
    half = core if mine else 1 - core
    size = out.shape[1]
    block = lefts[0].shape[1]
    for k, ref in enumerate(lefts):
        whole[:, k * block : (k + 1) * block] = ref[...]

    def step(k, carry):
        cols = pl.ds(pl.multiple_of(half * size + k * width, 128), width)
        at = pl.ds(pl.multiple_of(k * width, 128), width)
        b = buffer_rows((buf0, buf1), late(depth), depth, cols)
        out[:, at] = (sums[:, at] + dot(whole[...], b)).astype(out.dtype)
        return carry

    lax.fori_loop(0, size // width, step, 0)


def last_product(bufs, sums, lefts, depth, width, mine, *after):
    r, block = lefts[0].shape
    return pl.pallas_call(
        functools.partial(last_kernel, depth, width, mine),
        out_shape=shape(sums.shape, f32 if mine else bf16),
        in_specs=[VMEM] * (3 + len(lefts)) + [ANY] * len(after),
        out_specs=VMEM,
        scratch_shapes=[pltpu.VMEM((r, block * len(lefts)), bf16)],
        compiler_params=params(8),
        cost_estimate=cost(*bufs[:1], sums),
        name="mine_product" if mine else "other_product",
    )(*map(keep, bufs), sums, *lefts, *after)


def pair_sum_kernel(chips, mine, received, _, *outs):
    me = lax.div(lax.axis_index("row"), jnp.int32(2))
    width = outs[0].shape[1]
    for d in range(chips):
        cols = pl.ds(pl.multiple_of(flip(me, d) * width, 128), width)
        outs[d][...] = (mine[:, cols] + received[:, cols].astype(f32)).astype(outs[d].dtype)


def pair_sum(mine, received, chips, after):
    r, n = mine.shape
    kinds = [f32] + [bf16] * (chips - 1)
    return pl.pallas_call(
        functools.partial(pair_sum_kernel, chips),
        out_shape=[shape((r, n // chips), k) for k in kinds],
        in_specs=[VMEM, VMEM, ANY],
        out_specs=[VMEM] * chips,
        compiler_params=params(8),
        name="pair_sum",
    )(mine, received, after)


def eliminate(tiles, at, nb, group):
    sub = lax.broadcasted_iota(jnp.int32, (nb, 128), 0)
    scale = jnp.zeros((nb, 128), f32)
    for g in range(0, nb, group):
        cols = [
            jnp.broadcast_to(tiles[0][:, at + g + j : at + g + j + 1], (nb, 128)) for j in range(group)
        ]
        for j in range(group):
            t = g + j
            pivot = cols[j][t : t + 1, :]
            factor = jnp.where(sub > t, cols[j], 0.0) * (1.0 / pivot)
            scale = jnp.where(sub == t, lax.rsqrt(pivot), scale)
            for l in range(j + 1, group):
                cols[l] = cols[l] - factor * cols[l][t : t + 1, :]
            tiles = [x - factor * x[t : t + 1, :] for x in tiles]
    return [x * scale for x in tiles]


def chol_inverse_kernel(mine, other, weight, out, fetched, work, sem):
    piece = weight.shape[0] // sem.shape[0]
    fetches = [
        pltpu.make_async_copy(weight.at[pl.ds(k * piece, piece), :], fetched.at[pl.ds(k * piece, piece), :], sem.at[k])
        for k in range(sem.shape[0])
    ]
    for fetch in fetches:
        fetch.start()
    n = out.shape[0]
    h = n // 2
    core = lax.bitwise_and(lax.axis_index("row"), jnp.int32(1))
    work[pl.ds(pl.multiple_of(core * h, h), h), :n] = mine[...]
    work[pl.ds(pl.multiple_of((1 - core) * h, h), h), :n] = other[...]
    r_id = lax.broadcasted_iota(jnp.int32, (n, n), 0)
    c_id = lax.broadcasted_iota(jnp.int32, (n, n), 1)
    work[:, n:] = jnp.where(r_id == c_id, 1.0, 0.0).astype(f32)
    nb = 32
    for p in range(n // nb):
        lo = p * nb
        left = (lo // 128) * 128
        right = n + ((lo + nb + 127) // 128) * 128
        tiles = [work[lo : lo + nb, c : c + 128] for c in range(left, right, 128)]
        s = jnp.concatenate(eliminate(tiles, lo - left, nb, 8), axis=1)
        work[lo : lo + nb, left:right] = s
        if lo + nb < n:
            lead = s[:, lo + nb - left : n - left]
            work[lo + nb :, left:right] -= lax.dot_general(
                lead, s, (((0,), (0,)), ((), ())), precision=lax.Precision.HIGHEST, preferred_element_type=f32
            )
    out[...] = jnp.where(r_id >= c_id, work[:, n:], 0.0)
    for fetch in fetches:
        fetch.wait()


def chol_inverse(mine, other, weight):
    n = mine.shape[1]
    return pl.pallas_call(
        chol_inverse_kernel,
        out_shape=(shape((n, n), f32), pltpu.VMEM(weight.shape, weight.dtype)),
        in_specs=[VMEM, VMEM, ANY],
        out_specs=(VMEM, VMEM),
        scratch_shapes=[pltpu.VMEM((n, 2 * n), f32), pltpu.SemaphoreType.DMA((8,))],
        compiler_params=params(8),
        cost_estimate=cost(*[mine] * 256),
        name="chol_inverse",
    )(mine, other, stay(weight))


def ortho_kernel(inverse, *refs):
    lefts, out = refs[:-1], refs[-1]
    block = lefts[0].shape[1]
    me = lax.axis_index("col")
    parts = split(inverse[...], 3)
    for d, ref in enumerate(lefts):
        rows = pl.ds(pl.multiple_of(flip(me, d) * block, block), block)
        out[rows, :] = sum(dot(ref[...], x, ((0,), (1,))) for x in reversed(parts)).astype(bf16)


def ortho(inverse, lefts):
    r, block = lefts[0].shape
    return pl.pallas_call(
        ortho_kernel,
        out_shape=shape((block * len(lefts), r), bf16),
        in_specs=[VMEM] * (1 + len(lefts)),
        out_specs=VMEM,
        compiler_params=params(8),
        cost_estimate=cost(*[shape((block * len(lefts), r), bf16)] * 8),
        name="ortho",
    )(inverse, *lefts)


def hand_on(x, *earlier):
    return pl.pallas_call(
        lambda *refs: None,
        out_shape=shape(x.shape, x.dtype),
        in_specs=[ANY] * (1 + len(earlier)),
        out_specs=ANY,
        input_output_aliases={0: 0},
        compiler_params=params(1),
        name="hand_on",
    )(x, *earlier)


def block_ids(pairs):
    row = lax.axis_index("row")
    core = lax.bitwise_and(row, jnp.int32(1))
    chip = lax.div(row, jnp.int32(2))
    chips = lax.axis_size("row") // 2
    return [half * chips + flip(chip, d) for d in pairs for half in (core, 1 - core)]


def share_kernel(inverse, own, *refs):
    received, (out, squares) = refs[:-2], refs[-2:]
    total = own[...] + sum(ref[...].astype(f32) for ref in received)
    x_high, x_low = split(inverse[...], 2)
    high, low = split(total, 2)
    right = dot(x_high, low) + dot(x_low, high) + dot(x_high, high)
    out[...] = right.astype(bf16)
    r = out.shape[0]
    sums = jnp.sum(right * right, axis=1, keepdims=True)
    sums = jnp.transpose(jnp.broadcast_to(sums, (r, 128)))[: squares.shape[0], :]
    block_id = lax.broadcasted_iota(jnp.int32, squares.shape, 0)
    squares[...] = jnp.where(block_id == block_ids((0,))[0], sums, 0.0)


def share_of(inverse, own, received):
    r, width = own.shape
    rows = max(8, lax.axis_size("row"))
    return pl.pallas_call(
        share_kernel,
        out_shape=(shape((r, width), bf16), shape((rows, r), f32)),
        in_specs=[VMEM] * (2 + len(received)),
        out_specs=(VMEM, VMEM),
        compiler_params=params(8),
        name="share",
    )(inverse, own, *received)


def result_kernel(pairs, momentum_too, weight_too, factor, buf0, buf1, ortho_ref, weight, squares, *refs):
    blocks, rest = refs[: 2 * len(pairs)], refs[2 * len(pairs) :]
    *outs, token, mbuf, vbuf, nbuf, out_sems, basis_sems = rest
    new_momentum = outs[-1] if momentum_too else None
    new_weight, basis = outs[-2 - momentum_too : len(outs) - momentum_too] if weight_too else (None, None)
    r, width = blocks[0].shape
    tile = 256
    tiles = width // tile
    count = len(blocks)
    starts = [i * width for i in block_ids(pairs)]

    def store_basis(b):
        cols = pl.ds(pl.multiple_of(starts[b], 128), width)
        return pltpu.make_async_copy(nbuf.at[b % 2], basis.at[:, cols], basis_sems.at[b % 2])

    def place(b, t):
        return pl.ds(t * tile, tile), pl.ds(pl.multiple_of(starts[b] + t * tile, 128), tile)

    def stores(b, t):
        at, there = place(b, t)
        copies = []
        if momentum_too:
            copies.append((mbuf, new_momentum))
        if weight_too:
            copies.append((vbuf, new_weight))
        pieces = out_sems.shape[3]
        piece = ortho_ref.shape[0] // pieces
        return [
            pltpu.make_async_copy(
                src.at[b % 2, pl.ds(i * piece, piece), at],
                dst.at[pl.ds(i * piece, piece), there],
                out_sems.at[k, b % 2, t, i],
            )
            for k, (src, dst) in enumerate(copies)
            for i in range(pieces)
        ]

    def finish(b):
        if weight_too:
            store_basis(b).wait()
        for t in range(tiles):
            for store in stores(b, t):
                store.wait()

    if weight_too:
        scale = lax.rsqrt(jnp.sum(squares[...], axis=0, keepdims=True) / FF + epsilon)
        scale = jnp.transpose(jnp.broadcast_to(scale, (128, r)))[:, :1]
    token[...] = jnp.zeros_like(token)
    depth = lax.axis_size("col")
    size = buf0.shape[0] // depth
    for b in range(count):
        k = b % 2
        if b >= 2:
            finish(b - 2)
        if weight_too:
            nbuf[k] = (blocks[b][...].astype(f32) * scale).astype(bf16)
            store_basis(b).start()
        for t in range(tiles):
            at, there = place(b, t)
            if momentum_too:
                correction = dot(ortho_ref[...], blocks[b][:, at])
                for j in range(2 * depth):
                    rows = slice(j * size, (j + 1) * size)
                    here = slice(j // 2 * size, (j // 2 + 1) * size)
                    old = (buf0, buf1)[j % 2][here, there]
                    mbuf[k, rows, at] = old - (1.0 - momentum_decay) * correction[rows]
            if weight_too:
                change = dot(ortho_ref[...], nbuf[k, :, at])
                vbuf[k, :, at] = (weight[:, there].astype(f32) - factor * change).astype(bf16)
            for store in stores(b, t):
                store.start()
    for b in range(count - 2, count):
        finish(b)


def results(pairs, kinds, factor, bufs, ortho_bf, weight, squares, blocks, outs=(), after=(), last=()):
    momentum_too, weight_too = kinds
    m, n = weight.shape
    r, width = blocks[0].shape
    outs = [*outs, *last]
    ins = [*map(keep, bufs), ortho_bf, keep(weight), squares, *blocks, *after, *map(stay, outs)]
    at = len(ins) - len(outs)
    skipped = 2 * weight_too + momentum_too - len(outs) if last else 0
    out_shape = []
    if weight_too:
        out_shape += [shape((m, n), bf16), shape((r, n), bf16)]
    if momentum_too:
        out_shape += [shape((m, n), f32)]
    m_rows, w_rows = (m if momentum_too else 8), (m if weight_too else 16)
    *outs, token = pl.pallas_call(
        functools.partial(result_kernel, pairs, *kinds, factor),
        out_shape=[*out_shape, shape((8, 128), f32)],
        in_specs=[VMEM] * (5 + len(blocks)) + [ANY] * (len(after) + len(outs)),
        out_specs=[ANY] * len(out_shape) + [VMEM],
        input_output_aliases={at + k: skipped + k for k in range(len(outs))},
        scratch_shapes=[
            pltpu.VMEM((2, m_rows, width), f32),
            pltpu.VMEM((2, w_rows, width), bf16),
            pltpu.VMEM((2, r, width), bf16),
            pltpu.SemaphoreType.DMA((2, 2, width // 256, 4)),
            pltpu.SemaphoreType.DMA((2,)),
        ],
        compiler_params=params(12),
        cost_estimate=cost(*[shape((m, width), f32)] * (len(blocks) * (momentum_too + weight_too))),
        name="results",
    )(*ins)
    return outs, token


def sum_over(x, axis, least=1):
    d = least
    while d < lax.axis_size(axis):
        x = x + swap(x, axis, d)
        d *= 2
    return x


def exchange(x, axis, count, unit=1):
    return [x] + [swap(x, axis, unit * d) for d in range(1, count)]


def pair_up(terms):
    while len(terms) > 1:
        terms = [terms[2 * i] + terms[2 * i + 1] for i in range(len(terms) // 2)]
    return terms[0]


def gather(x, axis):
    blocks = [x]
    size = lax.axis_size(axis)
    for d in range(1, size):
        low = d & -d
        blocks.append(swap(blocks[d - low] if d != low else x, axis, low))
    return blocks


def per_device(weight, gradient, momentum, old_basis):
    depth, rows = lax.axis_size("col"), lax.axis_size("row")
    chips = rows // 2
    m, n = momentum.shape
    width = n // rows

    def sum_over_col(held, sent, *before):
        half = m // 2 // depth
        d = 1
        while held.shape[1] > half:
            held, sent = fold(held, swap(sent, "col", d), half)
            d *= 2
        return fold_last(held, swap(sent, "col", d), *before)

    buf0, kept, *outs = project(momentum, gradient, old_basis, depth, width, 0)
    low = sum_over_col(*outs)
    buf1, *outs = project(momentum, gradient, kept, depth, width, 1, (outs[1],))
    lefts = gather(sum_over_col(*outs, low), "col")
    bufs = (buf0, buf1)

    other, mine, g_sums = first_product(bufs, [lefts[d] for d in early(depth)], depth, width)
    lefts_late = [lefts[d] for d in late(depth)]
    g_mine, g_other = gram(lefts_late, g_sums)
    other = last_product(bufs, other, lefts_late, depth, width, False, g_mine)
    g_mine = g_mine + swap(g_other, "row", 1)
    other = hand_on(other, g_mine)
    received = swap(other, "row", 1)
    mine = last_product(bufs, mine, lefts_late, depth, width, True, g_mine, other)
    own, *sent = pair_sum(mine, received, chips, g_mine)
    g_mine = pair_up(exchange(g_mine, "row", chips, 2))
    got = [swap(x, "row", 2 * (d + 1)) for d, x in enumerate(sent)]
    inverse, weight = chol_inverse(g_mine, swap(g_mine, "row", 1), weight)

    share, squares = share_of(inverse, own, got)
    ortho_bf = ortho(inverse, lefts)

    near = [d for d in range(chips) if d & (d - 1) == 0]
    blocks = {d: swap(share, "row", 2 * d) for d in near[1:]}
    own_pair = swap(share, "row", 1)
    factor = step_rate * math.sqrt(D / RANK)
    common = (factor, bufs, ortho_bf, weight)
    squares = exchange(hand_on(squares, own_pair), "col", depth)
    (momentum,), token = results((0,), (True, False), *common, squares[0], (share, own_pair))
    squares = pair_up(squares)
    squares = squares + swap(squares, "row", 1)
    squares = hand_on(squares, *blocks.values(), token)
    squares = pair_up(exchange(squares, "row", chips, 2))
    pairs = {}
    for d in near[1:]:
        block = hand_on(blocks[d], squares)
        pairs[d] = (block, swap(block, "row", 1))
    pairs[0] = (share, own_pair)
    h = share.shape[0] // 2
    blocks = {d: pairs[d][0] for d in near}
    halves = {}
    for d in range(chips):
        if d not in near:
            least, most = d & -d, 1 << (d.bit_length() - 1)
            top = swap(blocks[d ^ most][:h], "row", 2 * most)
            bottom = swap(blocks[d ^ least][h:], "row", 2 * least)
            halves[d] = top, bottom
            blocks[d] = jnp.concatenate([top, bottom], axis=0)

    common = (*common, squares)
    weight_basis = ()
    if near[1:]:
        rest = [x for d in near[1:] for x in pairs[d]]
        (*weight_basis, momentum), token = results(
            tuple(near[1:]), (True, True), *common, rest, (), (), [momentum]
        )
    blocks = {d: jnp.concatenate([hand_on(top, token), bottom], axis=0) for d, (top, bottom) in halves.items()}
    weight_basis, token = results((0,), (False, True), *common, pairs[0], weight_basis)
    outs = [*weight_basis, momentum]
    for d, block in blocks.items():
        outs, token = results((d,), (True, True), *common, (block, swap(block, "row", 1)), outs)
    new_weight, new_basis, new_momentum = outs
    return (new_weight, new_momentum, new_basis)


def plain_per_device(weight, gradient, momentum, old_basis):
    buffer = momentum + gradient.astype(f32)
    buffer_low = buffer.astype(bf16)
    left_factor = lax.psum(dot(buffer_low, old_basis, ((1,), (1,))), "col")
    gram_share = lax.dot_general(
        left_factor,
        left_factor,
        (((0,), (0,)), ((), ())),
        precision=lax.Precision.HIGHEST,
        preferred_element_type=f32,
    )
    chol_factor = jnp.linalg.cholesky(lax.psum(gram_share, "row"))
    orthonormal = lax.linalg.triangular_solve(
        chol_factor, left_factor, left_side=False, lower=True, transpose_a=True
    ).astype(bf16)
    right_share = lax.psum_scatter(
        dot(orthonormal, buffer_low, ((0,), (0,))), "row", scatter_dimension=0, tiled=True
    )
    sum_squares = lax.psum(jnp.sum(right_share * right_share, axis=1), "col")
    scale_share = jnp.sqrt(sum_squares / FF + epsilon)
    basis_share = (right_share / scale_share[:, None]).astype(bf16)
    new_basis = lax.all_gather(basis_share, "row", axis=0, tiled=True)
    col_scale = lax.all_gather(scale_share, "row", axis=0, tiled=True)
    scaled = (orthonormal.astype(f32) * col_scale[None, :]).astype(bf16)
    new_momentum = buffer - (1.0 - momentum_decay) * dot(scaled, new_basis)
    factor = step_rate * math.sqrt(D / RANK)
    new_weight = (weight.astype(f32) - factor * dot(orthonormal, new_basis)).astype(bf16)
    return (new_weight, new_momentum, new_basis)


def power_of_two(k):
    return k > 1 and k & (k - 1) == 0


def solution(mesh):
    rows, depth = mesh.shape["row"], mesh.shape["col"]
    tiled = (
        power_of_two(rows // 2)
        and power_of_two(depth)
        and depth > 2
        and D % (rows * depth * 128) == 0
        and FF % (rows * depth * 256) == 0
    )
    return jax.shard_map(
        per_device if tiled else plain_per_device,
        mesh=mesh,
        in_specs=(P("row", "col"), P("row", "col"), P("row", "col"), P(None, "col")),
        out_specs=(P("row", "col"), P("row", "col"), P(None, "col")),
        check_vma=False,
    )
```

```python
import functools
import math

import jax
import jax.numpy as jnp
from jax import lax
from jax.experimental import pallas as pl
from jax.experimental.pallas import tpu as pltpu
from jax.sharding import PartitionSpec as P

D = 8192
FF = 24576
RANK = 256

epsilon = 1e-06
momentum_decay = 0.6
step_rate = 0.5

bf16, f32 = jnp.bfloat16, jnp.float32
VMEM = pl.BlockSpec(memory_space=pltpu.VMEM)
ANY = pl.BlockSpec(memory_space=pl.ANY)
MIB = 1 << 20


def shape(dims, kind):
    return jax.ShapeDtypeStruct(dims, kind)


def params(mib):
    return pltpu.CompilerParams(vmem_limit_bytes=mib * MIB)


def dot(a, b, dims=((1,), (0,))):
    return lax.dot_general(a, b, (dims, ((), ())), preferred_element_type=f32)


def split(x, terms):
    parts = []
    for _ in range(terms):
        part = x.astype(bf16)
        parts.append(part)
        x = x - part.astype(f32)
    return parts


def flip(i, d):
    return lax.bitwise_xor(i, jnp.int32(d))


def swap(x, axis, d):
    return lax.ppermute(x, axis, [(i, i ^ d) for i in range(lax.axis_size(axis))])


def project_kernel(part, depth, width, mom, grad, basis, *rest):
    if part == 0:
        (buf, kept), rest = rest[:2], rest[2:]
    else:
        kept, buf, rest = basis, rest[1], rest[2:]
    held, sent, gbuf, total, sems, basis_sem = rest
    m, n = buf.shape
    half = m // depth

    def copies(c):
        cols = pl.ds(pl.multiple_of(c * width, 128), width)
        pairs = []
        for k in range(depth):
            there = pl.ds((2 * k + part) * half, half)
            here = pl.ds(k * half, half)
            pairs.append(pltpu.make_async_copy(mom.at[there, cols], buf.at[here, cols], sems.at[0, k, c]))
            pairs.append(pltpu.make_async_copy(grad.at[there, cols], gbuf.at[here, cols], sems.at[1, k, c]))
        if part == 0:
            pairs.append(pltpu.make_async_copy(basis.at[:, cols], kept.at[:, cols], basis_sem.at[c]))
        return pairs

    def start(c, carry):
        for copy in copies(c):
            copy.start()
        return carry

    def step(c, carry):
        for copy in copies(c):
            copy.wait()
        cols = pl.ds(pl.multiple_of(c * width, 128), width)
        added = buf[:, cols] + gbuf[:, cols].astype(f32)
        buf[:, cols] = added
        total[...] += dot(added.astype(bf16), kept[:, cols], ((1,), (1,)))
        return carry

    total[...] = jnp.zeros_like(total)
    lax.fori_loop(0, n // width, start, 0)
    lax.fori_loop(0, n // width, step, 0)
    me = lax.axis_index("col")
    for out, odd in ((held, 0), (sent, 1)):
        for j in range(depth // 2):
            rows = pl.ds(pl.multiple_of(flip(me, 2 * j + odd) * half, half), half)
            out[:, j * half : (j + 1) * half] = jnp.transpose(total[rows, :]).astype(out.dtype)


def project(momentum, gradient, basis, depth, width, part, after=()):
    m, n = momentum.shape
    m = m // 2
    r = basis.shape[0]
    kept = [] if part else [pltpu.VMEM((r, n), bf16)]
    return pl.pallas_call(
        functools.partial(project_kernel, part, depth, width),
        out_shape=(pltpu.VMEM((m, n), f32), *kept, shape((r, m // 2), f32), shape((r, m // 2), bf16)),
        in_specs=[ANY, ANY] + [VMEM if part else ANY] + [ANY] * len(after),
        out_specs=(VMEM,) * (3 + len(kept)),
        scratch_shapes=[
            pltpu.VMEM((m, n), bf16),
            pltpu.VMEM((m, r), f32),
            pltpu.SemaphoreType.DMA((2, depth, n // width)),
            pltpu.SemaphoreType.DMA((n // width,)),
        ],
        compiler_params=params(14),
        cost_estimate=cost(momentum, gradient),
        name="project",
    )(stay(momentum), stay(gradient), keep(basis) if part else stay(basis), *after)


def fold_kernel(half, held, received, held_out, sent_out):
    added = held[...] + received[...].astype(f32)
    for j in range(held_out.shape[1] // half):
        at = slice(j * half, (j + 1) * half)
        held_out[:, at] = added[:, 2 * j * half : (2 * j + 1) * half]
        sent_out[:, at] = added[:, (2 * j + 1) * half : (2 * j + 2) * half].astype(bf16)


def fold(held, received, half):
    r, size = held.shape
    return pl.pallas_call(
        functools.partial(fold_kernel, half),
        out_shape=(shape((r, size // 2), f32), shape((r, size // 2), bf16)),
        in_specs=[VMEM, VMEM],
        out_specs=(VMEM, VMEM),
        compiler_params=params(8),
        name="fold",
    )(held, received)


def fold_last_kernel(held, received, *rest):
    before, out = rest[:-1], rest[-1]
    half = held.shape[1]
    for k, ref in enumerate(before):
        out[:, k * half : (k + 1) * half] = ref[...]
    out[:, len(before) * half :] = (held[...] + received[...].astype(f32)).astype(bf16)


def fold_last(held, received, *before):
    r, half = held.shape
    return pl.pallas_call(
        fold_last_kernel,
        out_shape=shape((r, half * (1 + len(before))), bf16),
        in_specs=[VMEM] * (2 + len(before)),
        out_specs=VMEM,
        compiler_params=params(8),
        name="fold_last",
    )(held, received, *before)


def cost(*arrays):
    size = sum(math.prod(x.shape) * x.dtype.itemsize for x in arrays)
    return pl.CostEstimate(flops=0, bytes_accessed=size, transcendentals=0)


def keep(x):
    return pltpu.with_memory_space_constraint(x, pltpu.VMEM)


def stay(x):
    return pltpu.with_memory_space_constraint(x, pltpu.HBM)


def buffer_rows(bufs, ds, depth, cols):
    half = bufs[0].shape[0] // depth
    me = lax.axis_index("col")
    rows = [pl.ds(pl.multiple_of(flip(me, d) * half, half), half) for d in ds]
    return jnp.concatenate([buf[at, cols].astype(bf16) for at in rows for buf in bufs], axis=0)


def early(depth):
    return (0, depth // 2)


def late(depth):
    return tuple(d for d in range(depth) if d not in early(depth))


def first_kernel(depth, width, buf0, buf1, *rest):
    lefts, (other, mine, gram, whole) = rest[:-4], rest[-4:]
    core = lax.bitwise_and(lax.axis_index("row"), jnp.int32(1))
    size = other.shape[1]
    block = lefts[0].shape[1]
    for d, ref in enumerate(lefts):
        whole[:, d * block : (d + 1) * block] = ref[...]
    gram[...] = dot(whole[...], whole[...], ((1,), (1,)))
    for out, half in ((other, 1 - core), (mine, core)):

        def step(k, carry, out=out, half=half):
            cols = pl.ds(pl.multiple_of(half * size + k * width, 128), width)
            b = buffer_rows((buf0, buf1), early(depth), depth, cols)
            out[:, pl.ds(pl.multiple_of(k * width, 128), width)] = dot(whole[...], b)
            return carry

        lax.fori_loop(0, size // width, step, 0)


def first_product(bufs, lefts, depth, width):
    m, n = bufs[0].shape
    r, block = lefts[0].shape
    return pl.pallas_call(
        functools.partial(first_kernel, depth, width),
        out_shape=(shape((r, n // 2), f32), shape((r, n // 2), f32), shape((r, r), f32)),
        in_specs=[VMEM] * (2 + len(lefts)),
        out_specs=[VMEM] * 3,
        scratch_shapes=[pltpu.VMEM((r, block * len(lefts)), bf16)],
        compiler_params=params(10),
        cost_estimate=cost(*bufs, shape((r, n), f32)),
        name="first_product",
    )(*map(keep, bufs), *lefts)


def gram_kernel(sums, *rest):
    lefts, (g_mine, g_other, total) = rest[:-3], rest[-3:]
    core = lax.bitwise_and(lax.axis_index("row"), jnp.int32(1))
    total[...] = sums[...] + sum(dot(ref[...], ref[...], ((1,), (1,))) for ref in lefts)
    h = g_mine.shape[0]
    g_mine[...] = total[pl.ds(pl.multiple_of(core * h, h), h), :]
    g_other[...] = total[pl.ds(pl.multiple_of((1 - core) * h, h), h), :]


def gram(lefts, sums):
    r = lefts[0].shape[0]
    return pl.pallas_call(
        gram_kernel,
        out_shape=[shape((r // 2, r), f32)] * 2,
        in_specs=[VMEM] * (1 + len(lefts)),
        out_specs=[VMEM] * 2,
        scratch_shapes=[pltpu.VMEM((r, r), f32)],
        compiler_params=params(8),
        name="gram",
    )(sums, *lefts)


def last_kernel(depth, width, mine, buf0, buf1, sums, *rest):
    lefts, (*_, out, whole) = rest[: len(late(depth))], rest[len(late(depth)) :]
    core = lax.bitwise_and(lax.axis_index("row"), jnp.int32(1))
    half = core if mine else 1 - core
    size = out.shape[1]
    block = lefts[0].shape[1]
    for k, ref in enumerate(lefts):
        whole[:, k * block : (k + 1) * block] = ref[...]

    def step(k, carry):
        cols = pl.ds(pl.multiple_of(half * size + k * width, 128), width)
        at = pl.ds(pl.multiple_of(k * width, 128), width)
        b = buffer_rows((buf0, buf1), late(depth), depth, cols)
        out[:, at] = (sums[:, at] + dot(whole[...], b)).astype(out.dtype)
        return carry

    lax.fori_loop(0, size // width, step, 0)


def last_product(bufs, sums, lefts, depth, width, mine, *after):
    r, block = lefts[0].shape
    return pl.pallas_call(
        functools.partial(last_kernel, depth, width, mine),
        out_shape=shape(sums.shape, f32 if mine else bf16),
        in_specs=[VMEM] * (3 + len(lefts)) + [ANY] * len(after),
        out_specs=VMEM,
        scratch_shapes=[pltpu.VMEM((r, block * len(lefts)), bf16)],
        compiler_params=params(8),
        cost_estimate=cost(*bufs[:1], sums),
        name="mine_product" if mine else "other_product",
    )(*map(keep, bufs), sums, *lefts, *after)


def pair_sum_kernel(chips, mine, received, _, *outs):
    me = lax.div(lax.axis_index("row"), jnp.int32(2))
    width = outs[0].shape[1]
    for d in range(chips):
        cols = pl.ds(pl.multiple_of(flip(me, d) * width, 128), width)
        outs[d][...] = (mine[:, cols] + received[:, cols].astype(f32)).astype(outs[d].dtype)


def pair_sum(mine, received, chips, after):
    r, n = mine.shape
    kinds = [f32] + [bf16] * (chips - 1)
    return pl.pallas_call(
        functools.partial(pair_sum_kernel, chips),
        out_shape=[shape((r, n // chips), k) for k in kinds],
        in_specs=[VMEM, VMEM, ANY],
        out_specs=[VMEM] * chips,
        compiler_params=params(8),
        name="pair_sum",
    )(mine, received, after)


def eliminate(tiles, at, nb, group):
    sub = lax.broadcasted_iota(jnp.int32, (nb, 128), 0)
    scale = jnp.zeros((nb, 128), f32)
    for g in range(0, nb, group):
        cols = [
            jnp.broadcast_to(tiles[0][:, at + g + j : at + g + j + 1], (nb, 128)) for j in range(group)
        ]
        for j in range(group):
            t = g + j
            pivot = cols[j][t : t + 1, :]
            factor = jnp.where(sub > t, cols[j], 0.0) * (1.0 / pivot)
            scale = jnp.where(sub == t, lax.rsqrt(pivot), scale)
            for l in range(j + 1, group):
                cols[l] = cols[l] - factor * cols[l][t : t + 1, :]
            tiles = [x - factor * x[t : t + 1, :] for x in tiles]
    return [x * scale for x in tiles]


def chol_inverse_kernel(mine, other, weight, out, fetched, work, sem):
    piece = weight.shape[0] // sem.shape[0]
    fetches = [
        pltpu.make_async_copy(weight.at[pl.ds(k * piece, piece), :], fetched.at[pl.ds(k * piece, piece), :], sem.at[k])
        for k in range(sem.shape[0])
    ]
    for fetch in fetches:
        fetch.start()
    n = out.shape[0]
    h = n // 2
    core = lax.bitwise_and(lax.axis_index("row"), jnp.int32(1))
    work[pl.ds(pl.multiple_of(core * h, h), h), :n] = mine[...]
    work[pl.ds(pl.multiple_of((1 - core) * h, h), h), :n] = other[...]
    r_id = lax.broadcasted_iota(jnp.int32, (n, n), 0)
    c_id = lax.broadcasted_iota(jnp.int32, (n, n), 1)
    work[:, n:] = jnp.where(r_id == c_id, 1.0, 0.0).astype(f32)
    nb = 32
    for p in range(n // nb):
        lo = p * nb
        left = (lo // 128) * 128
        right = n + ((lo + nb + 127) // 128) * 128
        tiles = [work[lo : lo + nb, c : c + 128] for c in range(left, right, 128)]
        s = jnp.concatenate(eliminate(tiles, lo - left, nb, 8), axis=1)
        work[lo : lo + nb, left:right] = s
        if lo + nb < n:
            lead = s[:, lo + nb - left : n - left]
            work[lo + nb :, left:right] -= lax.dot_general(
                lead, s, (((0,), (0,)), ((), ())), precision=lax.Precision.HIGHEST, preferred_element_type=f32
            )
    out[...] = jnp.where(r_id >= c_id, work[:, n:], 0.0)
    for fetch in fetches:
        fetch.wait()


def chol_inverse(mine, other, weight):
    n = mine.shape[1]
    return pl.pallas_call(
        chol_inverse_kernel,
        out_shape=(shape((n, n), f32), pltpu.VMEM(weight.shape, weight.dtype)),
        in_specs=[VMEM, VMEM, ANY],
        out_specs=(VMEM, VMEM),
        scratch_shapes=[pltpu.VMEM((n, 2 * n), f32), pltpu.SemaphoreType.DMA((8,))],
        compiler_params=params(8),
        cost_estimate=cost(*[mine] * 256),
        name="chol_inverse",
    )(mine, other, stay(weight))


def ortho_kernel(inverse, *refs):
    lefts, out = refs[:-1], refs[-1]
    block = lefts[0].shape[1]
    me = lax.axis_index("col")
    parts = split(inverse[...], 3)
    for d, ref in enumerate(lefts):
        rows = pl.ds(pl.multiple_of(flip(me, d) * block, block), block)
        out[rows, :] = sum(dot(ref[...], x, ((0,), (1,))) for x in reversed(parts)).astype(bf16)


def ortho(inverse, lefts):
    r, block = lefts[0].shape
    return pl.pallas_call(
        ortho_kernel,
        out_shape=shape((block * len(lefts), r), bf16),
        in_specs=[VMEM] * (1 + len(lefts)),
        out_specs=VMEM,
        compiler_params=params(8),
        cost_estimate=cost(*[shape((block * len(lefts), r), bf16)] * 8),
        name="ortho",
    )(inverse, *lefts)


def hand_on(x, *earlier):
    return pl.pallas_call(
        lambda *refs: None,
        out_shape=shape(x.shape, x.dtype),
        in_specs=[ANY] * (1 + len(earlier)),
        out_specs=ANY,
        input_output_aliases={0: 0},
        compiler_params=params(1),
        name="hand_on",
    )(x, *earlier)


def block_ids(pairs):
    row = lax.axis_index("row")
    core = lax.bitwise_and(row, jnp.int32(1))
    chip = lax.div(row, jnp.int32(2))
    chips = lax.axis_size("row") // 2
    return [half * chips + flip(chip, d) for d in pairs for half in (core, 1 - core)]


def share_kernel(inverse, own, *refs):
    received, (out, squares) = refs[:-2], refs[-2:]
    total = own[...] + sum(ref[...].astype(f32) for ref in received)
    x_high, x_low = split(inverse[...], 2)
    high, low = split(total, 2)
    right = dot(x_high, low) + dot(x_low, high) + dot(x_high, high)
    out[...] = right.astype(bf16)
    r = out.shape[0]
    sums = jnp.sum(right * right, axis=1, keepdims=True)
    sums = jnp.transpose(jnp.broadcast_to(sums, (r, 128)))[: squares.shape[0], :]
    block_id = lax.broadcasted_iota(jnp.int32, squares.shape, 0)
    squares[...] = jnp.where(block_id == block_ids((0,))[0], sums, 0.0)


def share_of(inverse, own, received):
    r, width = own.shape
    rows = max(8, lax.axis_size("row"))
    return pl.pallas_call(
        share_kernel,
        out_shape=(shape((r, width), bf16), shape((rows, r), f32)),
        in_specs=[VMEM] * (2 + len(received)),
        out_specs=(VMEM, VMEM),
        compiler_params=params(8),
        name="share",
    )(inverse, own, *received)


def result_kernel(pairs, momentum_too, weight_too, factor, buf0, buf1, ortho_ref, weight, squares, *refs):
    blocks, rest = refs[: 2 * len(pairs)], refs[2 * len(pairs) :]
    *outs, token, mbuf, vbuf, nbuf, out_sems, basis_sems = rest
    new_momentum = outs[-1] if momentum_too else None
    new_weight, basis = outs[-2 - momentum_too : len(outs) - momentum_too] if weight_too else (None, None)
    r, width = blocks[0].shape
    tile = 256
    tiles = width // tile
    count = len(blocks)
    starts = [i * width for i in block_ids(pairs)]

    def store_basis(b):
        cols = pl.ds(pl.multiple_of(starts[b], 128), width)
        return pltpu.make_async_copy(nbuf.at[b % 2], basis.at[:, cols], basis_sems.at[b % 2])

    def place(b, t):
        return pl.ds(pl.multiple_of(t * tile, tile), tile), pl.ds(pl.multiple_of(starts[b] + t * tile, 128), tile)

    def stores(b, t):
        at, there = place(b, t)
        copies = []
        if momentum_too:
            copies.append((mbuf, new_momentum))
        if weight_too:
            copies.append((vbuf, new_weight))
        return [
            pltpu.make_async_copy(src.at[b % 2, :, at], dst.at[:, there], out_sems.at[k, b % 2, t])
            for k, (src, dst) in enumerate(copies)
        ]

    def finish(b):
        if weight_too:
            store_basis(b).wait()
        for t in range(tiles):
            for store in stores(b, t):
                store.wait()

    if weight_too:
        scale = lax.rsqrt(jnp.sum(squares[...], axis=0, keepdims=True) / FF + epsilon)
        scale = jnp.transpose(jnp.broadcast_to(scale, (128, r)))[:, :1]
    token[...] = jnp.zeros_like(token)
    depth = lax.axis_size("col")
    size = buf0.shape[0] // depth
    for b in range(count):
        k = b % 2
        if b >= 2:
            finish(b - 2)
        if weight_too:
            nbuf[k] = (blocks[b][...].astype(f32) * scale).astype(bf16)
            store_basis(b).start()

        def step(t, carry, b=b, k=k):
            at, there = place(b, t)
            if momentum_too:
                correction = dot(ortho_ref[...], blocks[b][:, at])
                for j in range(2 * depth):
                    rows = slice(j * size, (j + 1) * size)
                    here = slice(j // 2 * size, (j // 2 + 1) * size)
                    old = (buf0, buf1)[j % 2][here, there]
                    mbuf[k, rows, at] = old - (1.0 - momentum_decay) * correction[rows]
            if weight_too:
                change = dot(ortho_ref[...], nbuf[k, :, at])
                vbuf[k, :, at] = (weight[:, there].astype(f32) - factor * change).astype(bf16)
            for store in stores(b, t):
                store.start()
            return carry

        lax.fori_loop(0, tiles, step, 0)
    for b in range(count - 2, count):
        finish(b)


def results(pairs, kinds, factor, bufs, ortho_bf, weight, squares, blocks, outs=(), after=(), last=()):
    momentum_too, weight_too = kinds
    m, n = weight.shape
    r, width = blocks[0].shape
    outs = [*outs, *last]
    ins = [*map(keep, bufs), ortho_bf, keep(weight), squares, *blocks, *after, *map(stay, outs)]
    at = len(ins) - len(outs)
    skipped = 2 * weight_too + momentum_too - len(outs) if last else 0
    out_shape = []
    if weight_too:
        out_shape += [shape((m, n), bf16), shape((r, n), bf16)]
    if momentum_too:
        out_shape += [shape((m, n), f32)]
    m_rows, w_rows = (m if momentum_too else 8), (m if weight_too else 16)
    *outs, token = pl.pallas_call(
        functools.partial(result_kernel, pairs, *kinds, factor),
        out_shape=[*out_shape, shape((8, 128), f32)],
        in_specs=[VMEM] * (5 + len(blocks)) + [ANY] * (len(after) + len(outs)),
        out_specs=[ANY] * len(out_shape) + [VMEM],
        input_output_aliases={at + k: skipped + k for k in range(len(outs))},
        scratch_shapes=[
            pltpu.VMEM((2, m_rows, width), f32),
            pltpu.VMEM((2, w_rows, width), bf16),
            pltpu.VMEM((2, r, width), bf16),
            pltpu.SemaphoreType.DMA((2, 2, width // 256)),
            pltpu.SemaphoreType.DMA((2,)),
        ],
        compiler_params=params(12),
        cost_estimate=cost(*[shape((m, width), f32)] * (len(blocks) * (momentum_too + weight_too))),
        name="results",
    )(*ins)
    return outs, token


def sum_over(x, axis, least=1):
    d = least
    while d < lax.axis_size(axis):
        x = x + swap(x, axis, d)
        d *= 2
    return x


def exchange(x, axis, count, unit=1):
    return [x] + [swap(x, axis, unit * d) for d in range(1, count)]


def pair_up(terms):
    while len(terms) > 1:
        terms = [terms[2 * i] + terms[2 * i + 1] for i in range(len(terms) // 2)]
    return terms[0]


def gather(x, axis):
    blocks = [x]
    size = lax.axis_size(axis)
    for d in range(1, size):
        low = d & -d
        blocks.append(swap(blocks[d - low] if d != low else x, axis, low))
    return blocks


def per_device(weight, gradient, momentum, old_basis):
    depth, rows = lax.axis_size("col"), lax.axis_size("row")
    chips = rows // 2
    m, n = momentum.shape
    width = n // rows

    def sum_over_col(held, sent, *before):
        half = m // 2 // depth
        d = 1
        while held.shape[1] > half:
            held, sent = fold(held, swap(sent, "col", d), half)
            d *= 2
        return fold_last(held, swap(sent, "col", d), *before)

    buf0, kept, *outs = project(momentum, gradient, old_basis, depth, width, 0)
    low = sum_over_col(*outs)
    buf1, *outs = project(momentum, gradient, kept, depth, width, 1, (outs[1],))
    lefts = gather(sum_over_col(*outs, low), "col")
    bufs = (buf0, buf1)

    other, mine, g_sums = first_product(bufs, [lefts[d] for d in early(depth)], depth, width)
    lefts_late = [lefts[d] for d in late(depth)]
    g_mine, g_other = gram(lefts_late, g_sums)
    other = last_product(bufs, other, lefts_late, depth, width, False, g_mine)
    g_mine = g_mine + swap(g_other, "row", 1)
    other = hand_on(other, g_mine)
    received = swap(other, "row", 1)
    mine = last_product(bufs, mine, lefts_late, depth, width, True, g_mine, other)
    own, *sent = pair_sum(mine, received, chips, g_mine)
    g_mine = pair_up(exchange(g_mine, "row", chips, 2))
    got = [swap(x, "row", 2 * (d + 1)) for d, x in enumerate(sent)]
    inverse, weight = chol_inverse(g_mine, swap(g_mine, "row", 1), weight)

    share, squares = share_of(inverse, own, got)
    ortho_bf = ortho(inverse, lefts)

    near = [d for d in range(chips) if d & (d - 1) == 0]
    blocks = {d: swap(share, "row", 2 * d) for d in near[1:]}
    own_pair = swap(share, "row", 1)
    factor = step_rate * math.sqrt(D / RANK)
    common = (factor, bufs, ortho_bf, weight)
    squares = exchange(hand_on(squares, own_pair), "col", depth)
    (momentum,), token = results((0,), (True, False), *common, squares[0], (share, own_pair))
    squares = pair_up([hand_on(squares[0], token), *squares[1:]])
    squares = squares + swap(squares, "row", 1)
    squares = hand_on(squares, *blocks.values())
    squares = pair_up(exchange(squares, "row", chips, 2))
    pairs = {}
    for d in near[1:]:
        block = hand_on(blocks[d], squares)
        pairs[d] = (block, swap(block, "row", 1))
    pairs[0] = (share, own_pair)
    h = share.shape[0] // 2
    blocks = {d: pairs[d][0] for d in near}
    halves = {}
    for d in range(chips):
        if d not in near:
            least, most = d & -d, 1 << (d.bit_length() - 1)
            top = swap(blocks[d ^ most][:h], "row", 2 * most)
            bottom = swap(blocks[d ^ least][h:], "row", 2 * least)
            halves[d] = top, bottom
            blocks[d] = jnp.concatenate([top, bottom], axis=0)

    common = (*common, squares)
    weight_basis = ()
    if near[1:]:
        rest = [x for d in near[1:] for x in pairs[d]]
        (*weight_basis, momentum), token = results(
            tuple(near[1:]), (True, True), *common, rest, (), (), [momentum]
        )
    blocks = {d: jnp.concatenate([hand_on(top, token), bottom], axis=0) for d, (top, bottom) in halves.items()}
    weight_basis, token = results((0,), (False, True), *common, pairs[0], weight_basis)
    outs = [*weight_basis, momentum]
    for d, block in blocks.items():
        outs, token = results((d,), (True, True), *common, (block, swap(block, "row", 1)), outs)
    new_weight, new_basis, new_momentum = outs
    return (new_weight, new_momentum, new_basis)


def plain_per_device(weight, gradient, momentum, old_basis):
    buffer = momentum + gradient.astype(f32)
    buffer_low = buffer.astype(bf16)
    left_factor = lax.psum(dot(buffer_low, old_basis, ((1,), (1,))), "col")
    gram_share = lax.dot_general(
        left_factor,
        left_factor,
        (((0,), (0,)), ((), ())),
        precision=lax.Precision.HIGHEST,
        preferred_element_type=f32,
    )
    chol_factor = jnp.linalg.cholesky(lax.psum(gram_share, "row"))
    orthonormal = lax.linalg.triangular_solve(
        chol_factor, left_factor, left_side=False, lower=True, transpose_a=True
    ).astype(bf16)
    right_share = lax.psum_scatter(
        dot(orthonormal, buffer_low, ((0,), (0,))), "row", scatter_dimension=0, tiled=True
    )
    sum_squares = lax.psum(jnp.sum(right_share * right_share, axis=1), "col")
    scale_share = jnp.sqrt(sum_squares / FF + epsilon)
    basis_share = (right_share / scale_share[:, None]).astype(bf16)
    new_basis = lax.all_gather(basis_share, "row", axis=0, tiled=True)
    col_scale = lax.all_gather(scale_share, "row", axis=0, tiled=True)
    scaled = (orthonormal.astype(f32) * col_scale[None, :]).astype(bf16)
    new_momentum = buffer - (1.0 - momentum_decay) * dot(scaled, new_basis)
    factor = step_rate * math.sqrt(D / RANK)
    new_weight = (weight.astype(f32) - factor * dot(orthonormal, new_basis)).astype(bf16)
    return (new_weight, new_momentum, new_basis)


def power_of_two(k):
    return k > 1 and k & (k - 1) == 0


def solution(mesh):
    rows, depth = mesh.shape["row"], mesh.shape["col"]
    tiled = (
        power_of_two(rows // 2)
        and power_of_two(depth)
        and depth > 2
        and D % (rows * depth * 128) == 0
        and FF % (rows * depth * 256) == 0
    )
    return jax.shard_map(
        per_device if tiled else plain_per_device,
        mesh=mesh,
        in_specs=(P("row", "col"), P("row", "col"), P("row", "col"), P(None, "col")),
        out_specs=(P("row", "col"), P("row", "col"), P(None, "col")),
        check_vma=False,
    )
```

```python
import functools
import math

import jax
import jax.numpy as jnp
from jax import lax
from jax.experimental import pallas as pl
from jax.experimental.pallas import tpu as pltpu
from jax.sharding import PartitionSpec as P

D = 8192
FF = 24576
RANK = 256

epsilon = 1e-06
momentum_decay = 0.6
step_rate = 0.5

bf16, f32 = jnp.bfloat16, jnp.float32
VMEM = pl.BlockSpec(memory_space=pltpu.VMEM)
ANY = pl.BlockSpec(memory_space=pl.ANY)
MIB = 1 << 20


def shape(dims, kind):
    return jax.ShapeDtypeStruct(dims, kind)


def params(mib):
    return pltpu.CompilerParams(vmem_limit_bytes=mib * MIB)


def dot(a, b, dims=((1,), (0,))):
    return lax.dot_general(a, b, (dims, ((), ())), preferred_element_type=f32)


def split(x, terms):
    parts = []
    for _ in range(terms):
        part = x.astype(bf16)
        parts.append(part)
        x = x - part.astype(f32)
    return parts


def flip(i, d):
    return lax.bitwise_xor(i, jnp.int32(d))


def swap(x, axis, d):
    return lax.ppermute(x, axis, [(i, i ^ d) for i in range(lax.axis_size(axis))])


def project_kernel(part, depth, width, mom, grad, basis, *rest):
    if part == 0:
        (buf, kept), rest = rest[:2], rest[2:]
    else:
        kept, buf, rest = basis, rest[1], rest[2:]
    held, sent, gbuf, total, sems, basis_sem = rest
    m, n = buf.shape
    half = m // depth

    def copies(c):
        cols = pl.ds(pl.multiple_of(c * width, 128), width)
        pairs = []
        for k in range(depth):
            there = pl.ds((2 * k + part) * half, half)
            here = pl.ds(k * half, half)
            pairs.append(pltpu.make_async_copy(mom.at[there, cols], buf.at[here, cols], sems.at[0, k, c]))
            pairs.append(pltpu.make_async_copy(grad.at[there, cols], gbuf.at[here, cols], sems.at[1, k, c]))
        if part == 0:
            pairs.append(pltpu.make_async_copy(basis.at[:, cols], kept.at[:, cols], basis_sem.at[c]))
        return pairs

    def start(c, carry):
        for copy in copies(c):
            copy.start()
        return carry

    def step(c, carry):
        for copy in copies(c):
            copy.wait()
        cols = pl.ds(pl.multiple_of(c * width, 128), width)
        added = buf[:, cols] + gbuf[:, cols].astype(f32)
        buf[:, cols] = added
        total[...] += dot(added.astype(bf16), kept[:, cols], ((1,), (1,)))
        return carry

    total[...] = jnp.zeros_like(total)
    lax.fori_loop(0, n // width, start, 0)
    lax.fori_loop(0, n // width, step, 0)
    me = lax.axis_index("col")
    for out, odd in ((held, 0), (sent, 1)):
        for j in range(depth // 2):
            rows = pl.ds(pl.multiple_of(flip(me, 2 * j + odd) * half, half), half)
            out[:, j * half : (j + 1) * half] = jnp.transpose(total[rows, :]).astype(out.dtype)


def project(momentum, gradient, basis, depth, width, part, after=()):
    m, n = momentum.shape
    m = m // 2
    r = basis.shape[0]
    kept = [] if part else [pltpu.VMEM((r, n), bf16)]
    return pl.pallas_call(
        functools.partial(project_kernel, part, depth, width),
        out_shape=(pltpu.VMEM((m, n), f32), *kept, shape((r, m // 2), f32), shape((r, m // 2), bf16)),
        in_specs=[ANY, ANY] + [VMEM if part else ANY] + [ANY] * len(after),
        out_specs=(VMEM,) * (3 + len(kept)),
        scratch_shapes=[
            pltpu.VMEM((m, n), bf16),
            pltpu.VMEM((m, r), f32),
            pltpu.SemaphoreType.DMA((2, depth, n // width)),
            pltpu.SemaphoreType.DMA((n // width,)),
        ],
        compiler_params=params(14),
        cost_estimate=cost(momentum, gradient),
        name="project",
    )(stay(momentum), stay(gradient), keep(basis) if part else stay(basis), *after)


def fold_kernel(half, held, received, held_out, sent_out):
    added = held[...] + received[...].astype(f32)
    for j in range(held_out.shape[1] // half):
        at = slice(j * half, (j + 1) * half)
        held_out[:, at] = added[:, 2 * j * half : (2 * j + 1) * half]
        sent_out[:, at] = added[:, (2 * j + 1) * half : (2 * j + 2) * half].astype(bf16)


def fold(held, received, half):
    r, size = held.shape
    return pl.pallas_call(
        functools.partial(fold_kernel, half),
        out_shape=(shape((r, size // 2), f32), shape((r, size // 2), bf16)),
        in_specs=[VMEM, VMEM],
        out_specs=(VMEM, VMEM),
        compiler_params=params(8),
        name="fold",
    )(held, received)


def fold_last_kernel(held, received, *rest):
    before, out = rest[:-1], rest[-1]
    half = held.shape[1]
    for k, ref in enumerate(before):
        out[:, k * half : (k + 1) * half] = ref[...]
    out[:, len(before) * half :] = (held[...] + received[...].astype(f32)).astype(bf16)


def fold_last(held, received, *before):
    r, half = held.shape
    return pl.pallas_call(
        fold_last_kernel,
        out_shape=shape((r, half * (1 + len(before))), bf16),
        in_specs=[VMEM] * (2 + len(before)),
        out_specs=VMEM,
        compiler_params=params(8),
        name="fold_last",
    )(held, received, *before)


def cost(*arrays):
    size = sum(math.prod(x.shape) * x.dtype.itemsize for x in arrays)
    return pl.CostEstimate(flops=0, bytes_accessed=size, transcendentals=0)


def keep(x):
    return pltpu.with_memory_space_constraint(x, pltpu.VMEM)


def stay(x):
    return pltpu.with_memory_space_constraint(x, pltpu.HBM)


def buffer_rows(bufs, ds, depth, cols):
    half = bufs[0].shape[0] // depth
    me = lax.axis_index("col")
    rows = [pl.ds(pl.multiple_of(flip(me, d) * half, half), half) for d in ds]
    return jnp.concatenate([buf[at, cols].astype(bf16) for at in rows for buf in bufs], axis=0)


def early(depth):
    return (0, depth // 2)


def late(depth):
    return tuple(d for d in range(depth) if d not in early(depth))


def first_kernel(depth, width, buf0, buf1, *rest):
    lefts, (other, mine, gram, whole) = rest[:-4], rest[-4:]
    core = lax.bitwise_and(lax.axis_index("row"), jnp.int32(1))
    size = other.shape[1]
    block = lefts[0].shape[1]
    for d, ref in enumerate(lefts):
        whole[:, d * block : (d + 1) * block] = ref[...]
    gram[...] = dot(whole[...], whole[...], ((1,), (1,)))
    for out, half in ((other, 1 - core), (mine, core)):

        def step(k, carry, out=out, half=half):
            cols = pl.ds(pl.multiple_of(half * size + k * width, 128), width)
            b = buffer_rows((buf0, buf1), early(depth), depth, cols)
            out[:, pl.ds(pl.multiple_of(k * width, 128), width)] = dot(whole[...], b)
            return carry

        lax.fori_loop(0, size // width, step, 0)


def first_product(bufs, lefts, depth, width):
    m, n = bufs[0].shape
    r, block = lefts[0].shape
    return pl.pallas_call(
        functools.partial(first_kernel, depth, width),
        out_shape=(shape((r, n // 2), f32), shape((r, n // 2), f32), shape((r, r), f32)),
        in_specs=[VMEM] * (2 + len(lefts)),
        out_specs=[VMEM] * 3,
        scratch_shapes=[pltpu.VMEM((r, block * len(lefts)), bf16)],
        compiler_params=params(10),
        cost_estimate=cost(*bufs, shape((r, n), f32)),
        name="first_product",
    )(*map(keep, bufs), *lefts)


def gram_kernel(sums, *rest):
    lefts, (g_mine, g_other, total) = rest[:-3], rest[-3:]
    core = lax.bitwise_and(lax.axis_index("row"), jnp.int32(1))
    total[...] = sums[...] + sum(dot(ref[...], ref[...], ((1,), (1,))) for ref in lefts)
    h = g_mine.shape[0]
    g_mine[...] = total[pl.ds(pl.multiple_of(core * h, h), h), :]
    g_other[...] = total[pl.ds(pl.multiple_of((1 - core) * h, h), h), :]


def gram(lefts, sums):
    r = lefts[0].shape[0]
    return pl.pallas_call(
        gram_kernel,
        out_shape=[shape((r // 2, r), f32)] * 2,
        in_specs=[VMEM] * (1 + len(lefts)),
        out_specs=[VMEM] * 2,
        scratch_shapes=[pltpu.VMEM((r, r), f32)],
        compiler_params=params(8),
        name="gram",
    )(sums, *lefts)


def last_kernel(depth, width, mine, buf0, buf1, sums, *rest):
    lefts, (*_, out, whole) = rest[: len(late(depth))], rest[len(late(depth)) :]
    core = lax.bitwise_and(lax.axis_index("row"), jnp.int32(1))
    half = core if mine else 1 - core
    size = out.shape[1]
    block = lefts[0].shape[1]
    for k, ref in enumerate(lefts):
        whole[:, k * block : (k + 1) * block] = ref[...]

    def step(k, carry):
        cols = pl.ds(pl.multiple_of(half * size + k * width, 128), width)
        at = pl.ds(pl.multiple_of(k * width, 128), width)
        b = buffer_rows((buf0, buf1), late(depth), depth, cols)
        out[:, at] = (sums[:, at] + dot(whole[...], b)).astype(out.dtype)
        return carry

    lax.fori_loop(0, size // width, step, 0)


def last_product(bufs, sums, lefts, depth, width, mine, *after):
    r, block = lefts[0].shape
    return pl.pallas_call(
        functools.partial(last_kernel, depth, width, mine),
        out_shape=shape(sums.shape, f32 if mine else bf16),
        in_specs=[VMEM] * (3 + len(lefts)) + [ANY] * len(after),
        out_specs=VMEM,
        scratch_shapes=[pltpu.VMEM((r, block * len(lefts)), bf16)],
        compiler_params=params(8),
        cost_estimate=cost(*bufs[:1], sums),
        name="mine_product" if mine else "other_product",
    )(*map(keep, bufs), sums, *lefts, *after)


def pair_sum_kernel(chips, mine, received, _, *outs):
    me = lax.div(lax.axis_index("row"), jnp.int32(2))
    width = outs[0].shape[1]
    for d in range(chips):
        cols = pl.ds(pl.multiple_of(flip(me, d) * width, 128), width)
        outs[d][...] = (mine[:, cols] + received[:, cols].astype(f32)).astype(outs[d].dtype)


def pair_sum(mine, received, chips, after):
    r, n = mine.shape
    kinds = [f32] + [bf16] * (chips - 1)
    return pl.pallas_call(
        functools.partial(pair_sum_kernel, chips),
        out_shape=[shape((r, n // chips), k) for k in kinds],
        in_specs=[VMEM, VMEM, ANY],
        out_specs=[VMEM] * chips,
        compiler_params=params(8),
        name="pair_sum",
    )(mine, received, after)


def eliminate(tiles, at, nb, group):
    sub = lax.broadcasted_iota(jnp.int32, (nb, 128), 0)
    scale = jnp.zeros((nb, 128), f32)
    for g in range(0, nb, group):
        cols = [
            jnp.broadcast_to(tiles[0][:, at + g + j : at + g + j + 1], (nb, 128)) for j in range(group)
        ]
        for j in range(group):
            t = g + j
            pivot = cols[j][t : t + 1, :]
            factor = jnp.where(sub > t, cols[j], 0.0) * (1.0 / pivot)
            scale = jnp.where(sub == t, lax.rsqrt(pivot), scale)
            for l in range(j + 1, group):
                cols[l] = cols[l] - factor * cols[l][t : t + 1, :]
            tiles = [x - factor * x[t : t + 1, :] for x in tiles]
    return [x * scale for x in tiles]


def chol_inverse_kernel(mine, other, weight, out, fetched, work, sem):
    piece = weight.shape[0] // sem.shape[0]
    fetches = [
        pltpu.make_async_copy(weight.at[pl.ds(k * piece, piece), :], fetched.at[pl.ds(k * piece, piece), :], sem.at[k])
        for k in range(sem.shape[0])
    ]
    for fetch in fetches:
        fetch.start()
    n = out.shape[0]
    h = n // 2
    core = lax.bitwise_and(lax.axis_index("row"), jnp.int32(1))
    work[pl.ds(pl.multiple_of(core * h, h), h), :n] = mine[...]
    work[pl.ds(pl.multiple_of((1 - core) * h, h), h), :n] = other[...]
    r_id = lax.broadcasted_iota(jnp.int32, (n, n), 0)
    c_id = lax.broadcasted_iota(jnp.int32, (n, n), 1)
    work[:, n:] = jnp.where(r_id == c_id, 1.0, 0.0).astype(f32)
    nb = 32
    for p in range(n // nb):
        lo = p * nb
        left = (lo // 128) * 128
        right = n + ((lo + nb + 127) // 128) * 128
        tiles = [work[lo : lo + nb, c : c + 128] for c in range(left, right, 128)]
        s = jnp.concatenate(eliminate(tiles, lo - left, nb, 8), axis=1)
        work[lo : lo + nb, left:right] = s
        if lo + nb < n:
            lead = s[:, lo + nb - left : n - left]
            work[lo + nb :, left:right] -= lax.dot_general(
                lead, s, (((0,), (0,)), ((), ())), precision=lax.Precision.HIGHEST, preferred_element_type=f32
            )
    out[...] = jnp.where(r_id >= c_id, work[:, n:], 0.0)
    for fetch in fetches:
        fetch.wait()


def chol_inverse(mine, other, weight):
    n = mine.shape[1]
    return pl.pallas_call(
        chol_inverse_kernel,
        out_shape=(shape((n, n), f32), pltpu.VMEM(weight.shape, weight.dtype)),
        in_specs=[VMEM, VMEM, ANY],
        out_specs=(VMEM, VMEM),
        scratch_shapes=[pltpu.VMEM((n, 2 * n), f32), pltpu.SemaphoreType.DMA((8,))],
        compiler_params=params(8),
        cost_estimate=cost(*[mine] * 256),
        name="chol_inverse",
    )(mine, other, stay(weight))


def ortho_kernel(inverse, *refs):
    lefts, out = refs[:-1], refs[-1]
    block = lefts[0].shape[1]
    me = lax.axis_index("col")
    parts = split(inverse[...], 3)
    for d, ref in enumerate(lefts):
        rows = pl.ds(pl.multiple_of(flip(me, d) * block, block), block)
        out[rows, :] = sum(dot(ref[...], x, ((0,), (1,))) for x in reversed(parts)).astype(bf16)


def ortho(inverse, lefts):
    r, block = lefts[0].shape
    return pl.pallas_call(
        ortho_kernel,
        out_shape=shape((block * len(lefts), r), bf16),
        in_specs=[VMEM] * (1 + len(lefts)),
        out_specs=VMEM,
        compiler_params=params(8),
        cost_estimate=cost(*[shape((block * len(lefts), r), bf16)] * 8),
        name="ortho",
    )(inverse, *lefts)


def hand_on(x, *earlier):
    return pl.pallas_call(
        lambda *refs: None,
        out_shape=shape(x.shape, x.dtype),
        in_specs=[ANY] * (1 + len(earlier)),
        out_specs=ANY,
        input_output_aliases={0: 0},
        compiler_params=params(1),
        name="hand_on",
    )(x, *earlier)


def block_ids(pairs):
    row = lax.axis_index("row")
    core = lax.bitwise_and(row, jnp.int32(1))
    chip = lax.div(row, jnp.int32(2))
    chips = lax.axis_size("row") // 2
    return [half * chips + flip(chip, d) for d in pairs for half in (core, 1 - core)]


def share_kernel(inverse, own, *refs):
    received, (out, squares) = refs[:-2], refs[-2:]
    total = own[...] + sum(ref[...].astype(f32) for ref in received)
    x_high, x_low = split(inverse[...], 2)
    high, low = split(total, 2)
    right = dot(x_high, low) + dot(x_low, high) + dot(x_high, high)
    out[...] = right.astype(bf16)
    r = out.shape[0]
    sums = jnp.sum(right * right, axis=1, keepdims=True)
    sums = jnp.transpose(jnp.broadcast_to(sums, (r, 128)))[: squares.shape[0], :]
    block_id = lax.broadcasted_iota(jnp.int32, squares.shape, 0)
    squares[...] = jnp.where(block_id == block_ids((0,))[0], sums, 0.0)


def share_of(inverse, own, received):
    r, width = own.shape
    rows = max(8, lax.axis_size("row"))
    return pl.pallas_call(
        share_kernel,
        out_shape=(shape((r, width), bf16), shape((rows, r), f32)),
        in_specs=[VMEM] * (2 + len(received)),
        out_specs=(VMEM, VMEM),
        compiler_params=params(8),
        name="share",
    )(inverse, own, *received)


def result_kernel(pairs, momenta, weight_too, terms, factor, buf0, buf1, ortho_ref, weight, *refs):
    squares, refs = refs[:terms], refs[terms:]
    blocks, rest = refs[: 2 * len(pairs)], refs[2 * len(pairs) :]
    *outs, token, mbuf, vbuf, nbuf, out_sems, basis_sems = rest
    momentum_too = any(momenta)
    new_momentum = outs[-1] if momentum_too else None
    new_weight, basis = outs[-2 - momentum_too : len(outs) - momentum_too] if weight_too else (None, None)
    r, width = blocks[0].shape
    tile = 256
    tiles = width // tile
    count = len(blocks)
    starts = [i * width for i in block_ids(pairs)]

    def store_basis(b):
        cols = pl.ds(pl.multiple_of(starts[b], 128), width)
        return pltpu.make_async_copy(nbuf.at[b % 2], basis.at[:, cols], basis_sems.at[b % 2])

    def place(b, t):
        return pl.ds(pl.multiple_of(t * tile, tile), tile), pl.ds(pl.multiple_of(starts[b] + t * tile, 128), tile)

    def stores(b, t):
        at, there = place(b, t)
        copies = []
        if momenta[b // 2]:
            copies.append((mbuf, new_momentum))
        if weight_too:
            copies.append((vbuf, new_weight))
        return [
            pltpu.make_async_copy(src.at[b % 2, :, at], dst.at[:, there], out_sems.at[k, b % 2, t])
            for k, (src, dst) in enumerate(copies)
        ]

    def finish(b):
        if weight_too:
            store_basis(b).wait()
        for t in range(tiles):
            for store in stores(b, t):
                store.wait()

    if weight_too:
        total = jnp.sum(pair_up([ref[...] for ref in squares]), axis=0, keepdims=True)
        scale = lax.rsqrt(total / FF + epsilon)
        scale = jnp.transpose(jnp.broadcast_to(scale, (128, r)))[:, :1]
    token[...] = jnp.zeros_like(token)
    depth = lax.axis_size("col")
    size = buf0.shape[0] // depth
    for b in range(count):
        k = b % 2
        if b >= 2:
            finish(b - 2)
        if weight_too:
            nbuf[k] = (blocks[b][...].astype(f32) * scale).astype(bf16)
            store_basis(b).start()

        def step(t, carry, b=b, k=k):
            at, there = place(b, t)
            if momenta[b // 2]:
                correction = dot(ortho_ref[...], blocks[b][:, at])
                for j in range(2 * depth):
                    rows = slice(j * size, (j + 1) * size)
                    here = slice(j // 2 * size, (j // 2 + 1) * size)
                    old = (buf0, buf1)[j % 2][here, there]
                    mbuf[k, rows, at] = old - (1.0 - momentum_decay) * correction[rows]
            if weight_too:
                change = dot(ortho_ref[...], nbuf[k, :, at])
                vbuf[k, :, at] = (weight[:, there].astype(f32) - factor * change).astype(bf16)
            for store in stores(b, t):
                store.start()
            return carry

        lax.fori_loop(0, tiles, step, 0)
    for b in range(count - 2, count):
        finish(b)


def results(pairs, kinds, factor, bufs, ortho_bf, weight, squares, blocks, outs=(), after=(), last=()):
    momenta, weight_too = kinds
    momentum_too = any(momenta)
    m, n = weight.shape
    r, width = blocks[0].shape
    outs = [*outs, *last]
    ins = [*map(keep, bufs), ortho_bf, keep(weight), *squares, *blocks, *after, *map(stay, outs)]
    at = len(ins) - len(outs)
    skipped = 2 * weight_too + momentum_too - len(outs) if last else 0
    out_shape = []
    if weight_too:
        out_shape += [shape((m, n), bf16), shape((r, n), bf16)]
    if momentum_too:
        out_shape += [shape((m, n), f32)]
    m_rows, w_rows = (m if momentum_too else 8), (m if weight_too else 16)
    *outs, token = pl.pallas_call(
        functools.partial(result_kernel, pairs, *kinds, len(squares), factor),
        out_shape=[*out_shape, shape((8, 128), f32)],
        in_specs=[VMEM] * (4 + len(squares) + len(blocks)) + [ANY] * (len(after) + len(outs)),
        out_specs=[ANY] * len(out_shape) + [VMEM],
        input_output_aliases={at + k: skipped + k for k in range(len(outs))},
        scratch_shapes=[
            pltpu.VMEM((2, m_rows, width), f32),
            pltpu.VMEM((2, w_rows, width), bf16),
            pltpu.VMEM((2, r, width), bf16),
            pltpu.SemaphoreType.DMA((2, 2, width // 256)),
            pltpu.SemaphoreType.DMA((2,)),
        ],
        compiler_params=params(12),
        cost_estimate=cost(*[shape((m, width), f32)] * (len(blocks) * (momentum_too + weight_too))),
        name="results",
    )(*ins)
    return outs, token


def sum_over(x, axis, least=1):
    d = least
    while d < lax.axis_size(axis):
        x = x + swap(x, axis, d)
        d *= 2
    return x


def exchange(x, axis, count, unit=1):
    return [x] + [swap(x, axis, unit * d) for d in range(1, count)]


def pair_up(terms):
    while len(terms) > 1:
        terms = [terms[2 * i] + terms[2 * i + 1] for i in range(len(terms) // 2)]
    return terms[0]


def gather(x, axis):
    blocks = [x]
    size = lax.axis_size(axis)
    for d in range(1, size):
        low = d & -d
        blocks.append(swap(blocks[d - low] if d != low else x, axis, low))
    return blocks


def per_device(weight, gradient, momentum, old_basis):
    depth, rows = lax.axis_size("col"), lax.axis_size("row")
    chips = rows // 2
    m, n = momentum.shape
    width = n // rows

    def sum_over_col(held, sent, *before):
        half = m // 2 // depth
        d = 1
        while held.shape[1] > half:
            held, sent = fold(held, swap(sent, "col", d), half)
            d *= 2
        return fold_last(held, swap(sent, "col", d), *before)

    buf0, kept, *outs = project(momentum, gradient, old_basis, depth, width, 0)
    low = sum_over_col(*outs)
    buf1, *outs = project(momentum, gradient, kept, depth, width, 1, (outs[1],))
    lefts = gather(sum_over_col(*outs, low), "col")
    bufs = (buf0, buf1)

    other, mine, g_sums = first_product(bufs, [lefts[d] for d in early(depth)], depth, width)
    lefts_late = [lefts[d] for d in late(depth)]
    g_mine, g_other = gram(lefts_late, g_sums)
    other = last_product(bufs, other, lefts_late, depth, width, False, g_mine)
    g_mine = g_mine + swap(g_other, "row", 1)
    other = hand_on(other, g_mine)
    received = swap(other, "row", 1)
    mine = last_product(bufs, mine, lefts_late, depth, width, True, g_mine, other)
    own, *sent = pair_sum(mine, received, chips, g_mine)
    g_mine = pair_up(exchange(g_mine, "row", chips, 2))
    got = [swap(x, "row", 2 * (d + 1)) for d, x in enumerate(sent)]
    inverse, weight = chol_inverse(g_mine, swap(g_mine, "row", 1), weight)

    share, squares = share_of(inverse, own, got)
    ortho_bf = ortho(inverse, lefts)

    near = [d for d in range(chips) if d & (d - 1) == 0]
    blocks = {d: swap(share, "row", 2 * d) for d in near[1:]}
    own_pair = swap(share, "row", 1)
    factor = step_rate * math.sqrt(D / RANK)
    common = (factor, bufs, ortho_bf, weight)
    squares = exchange(hand_on(squares, own_pair), "col", depth)
    (momentum,), token = results((0,), ((True,), False), *common, squares[:1], (share, own_pair))
    squares = pair_up([hand_on(squares[0], token), *squares[1:]])
    squares = squares + swap(squares, "row", 1)
    squares = hand_on(squares, *blocks.values())
    squares = pair_up(exchange(squares, "row", chips, 2))
    pairs = {}
    for d in near[1:]:
        block = hand_on(blocks[d], squares)
        pairs[d] = (block, swap(block, "row", 1))
    pairs[0] = (share, own_pair)
    h = share.shape[0] // 2
    blocks = {d: pairs[d][0] for d in near}
    halves = {}
    for d in range(chips):
        if d not in near:
            least, most = d & -d, 1 << (d.bit_length() - 1)
            top = swap(blocks[d ^ most][:h], "row", 2 * most)
            bottom = swap(blocks[d ^ least][h:], "row", 2 * least)
            halves[d] = top, bottom
            blocks[d] = jnp.concatenate([top, bottom], axis=0)

    common = (*common, [squares])
    order = (*near[1:], 0)
    rest = [x for d in order for x in pairs[d]]
    kinds = (tuple(d > 0 for d in order), True)
    outs, token = results(order, kinds, *common, rest, (), (), [momentum])
    blocks = {d: jnp.concatenate([hand_on(top, token), bottom], axis=0) for d, (top, bottom) in halves.items()}
    for d, block in blocks.items():
        outs, token = results((d,), ((True,), True), *common, (block, swap(block, "row", 1)), outs)
    new_weight, new_basis, new_momentum = outs
    return (new_weight, new_momentum, new_basis)


def plain_per_device(weight, gradient, momentum, old_basis):
    buffer = momentum + gradient.astype(f32)
    buffer_low = buffer.astype(bf16)
    left_factor = lax.psum(dot(buffer_low, old_basis, ((1,), (1,))), "col")
    gram_share = lax.dot_general(
        left_factor,
        left_factor,
        (((0,), (0,)), ((), ())),
        precision=lax.Precision.HIGHEST,
        preferred_element_type=f32,
    )
    chol_factor = jnp.linalg.cholesky(lax.psum(gram_share, "row"))
    orthonormal = lax.linalg.triangular_solve(
        chol_factor, left_factor, left_side=False, lower=True, transpose_a=True
    ).astype(bf16)
    right_share = lax.psum_scatter(
        dot(orthonormal, buffer_low, ((0,), (0,))), "row", scatter_dimension=0, tiled=True
    )
    sum_squares = lax.psum(jnp.sum(right_share * right_share, axis=1), "col")
    scale_share = jnp.sqrt(sum_squares / FF + epsilon)
    basis_share = (right_share / scale_share[:, None]).astype(bf16)
    new_basis = lax.all_gather(basis_share, "row", axis=0, tiled=True)
    col_scale = lax.all_gather(scale_share, "row", axis=0, tiled=True)
    scaled = (orthonormal.astype(f32) * col_scale[None, :]).astype(bf16)
    new_momentum = buffer - (1.0 - momentum_decay) * dot(scaled, new_basis)
    factor = step_rate * math.sqrt(D / RANK)
    new_weight = (weight.astype(f32) - factor * dot(orthonormal, new_basis)).astype(bf16)
    return (new_weight, new_momentum, new_basis)


def power_of_two(k):
    return k > 1 and k & (k - 1) == 0


def solution(mesh):
    rows, depth = mesh.shape["row"], mesh.shape["col"]
    tiled = (
        power_of_two(rows // 2)
        and power_of_two(depth)
        and depth > 2
        and D % (rows * depth * 128) == 0
        and FF % (rows * depth * 256) == 0
    )
    return jax.shard_map(
        per_device if tiled else plain_per_device,
        mesh=mesh,
        in_specs=(P("row", "col"), P("row", "col"), P("row", "col"), P(None, "col")),
        out_specs=(P("row", "col"), P("row", "col"), P(None, "col")),
        check_vma=False,
    )
```

```python
import functools
import math

import jax
import jax.numpy as jnp
from jax import lax
from jax.experimental import pallas as pl
from jax.experimental.pallas import tpu as pltpu
from jax.sharding import PartitionSpec as P

D = 8192
FF = 24576
RANK = 256

epsilon = 1e-06
momentum_decay = 0.6
step_rate = 0.5

bf16, f32 = jnp.bfloat16, jnp.float32
VMEM = pl.BlockSpec(memory_space=pltpu.VMEM)
ANY = pl.BlockSpec(memory_space=pl.ANY)
MIB = 1 << 20


def shape(dims, kind):
    return jax.ShapeDtypeStruct(dims, kind)


def params(mib):
    return pltpu.CompilerParams(vmem_limit_bytes=mib * MIB)


def dot(a, b, dims=((1,), (0,))):
    return lax.dot_general(a, b, (dims, ((), ())), preferred_element_type=f32)


def split(x, terms):
    parts = []
    for _ in range(terms):
        part = x.astype(bf16)
        parts.append(part)
        x = x - part.astype(f32)
    return parts


def flip(i, d):
    return lax.bitwise_xor(i, jnp.int32(d))


def swap(x, axis, d):
    return lax.ppermute(x, axis, [(i, i ^ d) for i in range(lax.axis_size(axis))])


def project_kernel(part, depth, width, mom, grad, basis, *rest):
    if part == 0:
        (buf, kept), rest = rest[:2], rest[2:]
    else:
        kept, buf, rest = basis, rest[1], rest[2:]
    held, sent, gbuf, total, sems, basis_sem = rest
    m, n = buf.shape
    half = m // depth

    def copies(c):
        cols = pl.ds(pl.multiple_of(c * width, 128), width)
        pairs = []
        for k in range(depth):
            there = pl.ds((2 * k + part) * half, half)
            here = pl.ds(k * half, half)
            pairs.append(pltpu.make_async_copy(mom.at[there, cols], buf.at[here, cols], sems.at[0, k, c]))
            pairs.append(pltpu.make_async_copy(grad.at[there, cols], gbuf.at[here, cols], sems.at[1, k, c]))
        if part == 0:
            pairs.append(pltpu.make_async_copy(basis.at[:, cols], kept.at[:, cols], basis_sem.at[c]))
        return pairs

    def start(c, carry):
        for copy in copies(c):
            copy.start()
        return carry

    def step(c, carry):
        for copy in copies(c):
            copy.wait()
        cols = pl.ds(pl.multiple_of(c * width, 128), width)
        added = buf[:, cols] + gbuf[:, cols].astype(f32)
        buf[:, cols] = added
        total[...] += dot(added.astype(bf16), kept[:, cols], ((1,), (1,)))
        return carry

    total[...] = jnp.zeros_like(total)
    lax.fori_loop(0, n // width, start, 0)
    lax.fori_loop(0, n // width, step, 0)
    me = lax.axis_index("col")
    for out, odd in ((held, 0), (sent, 1)):
        for j in range(depth // 2):
            rows = pl.ds(pl.multiple_of(flip(me, 2 * j + odd) * half, half), half)
            out[:, j * half : (j + 1) * half] = jnp.transpose(total[rows, :]).astype(out.dtype)


def project(momentum, gradient, basis, depth, width, part, after=()):
    m, n = momentum.shape
    m = m // 2
    r = basis.shape[0]
    kept = [] if part else [pltpu.VMEM((r, n), bf16)]
    return pl.pallas_call(
        functools.partial(project_kernel, part, depth, width),
        out_shape=(pltpu.VMEM((m, n), f32), *kept, shape((r, m // 2), f32), shape((r, m // 2), bf16)),
        in_specs=[ANY, ANY] + [VMEM if part else ANY] + [ANY] * len(after),
        out_specs=(VMEM,) * (3 + len(kept)),
        scratch_shapes=[
            pltpu.VMEM((m, n), bf16),
            pltpu.VMEM((m, r), f32),
            pltpu.SemaphoreType.DMA((2, depth, n // width)),
            pltpu.SemaphoreType.DMA((n // width,)),
        ],
        compiler_params=params(14),
        cost_estimate=cost(momentum, gradient),
        name="project",
    )(stay(momentum), stay(gradient), keep(basis) if part else stay(basis), *after)


def fold_kernel(half, held, received, held_out, sent_out):
    added = held[...] + received[...].astype(f32)
    for j in range(held_out.shape[1] // half):
        at = slice(j * half, (j + 1) * half)
        held_out[:, at] = added[:, 2 * j * half : (2 * j + 1) * half]
        sent_out[:, at] = added[:, (2 * j + 1) * half : (2 * j + 2) * half].astype(bf16)


def fold(held, received, half):
    r, size = held.shape
    return pl.pallas_call(
        functools.partial(fold_kernel, half),
        out_shape=(shape((r, size // 2), f32), shape((r, size // 2), bf16)),
        in_specs=[VMEM, VMEM],
        out_specs=(VMEM, VMEM),
        compiler_params=params(8),
        name="fold",
    )(held, received)


def fold_last_kernel(held, received, *rest):
    before, out = rest[:-1], rest[-1]
    half = held.shape[1]
    for k, ref in enumerate(before):
        out[:, k * half : (k + 1) * half] = ref[...]
    out[:, len(before) * half :] = (held[...] + received[...].astype(f32)).astype(bf16)


def fold_last(held, received, *before):
    r, half = held.shape
    return pl.pallas_call(
        fold_last_kernel,
        out_shape=shape((r, half * (1 + len(before))), bf16),
        in_specs=[VMEM] * (2 + len(before)),
        out_specs=VMEM,
        compiler_params=params(8),
        name="fold_last",
    )(held, received, *before)


def cost(*arrays):
    size = sum(math.prod(x.shape) * x.dtype.itemsize for x in arrays)
    return pl.CostEstimate(flops=0, bytes_accessed=size, transcendentals=0)


def keep(x):
    return pltpu.with_memory_space_constraint(x, pltpu.VMEM)


def stay(x):
    return pltpu.with_memory_space_constraint(x, pltpu.HBM)


def buffer_rows(bufs, ds, depth, cols):
    half = bufs[0].shape[0] // depth
    me = lax.axis_index("col")
    rows = [pl.ds(pl.multiple_of(flip(me, d) * half, half), half) for d in ds]
    return jnp.concatenate([buf[at, cols].astype(bf16) for at in rows for buf in bufs], axis=0)


def early(depth):
    return (0, depth // 2)


def late(depth):
    return tuple(d for d in range(depth) if d not in early(depth))


def first_kernel(depth, width, buf0, buf1, *rest):
    lefts, (other, mine, gram, whole) = rest[:-4], rest[-4:]
    core = lax.bitwise_and(lax.axis_index("row"), jnp.int32(1))
    size = other.shape[1]
    block = lefts[0].shape[1]
    for d, ref in enumerate(lefts):
        whole[:, d * block : (d + 1) * block] = ref[...]
    gram[...] = dot(whole[...], whole[...], ((1,), (1,)))
    for out, half in ((other, 1 - core), (mine, core)):

        def step(k, carry, out=out, half=half):
            cols = pl.ds(pl.multiple_of(half * size + k * width, 128), width)
            b = buffer_rows((buf0, buf1), early(depth), depth, cols)
            out[:, pl.ds(pl.multiple_of(k * width, 128), width)] = dot(whole[...], b)
            return carry

        lax.fori_loop(0, size // width, step, 0)


def first_product(bufs, lefts, depth, width):
    m, n = bufs[0].shape
    r, block = lefts[0].shape
    return pl.pallas_call(
        functools.partial(first_kernel, depth, width),
        out_shape=(shape((r, n // 2), f32), shape((r, n // 2), f32), shape((r, r), f32)),
        in_specs=[VMEM] * (2 + len(lefts)),
        out_specs=[VMEM] * 3,
        scratch_shapes=[pltpu.VMEM((r, block * len(lefts)), bf16)],
        compiler_params=params(10),
        cost_estimate=cost(*bufs, shape((r, n), f32)),
        name="first_product",
    )(*map(keep, bufs), *lefts)


def gram_kernel(sums, *rest):
    lefts, (g_mine, g_other, total) = rest[:-3], rest[-3:]
    core = lax.bitwise_and(lax.axis_index("row"), jnp.int32(1))
    total[...] = sums[...] + sum(dot(ref[...], ref[...], ((1,), (1,))) for ref in lefts)
    h = g_mine.shape[0]
    g_mine[...] = total[pl.ds(pl.multiple_of(core * h, h), h), :]
    g_other[...] = total[pl.ds(pl.multiple_of((1 - core) * h, h), h), :]


def gram(lefts, sums):
    r = lefts[0].shape[0]
    return pl.pallas_call(
        gram_kernel,
        out_shape=[shape((r // 2, r), f32)] * 2,
        in_specs=[VMEM] * (1 + len(lefts)),
        out_specs=[VMEM] * 2,
        scratch_shapes=[pltpu.VMEM((r, r), f32)],
        compiler_params=params(8),
        name="gram",
    )(sums, *lefts)


def last_kernel(depth, width, mine, buf0, buf1, sums, *rest):
    lefts, (*_, out, whole) = rest[: len(late(depth))], rest[len(late(depth)) :]
    core = lax.bitwise_and(lax.axis_index("row"), jnp.int32(1))
    half = core if mine else 1 - core
    size = out.shape[1]
    block = lefts[0].shape[1]
    for k, ref in enumerate(lefts):
        whole[:, k * block : (k + 1) * block] = ref[...]

    def step(k, carry):
        cols = pl.ds(pl.multiple_of(half * size + k * width, 128), width)
        at = pl.ds(pl.multiple_of(k * width, 128), width)
        b = buffer_rows((buf0, buf1), late(depth), depth, cols)
        out[:, at] = (sums[:, at] + dot(whole[...], b)).astype(out.dtype)
        return carry

    lax.fori_loop(0, size // width, step, 0)


def last_product(bufs, sums, lefts, depth, width, mine, *after):
    r, block = lefts[0].shape
    return pl.pallas_call(
        functools.partial(last_kernel, depth, width, mine),
        out_shape=shape(sums.shape, f32 if mine else bf16),
        in_specs=[VMEM] * (3 + len(lefts)) + [ANY] * len(after),
        out_specs=VMEM,
        scratch_shapes=[pltpu.VMEM((r, block * len(lefts)), bf16)],
        compiler_params=params(8),
        cost_estimate=cost(*bufs[:1], sums),
        name="mine_product" if mine else "other_product",
    )(*map(keep, bufs), sums, *lefts, *after)


def pair_sum_kernel(chips, mine, received, _, *outs):
    me = lax.div(lax.axis_index("row"), jnp.int32(2))
    width = outs[0].shape[1]
    for d in range(chips):
        cols = pl.ds(pl.multiple_of(flip(me, d) * width, 128), width)
        outs[d][...] = (mine[:, cols] + received[:, cols].astype(f32)).astype(outs[d].dtype)


def pair_sum(mine, received, chips, after):
    r, n = mine.shape
    kinds = [f32] + [bf16] * (chips - 1)
    return pl.pallas_call(
        functools.partial(pair_sum_kernel, chips),
        out_shape=[shape((r, n // chips), k) for k in kinds],
        in_specs=[VMEM, VMEM, ANY],
        out_specs=[VMEM] * chips,
        compiler_params=params(8),
        name="pair_sum",
    )(mine, received, after)


def eliminate(tiles, at, nb, group):
    sub = lax.broadcasted_iota(jnp.int32, (nb, 128), 0)
    scale = jnp.zeros((nb, 128), f32)
    for g in range(0, nb, group):
        cols = [
            jnp.broadcast_to(tiles[0][:, at + g + j : at + g + j + 1], (nb, 128)) for j in range(group)
        ]
        for j in range(group):
            t = g + j
            pivot = cols[j][t : t + 1, :]
            factor = jnp.where(sub > t, cols[j], 0.0) * (1.0 / pivot)
            scale = jnp.where(sub == t, lax.rsqrt(pivot), scale)
            for l in range(j + 1, group):
                cols[l] = cols[l] - factor * cols[l][t : t + 1, :]
            tiles = [x - factor * x[t : t + 1, :] for x in tiles]
    return [x * scale for x in tiles]


def chol_inverse_kernel(mine, other, weight, out, fetched, work, sem):
    piece = weight.shape[0] // sem.shape[0]
    fetches = [
        pltpu.make_async_copy(weight.at[pl.ds(k * piece, piece), :], fetched.at[pl.ds(k * piece, piece), :], sem.at[k])
        for k in range(sem.shape[0])
    ]
    for fetch in fetches:
        fetch.start()
    n = out.shape[0]
    h = n // 2
    core = lax.bitwise_and(lax.axis_index("row"), jnp.int32(1))
    work[pl.ds(pl.multiple_of(core * h, h), h), :n] = mine[...]
    work[pl.ds(pl.multiple_of((1 - core) * h, h), h), :n] = other[...]
    r_id = lax.broadcasted_iota(jnp.int32, (n, n), 0)
    c_id = lax.broadcasted_iota(jnp.int32, (n, n), 1)
    work[:, n:] = jnp.where(r_id == c_id, 1.0, 0.0).astype(f32)
    nb = 32
    for p in range(n // nb):
        lo = p * nb
        left = (lo // 128) * 128
        right = n + ((lo + nb + 127) // 128) * 128
        tiles = [work[lo : lo + nb, c : c + 128] for c in range(left, right, 128)]
        s = jnp.concatenate(eliminate(tiles, lo - left, nb, 8), axis=1)
        work[lo : lo + nb, left:right] = s
        if lo + nb < n:
            lead = s[:, lo + nb - left : n - left]
            work[lo + nb :, left:right] -= lax.dot_general(
                lead, s, (((0,), (0,)), ((), ())), precision=lax.Precision.HIGHEST, preferred_element_type=f32
            )
    out[...] = jnp.where(r_id >= c_id, work[:, n:], 0.0)
    for fetch in fetches:
        fetch.wait()


def chol_inverse(mine, other, weight):
    n = mine.shape[1]
    return pl.pallas_call(
        chol_inverse_kernel,
        out_shape=(shape((n, n), f32), pltpu.VMEM(weight.shape, weight.dtype)),
        in_specs=[VMEM, VMEM, ANY],
        out_specs=(VMEM, VMEM),
        scratch_shapes=[pltpu.VMEM((n, 2 * n), f32), pltpu.SemaphoreType.DMA((8,))],
        compiler_params=params(8),
        cost_estimate=cost(*[mine] * 256),
        name="chol_inverse",
    )(mine, other, stay(weight))


def ortho_kernel(inverse, *refs):
    lefts, out = refs[:-1], refs[-1]
    block = lefts[0].shape[1]
    me = lax.axis_index("col")
    parts = split(inverse[...], 3)
    for d, ref in enumerate(lefts):
        rows = pl.ds(pl.multiple_of(flip(me, d) * block, block), block)
        out[rows, :] = sum(dot(ref[...], x, ((0,), (1,))) for x in reversed(parts)).astype(bf16)


def ortho(inverse, lefts):
    r, block = lefts[0].shape
    return pl.pallas_call(
        ortho_kernel,
        out_shape=shape((block * len(lefts), r), bf16),
        in_specs=[VMEM] * (1 + len(lefts)),
        out_specs=VMEM,
        compiler_params=params(8),
        cost_estimate=cost(*[shape((block * len(lefts), r), bf16)] * 8),
        name="ortho",
    )(inverse, *lefts)


def hand_on(x, *earlier):
    return pl.pallas_call(
        lambda *refs: None,
        out_shape=shape(x.shape, x.dtype),
        in_specs=[ANY] * (1 + len(earlier)),
        out_specs=ANY,
        input_output_aliases={0: 0},
        compiler_params=params(1),
        name="hand_on",
    )(x, *earlier)


def block_ids(pairs):
    row = lax.axis_index("row")
    core = lax.bitwise_and(row, jnp.int32(1))
    chip = lax.div(row, jnp.int32(2))
    chips = lax.axis_size("row") // 2
    return [half * chips + flip(chip, d) for d in pairs for half in (core, 1 - core)]


def share_kernel(inverse, own, *refs):
    received, (out, squares) = refs[:-2], refs[-2:]
    total = own[...] + sum(ref[...].astype(f32) for ref in received)
    x_high, x_low = split(inverse[...], 2)
    high, low = split(total, 2)
    right = dot(x_high, low) + dot(x_low, high) + dot(x_high, high)
    out[...] = right.astype(bf16)
    r = out.shape[0]
    sums = jnp.sum(right * right, axis=1, keepdims=True)
    sums = jnp.transpose(jnp.broadcast_to(sums, (r, 128)))[: squares.shape[0], :]
    block_id = lax.broadcasted_iota(jnp.int32, squares.shape, 0)
    squares[...] = jnp.where(block_id == block_ids((0,))[0], sums, 0.0)


def share_of(inverse, own, received):
    r, width = own.shape
    rows = max(8, lax.axis_size("row"))
    return pl.pallas_call(
        share_kernel,
        out_shape=(shape((r, width), bf16), shape((rows, r), f32)),
        in_specs=[VMEM] * (2 + len(received)),
        out_specs=(VMEM, VMEM),
        compiler_params=params(8),
        name="share",
    )(inverse, own, *received)


def result_kernel(pairs, momenta, weight_too, terms, factor, buf0, buf1, ortho_ref, weight, *refs):
    squares, refs = refs[:terms], refs[terms:]
    blocks, rest = refs[: 2 * len(pairs)], refs[2 * len(pairs) :]
    *outs, token, mbuf, vbuf, nbuf, out_sems, basis_sems = rest
    momentum_too = any(momenta)
    new_momentum = outs[-1] if momentum_too else None
    new_weight, basis = outs[-2 - momentum_too : len(outs) - momentum_too] if weight_too else (None, None)
    r, width = blocks[0].shape
    tile = 256
    tiles = width // tile
    count = len(blocks)
    starts = [i * width for i in block_ids(pairs)]

    def store_basis(b):
        cols = pl.ds(pl.multiple_of(starts[b], 128), width)
        return pltpu.make_async_copy(nbuf.at[b % 2], basis.at[:, cols], basis_sems.at[b % 2])

    def place(b, t):
        return pl.ds(pl.multiple_of(t * tile, tile), tile), pl.ds(pl.multiple_of(starts[b] + t * tile, 128), tile)

    def stores(b, t):
        at, there = place(b, t)
        copies = []
        if momenta[b // 2]:
            copies.append((mbuf, new_momentum))
        if weight_too:
            copies.append((vbuf, new_weight))
        return [
            pltpu.make_async_copy(src.at[b % 2, :, at], dst.at[:, there], out_sems.at[k, b % 2, t])
            for k, (src, dst) in enumerate(copies)
        ]

    def finish(b):
        if weight_too:
            store_basis(b).wait()
        for t in range(tiles):
            for store in stores(b, t):
                store.wait()

    if weight_too:
        total = jnp.sum(pair_up([ref[...] for ref in squares]), axis=0, keepdims=True)
        scale = lax.rsqrt(total / FF + epsilon)
        scale = jnp.transpose(jnp.broadcast_to(scale, (128, r)))[:, :1]
    token[...] = jnp.zeros_like(token)
    depth = lax.axis_size("col")
    size = buf0.shape[0] // depth
    for b in range(count):
        k = b % 2
        if b >= 2:
            finish(b - 2)
        if weight_too:
            nbuf[k] = (blocks[b][...].astype(f32) * scale).astype(bf16)
            store_basis(b).start()

        def step(t, carry, b=b, k=k):
            at, there = place(b, t)
            if momenta[b // 2]:
                correction = dot(ortho_ref[...], blocks[b][:, at])
                for j in range(2 * depth):
                    rows = slice(j * size, (j + 1) * size)
                    here = slice(j // 2 * size, (j // 2 + 1) * size)
                    old = (buf0, buf1)[j % 2][here, there]
                    mbuf[k, rows, at] = old - (1.0 - momentum_decay) * correction[rows]
            if weight_too:
                change = dot(ortho_ref[...], nbuf[k, :, at])
                vbuf[k, :, at] = (weight[:, there].astype(f32) - factor * change).astype(bf16)
            for store in stores(b, t):
                store.start()
            return carry

        lax.fori_loop(0, tiles, step, 0)
    for b in range(count - 2, count):
        finish(b)


def results(pairs, kinds, factor, bufs, ortho_bf, weight, squares, blocks, outs=(), after=(), last=()):
    momenta, weight_too = kinds
    momentum_too = any(momenta)
    m, n = weight.shape
    r, width = blocks[0].shape
    outs = [*outs, *last]
    ins = [*map(keep, bufs), ortho_bf, keep(weight), *squares, *blocks, *after, *map(stay, outs)]
    at = len(ins) - len(outs)
    skipped = 2 * weight_too + momentum_too - len(outs) if last else 0
    out_shape = []
    if weight_too:
        out_shape += [shape((m, n), bf16), shape((r, n), bf16)]
    if momentum_too:
        out_shape += [shape((m, n), f32)]
    m_rows, w_rows = (m if momentum_too else 8), (m if weight_too else 16)
    *outs, token = pl.pallas_call(
        functools.partial(result_kernel, pairs, *kinds, len(squares), factor),
        out_shape=[*out_shape, shape((8, 128), f32)],
        in_specs=[VMEM] * (4 + len(squares) + len(blocks)) + [ANY] * (len(after) + len(outs)),
        out_specs=[ANY] * len(out_shape) + [VMEM],
        input_output_aliases={at + k: skipped + k for k in range(len(outs))},
        scratch_shapes=[
            pltpu.VMEM((2, m_rows, width), f32),
            pltpu.VMEM((2, w_rows, width), bf16),
            pltpu.VMEM((2, r, width), bf16),
            pltpu.SemaphoreType.DMA((2, 2, width // 256)),
            pltpu.SemaphoreType.DMA((2,)),
        ],
        compiler_params=params(12),
        cost_estimate=cost(*[shape((m, width), f32)] * (len(blocks) * (momentum_too + weight_too))),
        name="results",
    )(*ins)
    return outs, token


def sum_over(x, axis, least=1):
    d = least
    while d < lax.axis_size(axis):
        x = x + swap(x, axis, d)
        d *= 2
    return x


def exchange(x, axis, count, unit=1):
    return [x] + [swap(x, axis, unit * d) for d in range(1, count)]


def pair_up(terms):
    while len(terms) > 1:
        terms = [terms[2 * i] + terms[2 * i + 1] for i in range(len(terms) // 2)]
    return terms[0]


def gather(x, axis):
    blocks = [x]
    size = lax.axis_size(axis)
    for d in range(1, size):
        low = d & -d
        blocks.append(swap(blocks[d - low] if d != low else x, axis, low))
    return blocks


def per_device(weight, gradient, momentum, old_basis):
    depth, rows = lax.axis_size("col"), lax.axis_size("row")
    chips = rows // 2
    m, n = momentum.shape
    width = n // rows

    def sum_over_col(held, sent, *before):
        half = m // 2 // depth
        d = 1
        while held.shape[1] > half:
            held, sent = fold(held, swap(sent, "col", d), half)
            d *= 2
        return fold_last(held, swap(sent, "col", d), *before)

    buf0, kept, *outs = project(momentum, gradient, old_basis, depth, width, 0)
    low = sum_over_col(*outs)
    buf1, *outs = project(momentum, gradient, kept, depth, width, 1, (outs[1],))
    lefts = gather(sum_over_col(*outs, low), "col")
    bufs = (buf0, buf1)

    other, mine, g_sums = first_product(bufs, [lefts[d] for d in early(depth)], depth, width)
    lefts_late = [lefts[d] for d in late(depth)]
    g_mine, g_other = gram(lefts_late, g_sums)
    other = last_product(bufs, other, lefts_late, depth, width, False, g_mine)
    g_mine = g_mine + swap(g_other, "row", 1)
    other = hand_on(other, g_mine)
    received = swap(other, "row", 1)
    mine = last_product(bufs, mine, lefts_late, depth, width, True, g_mine, other)
    own, *sent = pair_sum(mine, received, chips, g_mine)
    g_mine = pair_up(exchange(g_mine, "row", chips, 2))
    got = [swap(x, "row", 2 * (d + 1)) for d, x in enumerate(sent)]
    inverse, weight = chol_inverse(g_mine, swap(g_mine, "row", 1), weight)

    share, squares = share_of(inverse, own, got)
    ortho_bf = ortho(inverse, lefts)

    near = [d for d in range(chips) if d & (d - 1) == 0]
    blocks = {d: swap(share, "row", 2 * d) for d in near[1:]}
    own_pair = swap(share, "row", 1)
    factor = step_rate * math.sqrt(D / RANK)
    common = (factor, bufs, ortho_bf, weight)
    squares = exchange(hand_on(squares, own_pair), "col", depth)
    (momentum,), token = results((0,), ((True,), False), *common, squares[:1], (share, own_pair))
    squares = pair_up([hand_on(squares[0], token), *squares[1:]])
    squares = squares + swap(squares, "row", 1)
    squares = hand_on(squares, *blocks.values())
    pairs = {}
    for d in near[1:]:
        block = hand_on(blocks[d], squares)
        pairs[d] = (block, swap(block, "row", 1))
    squares = pair_up(exchange(squares, "row", chips, 2))
    pairs = {d: (hand_on(block, squares), partner) for d, (block, partner) in pairs.items()}
    pairs[0] = (share, own_pair)
    h = share.shape[0] // 2
    blocks = {d: pairs[d][0] for d in near}
    halves = {}
    for d in range(chips):
        if d not in near:
            least, most = d & -d, 1 << (d.bit_length() - 1)
            top = swap(blocks[d ^ most][:h], "row", 2 * most)
            bottom = swap(blocks[d ^ least][h:], "row", 2 * least)
            halves[d] = top, bottom
            blocks[d] = jnp.concatenate([top, bottom], axis=0)

    common = (*common, [squares])
    order = (*near[1:], 0)
    rest = [x for d in order for x in pairs[d]]
    kinds = (tuple(d > 0 for d in order), True)
    outs, token = results(order, kinds, *common, rest, (), (), [momentum])
    blocks = {d: jnp.concatenate([hand_on(top, token), bottom], axis=0) for d, (top, bottom) in halves.items()}
    for d, block in blocks.items():
        outs, token = results((d,), ((True,), True), *common, (block, swap(block, "row", 1)), outs)
    new_weight, new_basis, new_momentum = outs
    return (new_weight, new_momentum, new_basis)


def plain_per_device(weight, gradient, momentum, old_basis):
    buffer = momentum + gradient.astype(f32)
    buffer_low = buffer.astype(bf16)
    left_factor = lax.psum(dot(buffer_low, old_basis, ((1,), (1,))), "col")
    gram_share = lax.dot_general(
        left_factor,
        left_factor,
        (((0,), (0,)), ((), ())),
        precision=lax.Precision.HIGHEST,
        preferred_element_type=f32,
    )
    chol_factor = jnp.linalg.cholesky(lax.psum(gram_share, "row"))
    orthonormal = lax.linalg.triangular_solve(
        chol_factor, left_factor, left_side=False, lower=True, transpose_a=True
    ).astype(bf16)
    right_share = lax.psum_scatter(
        dot(orthonormal, buffer_low, ((0,), (0,))), "row", scatter_dimension=0, tiled=True
    )
    sum_squares = lax.psum(jnp.sum(right_share * right_share, axis=1), "col")
    scale_share = jnp.sqrt(sum_squares / FF + epsilon)
    basis_share = (right_share / scale_share[:, None]).astype(bf16)
    new_basis = lax.all_gather(basis_share, "row", axis=0, tiled=True)
    col_scale = lax.all_gather(scale_share, "row", axis=0, tiled=True)
    scaled = (orthonormal.astype(f32) * col_scale[None, :]).astype(bf16)
    new_momentum = buffer - (1.0 - momentum_decay) * dot(scaled, new_basis)
    factor = step_rate * math.sqrt(D / RANK)
    new_weight = (weight.astype(f32) - factor * dot(orthonormal, new_basis)).astype(bf16)
    return (new_weight, new_momentum, new_basis)


def power_of_two(k):
    return k > 1 and k & (k - 1) == 0


def solution(mesh):
    rows, depth = mesh.shape["row"], mesh.shape["col"]
    tiled = (
        power_of_two(rows // 2)
        and power_of_two(depth)
        and depth > 2
        and D % (rows * depth * 128) == 0
        and FF % (rows * depth * 256) == 0
    )
    return jax.shard_map(
        per_device if tiled else plain_per_device,
        mesh=mesh,
        in_specs=(P("row", "col"), P("row", "col"), P("row", "col"), P(None, "col")),
        out_specs=(P("row", "col"), P("row", "col"), P(None, "col")),
        check_vma=False,
    )
```
